32 devices in a mesh: dp: 8 (over z, core), fsdp: 4 (over y, x).
Axes of the slice: x: 2, y: 2, z: 4, core: 2. Of those that a mesh axis runs over, the one named last changes fastest.
Arguments:
- context: bfloat16 [64, 208, 1024], P(('dp', 'fsdp')), may hold values from -6 to 6
- byte_ids: int32 [64, 1664], P(('dp', 'fsdp')), may hold values from 0 to 255
- segment_ids: int32 [64, 208], P(('dp', 'fsdp')), may hold values from -1 to 3, as said below
- cotangent: bfloat16 [64, 208, 1024], P(('dp', 'fsdp')), may hold values from -6 to 6
- byte_table: bfloat16 [256, 128], P(('dp', 'fsdp')), may hold values from -6 to 6
- norm_mixer: bfloat16 [1024], P(('dp', 'fsdp')), may hold values from 0.5 to 1.5
- proj_zgate: bfloat16 [1024, 2048], P(('dp', 'fsdp')), may hold values from -0.1875 to 0.1875
- proj_inputs: bfloat16 [1024, 2304], P(('dp', 'fsdp')), may hold values from -0.1875 to 0.1875
- proj_step: bfloat16 [1024, 32], P(('dp', 'fsdp')), may hold values from -0.1875 to 0.1875
- conv_kernel: bfloat16 [4, 2304], P(None, ('dp', 'fsdp')), may hold values from -3 to 3
- conv_bias: bfloat16 [2304], P(('dp', 'fsdp')), may hold values from -3 to 3
- step_bias: float32 [32], replicated, may hold values from -6.9 to -2.3
- decay_log: float32 [32], replicated, may hold values from 0 to 2.77
- skip_gain: float32 [32], replicated, may hold values from 0.5 to 1.5
- mixer_norm: bfloat16 [2048], P(('dp', 'fsdp')), may hold values from 0.5 to 1.5
- proj_mixed: bfloat16 [2048, 1024], P(('dp', 'fsdp')), may hold values from -0.125 to 0.125
- norm_attn: bfloat16 [1024], P(('dp', 'fsdp')), may hold values from 0.5 to 1.5
- proj_heads: bfloat16 [1024, 3072], P(('dp', 'fsdp')), may hold values from -0.1875 to 0.1875
- proj_attended: bfloat16 [1024, 1024], P(('dp', 'fsdp')), may hold values from -0.75 to 0.75
- norm_ffn: bfloat16 [1024], P(('dp', 'fsdp')), may hold values from 0.5 to 1.5
- ffn_gate: bfloat16 [1024, 4096], P(('dp', 'fsdp')), may hold values from -0.1875 to 0.1875
- ffn_up: bfloat16 [1024, 4096], P(('dp', 'fsdp')), may hold values from -0.1875 to 0.1875
- ffn_down: bfloat16 [4096, 1024], P(('dp', 'fsdp')), may hold values from -0.09375 to 0.09375
Outputs:
- mixed: float32 [64, 208, 1024], P(('dp', 'fsdp'))
- context_grad: float32 [64, 208, 1024], P(('dp', 'fsdp'))
- rms_stats: float32 [4], replicated
- byte_table_grad: float32 [256, 128], P(('dp', 'fsdp'))
- norm_mixer_grad: float32 [1024], P(('dp', 'fsdp'))
- proj_zgate_grad: float32 [1024, 2048], P(('dp', 'fsdp'))
- proj_inputs_grad: float32 [1024, 2304], P(('dp', 'fsdp'))
- proj_step_grad: float32 [1024, 32], P(('dp', 'fsdp'))
- conv_kernel_grad: float32 [4, 2304], P(None, ('dp', 'fsdp'))
- conv_bias_grad: float32 [2304], P(('dp', 'fsdp'))
- step_bias_grad: float32 [32], replicated
- decay_log_grad: float32 [32], replicated
- skip_gain_grad: float32 [32], replicated
- mixer_norm_grad: float32 [2048], P(('dp', 'fsdp'))
- proj_mixed_grad: float32 [2048, 1024], P(('dp', 'fsdp'))
- norm_attn_grad: float32 [1024], P(('dp', 'fsdp'))
- proj_heads_grad: float32 [1024, 3072], P(('dp', 'fsdp'))
- proj_attended_grad: float32 [1024, 1024], P(('dp', 'fsdp'))
- norm_ffn_grad: float32 [1024], P(('dp', 'fsdp'))
- ffn_gate_grad: float32 [1024, 4096], P(('dp', 'fsdp'))
- ffn_up_grad: float32 [1024, 4096], P(('dp', 'fsdp'))
- ffn_down_grad: float32 [4096, 1024], P(('dp', 'fsdp'))
The draws below stay inside these ranges and needn't reach their ends.
Inputs may be any that keep to these rules, and one draw needn't show every extreme that they name: `segment_ids`: each row holds documents of whole patches: ids start at 0 at the row's first patch and rise by one at each document's start, never falling; the valid prefix of a row holds at most 4 documents (often fewer in short rows), after which padding marked -1 fills its tail; row r has at least 52 + 156 * r // 63 valid patches, the last row has no padding, and the first row always ends in padding.
All inputs are finite; a program needn't handle non-finite values.
Results may differ from the reference program's by a relative error of at most 0.03.
Values may be sent and summed in bfloat16 or wider, within the bound.
No kernel may reach another device: no remote copies, remote signals or barrier semaphores. Data moves between devices by JAX's collectives and lax.ppermute only.
A program may use at most 320 MiB of HBM per device.

```python
import math
from functools import partial
import jax
import jax.numpy as jnp
import numpy as np
from jax import lax

D = 1024
DI = 2048
NS = 128
PM = 64
HD = 64
FF = 4096
KC = 4
PATCH = 8
VOCAB = 256
LEN = 208
HM = 32
HA = 16
BE = 128
XC = 2304
ROWS = 64


def draw_segment_ids(key, part):
    key = jax.random.fold_in(key, 7)
    starts_key, jitter_key = jax.random.split(key)
    row_index = jnp.arange(ROWS, dtype=jnp.int32)[:, None]
    base_valid = LEN // 4 + (LEN - LEN // 4) * row_index // max(ROWS - 1, 1)
    jitter = jax.random.randint(jitter_key, (ROWS, 1), 0, max(LEN // 8, 1))
    valid_length = jnp.minimum(base_valid + jitter, LEN)
    later = jnp.arange(LEN - 1, dtype=jnp.int32)[None, :]
    scores = jax.random.randint(starts_key, (ROWS, LEN - 1), 0, 65536) * LEN + later
    order = jnp.argsort(scores, axis=1)
    chosen = order[:, :3] + 1
    positions = jnp.arange(LEN, dtype=jnp.int32)[None, :]
    marks = jnp.sum((chosen[:, :, None] == positions[:, None, :]).astype(jnp.int32), axis=1)
    numbered = jnp.cumsum(marks, axis=1)
    return jnp.where(positions < valid_length, numbered, -1).astype(jnp.int32)


def set_ends(entries, key, low, top_value):
    index_at = [jax.random.randint(jax.random.fold_in(key, axis), (), 0, length) for axis, length in enumerate(entries.shape)]
    longest = entries.shape.index(max(entries.shape))
    next_to = index_at[:longest] + [(index_at[longest] + 1) % entries.shape[longest]] + index_at[longest + 1:]
    return entries.at[tuple(index_at)].set(low).at[tuple(next_to)].set(top_value)


def steps_of(own_key, dims, shards, low, high):
    gain, own = 1.0, jax.random.fold_in(own_key, 6)
    for position, blocks in shards:
        draws = jnp.exp(jax.random.uniform(jax.random.fold_in(own, position), (blocks,), jnp.float32, low / len(shards), high / len(shards)))
        gain = gain * jnp.repeat(draws, dims[position] // blocks).reshape([-1 if axis == position else 1 for axis in range(len(dims))])
    return gain


def cumulative_ranks(count, skew):
    weights = [(1 << 20) // math.isqrt(grade ** skew) + 1 for grade in range(1, count + 1)]
    spread = 1 + sum(weights) // (1 << 30)
    return np.cumsum(np.array([max(1, weight // spread) for weight in weights]))


def skewed_ids(rng, shape, number_of, skew):
    listing = cumulative_ranks(number_of, skew)
    lot = jax.random.randint(jax.random.fold_in(rng, 1), shape, 0, int(listing[number_of - 1]))
    grade = jnp.searchsorted(jnp.asarray(listing, jnp.int32), lot, side="right")
    return jax.random.permutation(jax.random.fold_in(rng, 2), number_of)[grade].astype(jnp.int32)


def normal_values(own_key, shape, spread, limit, cuts=(), kind=jnp.bfloat16):
    result = jax.random.normal(own_key, shape, jnp.float32) * spread
    if len(cuts) > 0:
        result = steps_of(own_key, shape, cuts, -0.22, 0.18) * result
    return jnp.clip(result, min=-limit, max=limit).astype(kind)


def setup_inputs(seed: int = 0) -> dict:
    keys = jax.random.split(jax.random.key(seed), 24)
    context = normal_values(keys[0], (ROWS, LEN, D), 1.0, 6.0, ((0, 32),))
    byte_ids = set_ends(skewed_ids(keys[1], (ROWS, LEN * PATCH), VOCAB, 2), jax.random.fold_in(keys[1], 3), 0, VOCAB - 1).astype(jnp.int32)
    segment_ids = draw_segment_ids(jax.random.fold_in(keys[23], 71), 0)
    cotangent = normal_values(keys[3], (ROWS, LEN, D), 1.0, 6.0, ((0, 32),))
    byte_table = normal_values(keys[4], (VOCAB, BE), 1.0, 6.0, ((0, 32),))
    norm_mixer = jnp.clip(1.0 + 0.1 * jax.random.normal(keys[5], (D,), jnp.float32), 0.5, 1.5).astype(jnp.bfloat16)
    proj_zgate = normal_values(keys[6], (D, DI), D ** -0.5, 0.1875, ((0, 32),))
    proj_inputs = normal_values(keys[7], (D, XC), D ** -0.5, 0.1875, ((0, 32),))
    proj_step = normal_values(keys[8], (D, HM), D ** -0.5, 0.1875, ((0, 32),))
    conv_kernel = normal_values(keys[9], (KC, XC), KC ** -0.5, 3.0, ((1, 32),))
    conv_bias = normal_values(keys[10], (XC,), 0.5, 3.0, ((0, 32),))
    step_bias = jnp.clip(jax.random.uniform(keys[11], (HM,), jnp.float32, -6.9, -2.3), -6.9, -2.3)
    decay_log = jnp.clip(jax.random.uniform(keys[12], (HM,), jnp.float32, 0.0, 2.77), 0.0, 2.77)
    skip_gain = jnp.clip(jax.random.uniform(keys[13], (HM,), jnp.float32, 0.5, 1.5), 0.5, 1.5)
    mixer_norm = jnp.clip(1.0 + 0.1 * jax.random.normal(keys[14], (DI,), jnp.float32), 0.5, 1.5).astype(jnp.bfloat16)
    proj_mixed = normal_values(keys[15], (DI, D), DI ** -0.5, 0.125, ((0, 32),))
    norm_attn = jnp.clip(1.0 + 0.1 * jax.random.normal(keys[16], (D,), jnp.float32), 0.5, 1.5).astype(jnp.bfloat16)
    proj_heads = normal_values(keys[17], (D, 3 * D), D ** -0.5, 0.1875, ((0, 32),))
    proj_attended = normal_values(keys[18], (D, D), (D // 16) ** -0.5, 0.75, ((0, 32),))
    norm_ffn = jnp.clip(1.0 + 0.1 * jax.random.normal(keys[19], (D,), jnp.float32), 0.5, 1.5).astype(jnp.bfloat16)
    ffn_gate = normal_values(keys[20], (D, FF), D ** -0.5, 0.1875, ((0, 32),))
    ffn_up = normal_values(keys[21], (D, FF), D ** -0.5, 0.1875, ((0, 32),))
    ffn_down = normal_values(keys[22], (FF, D), FF ** -0.5, 0.09375, ((0, 32),))
    return {"context": context, "byte_ids": byte_ids, "segment_ids": segment_ids, "cotangent": cotangent, "byte_table": byte_table, "norm_mixer": norm_mixer, "proj_zgate": proj_zgate, "proj_inputs": proj_inputs, "proj_step": proj_step, "conv_kernel": conv_kernel, "conv_bias": conv_bias, "step_bias": step_bias, "decay_log": decay_log, "skip_gain": skip_gain, "mixer_norm": mixer_norm, "proj_mixed": proj_mixed, "norm_attn": norm_attn, "proj_heads": proj_heads, "proj_attended": proj_attended, "norm_ffn": norm_ffn, "ffn_gate": ffn_gate, "ffn_up": ffn_up, "ffn_down": ffn_down}


EPS = 1e-05
HIGH = lax.Precision.HIGHEST

@jax.custom_vjp
def low(v):
    return lax.optimization_barrier(v.astype(jnp.bfloat16)).astype(jnp.float32)

@jax.custom_vjp
def low_back(v):
    return v

def low_keep(v):
    return (low(v), None)

def low_pass(kept, grad):
    return (grad,)

def back_keep(v):
    return (v, None)

def back_low(kept, grad):
    return (low(grad),)
low.defvjp(low_keep, low_pass)
low_back.defvjp(back_keep, back_low)

def product(former, latter):
    return jnp.matmul(former, latter, precision=HIGH)

def rms_norm(values, scaling):
    return values * lax.rsqrt(lax.optimization_barrier(jnp.mean(values * values, axis=-1, keepdims=True)) + EPS) * scaling

def conv_silu(inputs, kernel, offset, segments):
    kernel_taps = kernel.shape[0]
    length = inputs.shape[1]
    summed = inputs * kernel[kernel_taps - 1]
    for shift_by in range(1, kernel_taps):
        shifted = jnp.pad(inputs, ((0, 0), (shift_by, 0), (0, 0)))[:, :length]
        shifted_ids = jnp.pad(segments, ((0, 0), (shift_by, 0)), constant_values=-2)[:, :length]
        linked = (shifted_ids == segments).astype(jnp.float32)[:, :, None]
        summed = summed + shifted * linked * kernel[kernel_taps - 1 - shift_by]
    return jax.nn.silu(summed + offset)

def mix_weights(gram_matrix, step_raw, step_bias, decay_log, allowed):
    step_size = jax.nn.softplus(step_raw + step_bias)
    decay_rate = step_size * -jnp.exp(decay_log)
    cumulated = jnp.swapaxes(jnp.cumsum(decay_rate, axis=1), 1, 2)
    between = cumulated[:, :, :, None] - cumulated[:, :, None, :]
    keep_mask = allowed[:, None]
    decayed = jnp.where(keep_mask, jnp.exp(jnp.where(keep_mask, between, 0.0)), 0.0)
    return gram_matrix[:, None] * decayed * jnp.swapaxes(step_size, 1, 2)[:, :, None, :]

def gate_norm(heads_out, skip_values, zgate_raw, skip_gain, norm_gain):
    combined = heads_out + skip_gain[:, None] * skip_values
    gated_rows = combined.reshape(zgate_raw.shape) * jax.nn.silu(zgate_raw)
    return rms_norm(gated_rows, norm_gain)

def block_forward(params, context, byte_ids, segments):
    byte_rows, gain_one, zgate_w, inputs_w, step_w, kernel, offset, step_bias, decay_log, skip_gain, gated_gain, mixed_w, gain_two, heads_w, attended_w, gain_three, gate_w, upper_w, down_w = params
    row_count = segments.shape[0]
    symbols = jnp.arange(VOCAB, dtype=jnp.int32)
    onehot = (byte_ids[:, :, None] == symbols[None, None, :]).astype(jnp.float32)
    embedded = low_back(product(onehot, byte_rows)).reshape(row_count, LEN, D)
    stream_zero = embedded + context
    positions = jnp.arange(LEN, dtype=jnp.int32)
    causal = positions[:, None] >= positions[None, :]
    allowed = (segments[:, :, None] == segments[:, None, :]) & causal[None]
    normed_one = low(rms_norm(stream_zero, gain_one))
    zgate = low_back(product(normed_one, zgate_w))
    inputs_raw = low_back(product(normed_one, inputs_w))
    step_raw = low_back(product(normed_one, step_w))
    activated = conv_silu(inputs_raw, kernel, offset, segments)
    values_low = low(activated[:, :, :DI]).reshape(row_count, LEN, HM, PM)
    state_in = low(activated[:, :, DI:DI + NS])
    state_out = low(activated[:, :, DI + NS:])
    gram_matrix = low_back(jnp.einsum('ntk,nsk->nts', state_out, state_in, precision=HIGH))
    weights = low(mix_weights(gram_matrix, step_raw, step_bias, decay_log, allowed))
    heads_out = low_back(jnp.einsum('nhts,nshp->nthp', weights, values_low, precision=HIGH))
    normed_gate = low(gate_norm(heads_out, values_low, zgate, skip_gain, gated_gain))
    mixer_out = low_back(product(normed_gate, mixed_w))
    stream_one = stream_zero + mixer_out
    normed_two = low(rms_norm(stream_one, gain_two))
    joined = low_back(product(normed_two, heads_w))
    queries = low(joined[:, :, :D]).reshape(row_count, LEN, HA, HD)
    key_rows = low(joined[:, :, D:2 * D]).reshape(row_count, LEN, HA, HD)
    value_rows = low(joined[:, :, 2 * D:]).reshape(row_count, LEN, HA, HD)
    scores = low_back(jnp.einsum('nthd,nshd->nhts', queries, key_rows, precision=HIGH) * HD ** (-0.5))
    masked = jnp.where(allowed[:, None], scores, -1e+30)
    highest = lax.optimization_barrier(jnp.max(masked, axis=-1, keepdims=True))
    exponents = jnp.exp(masked - highest)
    probabilities = low(exponents / lax.optimization_barrier(jnp.sum(exponents, axis=-1, keepdims=True)))
    attended = low(low_back(jnp.einsum('nhts,nshd->nthd', probabilities, value_rows, precision=HIGH)))
    attn_out = low_back(product(attended.reshape(row_count, LEN, D), attended_w))
    stream_two = stream_one + attn_out
    normed_three = low(rms_norm(stream_two, gain_three))
    gate_pre = low_back(product(normed_three, gate_w))
    up_pre = low_back(product(normed_three, upper_w))
    hidden = low(jax.nn.silu(gate_pre) * up_pre)
    ffn_out = low_back(product(hidden, down_w))
    mixed_out = stream_two + ffn_out
    valid_rows = (segments >= 0).astype(jnp.float32)[:, :, None]
    moments = jnp.stack([jnp.sum(valid_rows * stream_zero * stream_zero), jnp.sum(valid_rows * mixer_out * mixer_out), jnp.sum(valid_rows * attn_out * attn_out), jnp.sum(valid_rows * ffn_out * ffn_out), jnp.sum(valid_rows)])
    return (mixed_out, moments)

def reference(context, byte_ids, segment_ids, cotangent, byte_table, norm_mixer, proj_zgate, proj_inputs, proj_step, conv_kernel, conv_bias, step_bias, decay_log, skip_gain, mixer_norm, proj_mixed, norm_attn, proj_heads, proj_attended, norm_ffn, ffn_gate, ffn_up, ffn_down):
    params = tuple((weight.astype(jnp.float32) for weight in (byte_table, norm_mixer, proj_zgate, proj_inputs, proj_step, conv_kernel, conv_bias, step_bias, decay_log, skip_gain, mixer_norm, proj_mixed, norm_attn, proj_heads, proj_attended, norm_ffn, ffn_gate, ffn_up, ffn_down)))
    group_rows = math.gcd(ROWS, 16)
    group_count = ROWS // group_rows

    def grouped(values):
        return values.reshape((group_count, group_rows) + values.shape[1:])

    def one_group(running, pieces):
        grad_sums, moment_sums = running
        context_part, ids_part, segment_part, cotangent_part = pieces
        forward = partial(block_forward, byte_ids=ids_part, segments=segment_part)
        mixed_out, pullback, moment_terms = jax.vjp(forward, params, context_part.astype(jnp.float32), has_aux=True)
        param_grads, context_part_grad = pullback(cotangent_part.astype(jnp.float32))
        grad_sums = jax.tree.map(jnp.add, grad_sums, param_grads)
        return ((grad_sums, moment_sums + moment_terms), (mixed_out, context_part_grad))
    zero_grads = jax.tree.map(jnp.zeros_like, params)
    initial = (zero_grads, jnp.zeros((5,), jnp.float32))
    (grad_sums, moment_sums), (mixed_all, context_grad) = lax.scan(one_group, initial, (grouped(context), grouped(byte_ids), grouped(segment_ids), grouped(cotangent)))
    rms_stats = jnp.sqrt(moment_sums[:4] / (moment_sums[4] * D))
    return (mixed_all.reshape(ROWS, LEN, D), context_grad.reshape(ROWS, LEN, D), rms_stats, grad_sums[0], grad_sums[1], grad_sums[2], grad_sums[3], grad_sums[4], grad_sums[5], grad_sums[6], grad_sums[7], grad_sums[8], grad_sums[9], grad_sums[10], grad_sums[11], grad_sums[12], grad_sums[13], grad_sums[14], grad_sums[15], grad_sums[16], grad_sums[17], grad_sums[18])
```

```python
from functools import partial

import jax
import jax.numpy as jnp
from jax import lax
from jax.experimental import pallas as pl
from jax.experimental.pallas import tpu as pltpu
from jax.sharding import PartitionSpec as P

DI = 2048
NS = 128
PM = 64
HD = 64
HM = 32
HA = 16


EPS = 1e-05


def matmul(former, latter):
    return jnp.dot(former, latter, preferred_element_type=jnp.float32)


def matmul_left(former, latter):
    return lax.dot_general(
        former, latter, (((0,), (0,)), ((), ())), preferred_element_type=jnp.float32
    )


def matmul_right(former, latter):
    return lax.dot_general(
        former, latter, (((1,), (1,)), ((), ())), preferred_element_type=jnp.float32
    )


def rms_norm(values, scaling):
    return values * lax.rsqrt(jnp.mean(values * values, axis=-1, keepdims=True) + EPS) * scaling


def conv_silu(inputs, kernel, offset, segments):
    kernel_taps = kernel.shape[0]
    length = inputs.shape[1]
    summed = inputs * kernel[kernel_taps - 1]
    for shift_by in range(1, kernel_taps):
        shifted = jnp.pad(inputs, ((0, 0), (shift_by, 0), (0, 0)))[:, :length]
        shifted_ids = jnp.pad(segments, ((0, 0), (shift_by, 0)), constant_values=-2)[:, :length]
        linked = (shifted_ids == segments).astype(jnp.float32)[:, :, None]
        summed = summed + shifted * linked * kernel[kernel_taps - 1 - shift_by]
    return jax.nn.silu(summed + offset)


def mix_weights(gram_matrix, step_raw, step_bias, decay_log, allowed):
    step_size = jax.nn.softplus(step_raw + step_bias)
    decay_rate = step_size * -jnp.exp(decay_log)
    cumulated = jnp.swapaxes(jnp.cumsum(decay_rate, axis=1), 1, 2)
    between = cumulated[:, :, :, None] - cumulated[:, :, None, :]
    keep_mask = allowed[:, None]
    decayed = jnp.where(keep_mask, jnp.exp(jnp.where(keep_mask, between, 0.0)), 0.0)
    return gram_matrix[:, None] * decayed * jnp.swapaxes(step_size, 1, 2)[:, :, None, :]


def gate_norm(heads_out, skip_values, zgate_raw, skip_gain, norm_gain):
    combined = heads_out + skip_gain[:, None] * skip_values
    gated_rows = combined.reshape(zgate_raw.shape) * jax.nn.silu(zgate_raw)
    return rms_norm(gated_rows, norm_gain)


def silu_product(gate_raw, upper_raw):
    return jax.nn.silu(gate_raw) * upper_raw


AXES = ("dp", "fsdp")


def axis_bits():
    bits = []
    for name in AXES:
        size = lax.axis_size(name)
        step = size // 2
        while step:
            bits.append((name, size, step))
            step //= 2
    return bits


def phases(flip):
    bits = axis_bits()
    outer = [k for k, b in enumerate(bits) if b[0] == "dp" and b[2] > 1]
    core = [k for k, b in enumerate(bits) if b[0] == "dp" and b[2] == 1]
    inner = [k for k, b in enumerate(bits) if b[0] == "fsdp"]
    return bits, outer[::-1] + (inner if flip else inner[::-1]) + core


def swap(v, bit):
    name, size, step = bit
    return lax.ppermute(v, name, [(i, i ^ step) for i in range(size)])


def own_bit(bit):
    return (lax.axis_index(bit[0]) // bit[2]) % 2


def own_index():
    return lax.axis_index("dp") * lax.axis_size("fsdp") + lax.axis_index("fsdp")


def bit_weight(bit):
    return bit[2] * (lax.axis_size("fsdp") if bit[0] == "dp" else 1)


def assemble_kernel(offsets, me_ref, *refs):
    pieces, out_ref, sems = refs[:-2], refs[-2], refs[-1]
    me = me_ref[0]
    copies = []
    count = 0
    for piece, places in zip(pieces, offsets):
        for j, place in enumerate(places):
            copies.append(
                pltpu.make_async_copy(piece.at[j], out_ref.at[me ^ place], sems.at[count])
            )
            count += 1
    for c in copies:
        c.start()
    for c in copies:
        c.wait()


def tie(*values):
    return lax.optimization_barrier(values)


class Gather:
    def __init__(self, shard, flip):
        self.rows, self.columns = shard.shape
        self.bits, self.order = phases(flip)
        self.pieces = [(shard[None], [0])]
        self.phase = 0

    def step(self):
        k = self.order[self.phase]
        weight = bit_weight(self.bits[k])
        if len(self.pieces) > 1 and self.phase < len(self.order) - 1:
            joined = jnp.concatenate([p for p, _ in self.pieces], axis=0)
            self.pieces = [(joined, sum((o for _, o in self.pieces), []))]
        self.pieces = self.pieces + [
            (swap(p, self.bits[k]), [o ^ weight for o in offs]) for p, offs in self.pieces
        ]
        self.phase += 1

    def last(self):
        return self.pieces[-1][0]

    def set_first(self, v):
        self.pieces[0] = (v, self.pieces[0][1])

    def done(self):
        while self.phase < len(self.order):
            self.step()
        count = 2 ** len(self.bits)
        me = own_index().astype(jnp.int32).reshape(1)
        out = pl.pallas_call(
            partial(assemble_kernel, [o for _, o in self.pieces]),
            out_shape=jax.ShapeDtypeStruct((count, self.rows, self.columns), jnp.bfloat16),
            in_specs=[pl.BlockSpec(memory_space=pltpu.SMEM)]
            + [pl.BlockSpec(memory_space=pl.ANY)] * len(self.pieces),
            out_specs=pl.BlockSpec(memory_space=pltpu.VMEM),
            scratch_shapes=[pltpu.SemaphoreType.DMA((count,))],
            compiler_params=pltpu.CompilerParams(vmem_limit_bytes=24 * 1024 * 1024),
        )(me, *[p for p, _ in self.pieces])
        return out.reshape(count * self.rows, self.columns)


def gather_small(shard):
    bits = axis_bits()
    out = shard[None]
    for bit in bits[::-1]:
        other = swap(out, bit)
        mine = own_bit(bit) == 0
        out = jnp.concatenate([jnp.where(mine, out, other), jnp.where(mine, other, out)], axis=0)
    return out


def scatter_sum(part, flip, core_done, wide=False):
    bits, order = phases(flip)
    names = [k for k in range(len(bits)) if not (core_done and bits[k][0] == "dp" and bits[k][2] == 1)]
    count = 2 ** len(names)
    part = part.reshape([2] * len(names) + [part.shape[0] // count, part.shape[1]])
    for n, k in enumerate([k for k in order[::-1] if k in names]):
        axis = names.index(k)
        names.remove(k)
        mine = own_bit(bits[k])
        send = lax.dynamic_index_in_dim(part, 1 - mine, axis, keepdims=False)
        keep = lax.dynamic_index_in_dim(part, mine, axis, keepdims=False)
        total = keep.astype(jnp.float32) + swap(send, bits[k]).astype(jnp.float32)
        part = total if not names else total.astype(part.dtype)
    return part.astype(jnp.float32)


def core_columns(former, core):
    outer = lax.axis_size("dp") // 2
    group = former.shape[1] // (2 * outer)
    return jnp.concatenate(
        [lax.dynamic_slice_in_dim(former, (2 * i + core) * group, group, 1) for i in range(outer)],
        axis=1,
    )


class Scatter:
    def __init__(self, former, latter, flip):
        self.bits, order = phases(flip)
        self.core = [k for k, b in enumerate(self.bits) if b[0] == "dp" and b[2] == 1][0]
        mine = own_bit(self.bits[self.core])
        send = matmul_left(core_columns(former, 1 - mine), latter).astype(jnp.bfloat16)
        self.received = swap(send, self.bits[self.core])
        self.keep = matmul_left(core_columns(former, mine), latter)
        self.names = [k for k in range(len(self.bits)) if k != self.core]
        self.order = [k for k in order[::-1] if k != self.core]
        self.shape = None

    def step(self):
        total = self.keep.astype(jnp.float32) + self.received.astype(jnp.float32)
        if not self.names:
            self.keep = total
            return
        part = total.astype(jnp.bfloat16)
        if self.shape is None:
            count = 2 ** len(self.names)
            self.shape = part.shape
            part = part.reshape([2] * len(self.names) + [part.shape[0] // count, part.shape[1]])
        k = self.order.pop(0)
        axis = self.names.index(k)
        self.names.remove(k)
        mine = own_bit(self.bits[k])
        self.received = swap(
            lax.dynamic_index_in_dim(part, 1 - mine, axis, keepdims=False), self.bits[k]
        )
        self.keep = lax.dynamic_index_in_dim(part, mine, axis, keepdims=False)

    def done(self):
        while self.names:
            self.step()
        self.step()
        return self.keep


def advance(value, *pipes):
    tied = tie(value, *[p.received for p in pipes])
    for p, received in zip(pipes, tied[1:]):
        p.received = received
        p.step()
    return tied[0]


def local(
    context,
    byte_ids,
    segment_ids,
    cotangent,
    byte_table,
    norm_mixer,
    proj_zgate,
    proj_inputs,
    proj_step,
    conv_kernel,
    conv_bias,
    step_bias,
    decay_log,
    skip_gain,
    mixer_norm,
    proj_mixed,
    norm_attn,
    proj_heads,
    proj_attended,
    norm_ffn,
    ffn_gate,
    ffn_up,
    ffn_down,
):
    row_count, length = segment_ids.shape
    tokens = row_count * length
    model_width = context.shape[2]
    model_rows = norm_mixer.shape[0]
    small = [
        byte_table.reshape(-1),
        norm_mixer,
        conv_kernel.reshape(-1),
        conv_bias,
        mixer_norm,
        norm_attn,
        norm_ffn,
    ]
    lengths = [v.shape[0] for v in small]
    packed = jnp.concatenate(small)
    packed = jnp.pad(packed, (0, -packed.shape[0] % 1024)).reshape(8, -1)
    everyone = gather_small(packed).reshape(-1, packed.size)
    unpacked = []
    start = 0
    for count in lengths:
        unpacked.append(everyone[:, start : start + count])
        start += count
    table_full = unpacked[0].reshape(-1, byte_table.shape[1])
    gain_one = unpacked[1].reshape(-1)
    taps = conv_kernel.shape[0]
    kernel_full = jnp.swapaxes(
        unpacked[2].reshape(-1, taps, conv_kernel.shape[1]), 0, 1
    ).reshape(taps, -1)
    offset_full = unpacked[3].reshape(-1)
    gated_gain = unpacked[4].reshape(-1)
    gain_two = unpacked[5].reshape(-1)
    gain_three = unpacked[6].reshape(-1)
    wide = proj_inputs.shape[1]
    step_padded = jnp.pad(proj_step, ((0, 0), (0, 128 - proj_step.shape[1])))
    g_inputs = Gather(jnp.concatenate([proj_inputs, step_padded], axis=1), False)
    g_zgate = Gather(proj_zgate, True)
    g_mixed = Gather(proj_mixed, False)
    g_heads = Gather(proj_heads, True)
    g_attended = Gather(proj_attended, False)
    g_gate = Gather(ffn_gate, False)
    g_upper = Gather(ffn_up, True)
    g_down = Gather(ffn_down, False)
    before = None
    for several in ([g_inputs, g_zgate], [g_mixed, g_heads], [g_attended, g_gate], [g_upper], [g_down]):
        if before is not None:
            tied = tie(*[g.pieces[0][0] for g in several], *[g.last() for g in before])
            for g, v in zip(several, tied):
                g.set_first(v)
        for g in several:
            g.step()
            g.step()
        before = several
    inputs_step_full = g_inputs.done()
    zgate_full = g_zgate.done()
    mixed_full = g_mixed.done()
    heads_full = g_heads.done()
    attended_full = g_attended.done()
    gate_full = g_gate.done()
    upper_full = g_upper.done()
    down_full = g_down.done()
    symbols = jnp.arange(table_full.shape[0], dtype=jnp.int32)
    onehot = (byte_ids.reshape(-1)[:, None] == symbols[None, :]).astype(jnp.bfloat16)
    embedded = matmul(onehot, table_full).reshape(tokens, model_width)
    stream_zero = embedded + context.reshape(tokens, model_width).astype(jnp.float32)
    positions = jnp.arange(length, dtype=jnp.int32)
    causal = positions[:, None] >= positions[None, :]
    allowed = (segment_ids[:, :, None] == segment_ids[:, None, :]) & causal[None]
    normed_one, norm_one_back = jax.vjp(rms_norm, stream_zero, gain_one.astype(jnp.float32))
    normed_one_low = normed_one.astype(jnp.bfloat16)
    zgate = matmul(normed_one_low, zgate_full)
    inputs_step = matmul(normed_one_low, inputs_step_full)
    inputs_raw = inputs_step[:, :wide]
    step_raw = inputs_step[:, wide : wide + HM]
    activated, conv_back = jax.vjp(
        partial(conv_silu, segments=segment_ids),
        inputs_raw.reshape(row_count, length, -1),
        kernel_full.astype(jnp.float32),
        offset_full.astype(jnp.float32),
    )
    values_low = activated[:, :, :DI].astype(jnp.bfloat16).reshape(row_count, length, HM, PM)
    state_in = activated[:, :, DI : DI + NS].astype(jnp.bfloat16)
    state_out = activated[:, :, DI + NS :].astype(jnp.bfloat16)
    gram_matrix = jnp.einsum(
        "ntk,nsk->nts", state_out, state_in, preferred_element_type=jnp.float32
    )
    weights, weights_back = jax.vjp(
        partial(mix_weights, allowed=allowed),
        gram_matrix,
        step_raw.reshape(row_count, length, -1),
        step_bias,
        decay_log,
    )
    weights_low = weights.astype(jnp.bfloat16)
    heads_out = jnp.einsum(
        "nhts,nshp->nthp", weights_low, values_low, preferred_element_type=jnp.float32
    )
    normed_gate, gate_back = jax.vjp(
        gate_norm,
        heads_out,
        values_low.astype(jnp.float32),
        zgate.reshape(row_count, length, -1),
        skip_gain,
        gated_gain.astype(jnp.float32),
    )
    gate_low = normed_gate.reshape(tokens, -1).astype(jnp.bfloat16)
    mixer_out = matmul(gate_low, mixed_full)
    stream_one = stream_zero + mixer_out
    normed_two, norm_two_back = jax.vjp(rms_norm, stream_one, gain_two.astype(jnp.float32))
    normed_two_low = normed_two.astype(jnp.bfloat16)
    joined = matmul(normed_two_low, heads_full)
    query_low = joined[:, :model_width].astype(jnp.bfloat16).reshape(row_count, length, HA, HD)
    key_low = (
        joined[:, model_width : 2 * model_width]
        .astype(jnp.bfloat16)
        .reshape(row_count, length, HA, HD)
    )
    value_low = joined[:, 2 * model_width :].astype(jnp.bfloat16).reshape(row_count, length, HA, HD)
    scale = HD ** (-0.5)
    scores = (
        jnp.einsum("nthd,nshd->nhts", query_low, key_low, preferred_element_type=jnp.float32)
        * scale
    )
    masked = jnp.where(allowed[:, None], scores, -1e30)
    highest = jnp.max(masked, axis=-1, keepdims=True)
    exponents = jnp.exp(masked - highest)
    summed = jnp.sum(exponents, axis=-1, keepdims=True)
    probabilities = (exponents / summed).astype(jnp.bfloat16)
    log_total = highest + jnp.log(summed)
    attended = jnp.einsum(
        "nhts,nshd->nthd", probabilities, value_low, preferred_element_type=jnp.float32
    )
    attended_low = attended.reshape(tokens, model_width).astype(jnp.bfloat16)
    attn_out = matmul(attended_low, attended_full)
    stream_two = stream_one + attn_out
    normed_three, norm_three_back = jax.vjp(rms_norm, stream_two, gain_three.astype(jnp.float32))
    normed_three_low = normed_three.astype(jnp.bfloat16)
    gate_pre = matmul(normed_three_low, gate_full)
    up_pre = matmul(normed_three_low, upper_full)
    hidden, hidden_back = jax.vjp(silu_product, gate_pre, up_pre)
    hidden_low = hidden.astype(jnp.bfloat16)
    ffn_out = matmul(hidden_low, down_full)
    stream_three = stream_two + ffn_out
    valid_rows = (segment_ids.reshape(tokens, 1) >= 0).astype(jnp.float32)
    moments = jnp.stack(
        [
            jnp.sum(valid_rows * stream_zero * stream_zero),
            jnp.sum(valid_rows * mixer_out * mixer_out),
            jnp.sum(valid_rows * attn_out * attn_out),
            jnp.sum(valid_rows * ffn_out * ffn_out),
            jnp.sum(valid_rows),
        ]
    )
    grad_three = cotangent.reshape(tokens, model_width).astype(jnp.float32)
    ffn_grad_low = grad_three.astype(jnp.bfloat16)
    grad_ffn_down = Scatter(hidden_low, ffn_grad_low, False)
    grad_hidden = matmul_right(ffn_grad_low, down_full)
    grad_gate_pre, grad_up_pre = hidden_back(grad_hidden)
    gate_grad_low = grad_gate_pre.astype(jnp.bfloat16)
    upper_grad_low = grad_up_pre.astype(jnp.bfloat16)
    grad_ffn_gate = Scatter(normed_three_low, gate_grad_low, True)
    grad_ffn_up = Scatter(normed_three_low, upper_grad_low, False)
    grad_normed_three = matmul_right(gate_grad_low, gate_full) + matmul_right(
        upper_grad_low, upper_full
    )
    stream_part, grad_norm_ffn = norm_three_back(grad_normed_three)
    grad_two = grad_three + stream_part
    attn_grad_low = grad_two.astype(jnp.bfloat16)
    attn_grad_low = advance(attn_grad_low, grad_ffn_down)
    grad_proj_attended = Scatter(attended_low, attn_grad_low, False)
    grad_attended = (
        matmul_right(attn_grad_low, attended_full)
        .astype(jnp.bfloat16)
        .reshape(row_count, length, HA, HD)
    )
    grad_attended = advance(grad_attended, grad_ffn_gate, grad_ffn_up)
    rescored = (
        jnp.einsum("nthd,nshd->nhts", query_low, key_low, preferred_element_type=jnp.float32)
        * scale
    )
    remasked = jnp.where(allowed[:, None], rescored, -1e30)
    probs_again = jnp.where(allowed[:, None], jnp.exp(remasked - log_total), 0.0)
    grad_probs = jnp.einsum(
        "nthd,nshd->nhts", grad_attended, value_low, preferred_element_type=jnp.float32
    )
    grad_value_rows = jnp.einsum(
        "nhts,nthd->nshd",
        probs_again.astype(jnp.bfloat16),
        grad_attended,
        preferred_element_type=jnp.float32,
    )
    grad_scores = (
        probs_again * (grad_probs - jnp.sum(probs_again * grad_probs, axis=-1, keepdims=True))
    ).astype(jnp.bfloat16)
    grad_scores = advance(grad_scores, grad_ffn_down)
    grad_query = (
        jnp.einsum("nhts,nshd->nthd", grad_scores, key_low, preferred_element_type=jnp.float32)
        * scale
    )
    grad_key = (
        jnp.einsum("nhts,nthd->nshd", grad_scores, query_low, preferred_element_type=jnp.float32)
        * scale
    )
    grad_joined = jnp.concatenate(
        [
            grad_query.reshape(tokens, model_width),
            grad_key.reshape(tokens, model_width),
            grad_value_rows.reshape(tokens, model_width),
        ],
        axis=1,
    ).astype(jnp.bfloat16)
    grad_proj_heads = Scatter(normed_two_low, grad_joined, True)
    grad_joined = advance(grad_joined, grad_ffn_down, grad_ffn_gate, grad_ffn_up)
    grad_normed_two = matmul_right(grad_joined, heads_full)
    stream_part_two, grad_norm_attn = norm_two_back(grad_normed_two)
    grad_one = grad_two + stream_part_two
    mixer_grad_low = grad_one.astype(jnp.bfloat16)
    grad_proj_mixed = Scatter(gate_low, mixer_grad_low, False)
    grad_normed_gate = matmul_right(mixer_grad_low, mixed_full).reshape(row_count, length, -1)
    grad_heads, grad_skip_values, grad_zgate, grad_skip_gain, grad_gated_gain = gate_back(
        grad_normed_gate
    )
    heads_grad_low = grad_heads.astype(jnp.bfloat16)
    heads_grad_low = advance(
        heads_grad_low, grad_ffn_down, grad_ffn_gate, grad_ffn_up, grad_proj_attended, grad_proj_heads
    )
    grad_weights = jnp.einsum(
        "nthp,nshp->nhts", heads_grad_low, values_low, preferred_element_type=jnp.float32
    )
    grad_values = (
        jnp.einsum(
            "nhts,nthp->nshp", weights_low, heads_grad_low, preferred_element_type=jnp.float32
        )
        + grad_skip_values
    )
    grad_weights = advance(
        grad_weights, grad_ffn_gate, grad_ffn_up, grad_proj_attended, grad_proj_heads, grad_proj_mixed
    )
    grad_gram, grad_step_raw, grad_step_bias, grad_decay_log = weights_back(grad_weights)
    gram_grad_low = grad_gram.astype(jnp.bfloat16)
    gram_grad_low = advance(
        gram_grad_low, grad_proj_attended, grad_proj_heads, grad_proj_mixed
    )
    grad_state_out = jnp.einsum(
        "nts,nsk->ntk", gram_grad_low, state_in, preferred_element_type=jnp.float32
    )
    grad_state_in = jnp.einsum(
        "nts,ntk->nsk", gram_grad_low, state_out, preferred_element_type=jnp.float32
    )
    grad_activated = jnp.concatenate(
        [grad_values.reshape(row_count, length, -1), grad_state_in, grad_state_out], axis=-1
    )
    grad_inputs_raw, grad_conv_kernel, grad_conv_bias = conv_back(grad_activated)
    zgate_grad_low = grad_zgate.reshape(tokens, -1).astype(jnp.bfloat16)
    inputs_grad_low = grad_inputs_raw.reshape(tokens, -1).astype(jnp.bfloat16)
    step_grad_low = grad_step_raw.reshape(tokens, -1).astype(jnp.bfloat16)
    grad_proj_zgate = Scatter(normed_one_low, zgate_grad_low, True)
    inputs_step_grad_low = jnp.concatenate(
        [inputs_grad_low, jnp.pad(step_grad_low, ((0, 0), (0, 128 - step_grad_low.shape[1])))], axis=1
    )
    grad_inputs_step = Scatter(normed_one_low, inputs_step_grad_low, False)
    grad_normed_one = matmul_right(zgate_grad_low, zgate_full) + matmul_right(
        inputs_step_grad_low, inputs_step_full
    )
    stream_part_one, grad_norm_mixer = norm_one_back(grad_normed_one)
    grad_zero = grad_one + stream_part_one
    embed_grad_low = grad_zero.reshape(-1, table_full.shape[1]).astype(jnp.bfloat16)
    grad_byte_table = matmul_left(onehot, embed_grad_low)
    late = jnp.concatenate(
        [
            grad_byte_table.reshape(-1, byte_table.size),
            grad_norm_mixer.reshape(-1, model_rows),
        ],
        axis=1,
    )
    late = jnp.pad(late, ((0, 0), (0, -late.shape[1] % 1024)))
    late = scatter_sum(late, False, False).reshape(-1)
    table_sum = late[: byte_table.size].reshape(byte_table.shape)
    norm_mixer_sum = late[byte_table.size : byte_table.size + model_rows]
    (
        totals,
        bias_total,
        decay_total,
        skip_total,
        kernel_sum,
        offset_sum,
        gated_sum,
        norm_attn_sum,
        norm_ffn_sum,
    ) = lax.psum(
        (
            moments,
            grad_step_bias,
            grad_decay_log,
            grad_skip_gain,
            grad_conv_kernel,
            grad_conv_bias,
            grad_gated_gain,
            grad_norm_attn,
            grad_norm_ffn,
        ),
        ("dp", "fsdp"),
    )

    def own_part(total, share):
        length = share.shape[-1]
        return lax.dynamic_slice_in_dim(total, own_index() * length, length, total.ndim - 1)

    grad_inputs_step = grad_inputs_step.done()
    rms_stats = jnp.sqrt(totals[:4] / (totals[4] * model_width))
    return (
        stream_three.reshape(row_count, length, model_width),
        grad_zero.reshape(row_count, length, model_width),
        rms_stats,
        table_sum,
        norm_mixer_sum,
        grad_proj_zgate.done(),
        grad_inputs_step[:, :wide],
        grad_inputs_step[:, wide : wide + HM],
        own_part(kernel_sum, conv_kernel),
        own_part(offset_sum, conv_bias),
        bias_total,
        decay_total,
        skip_total,
        own_part(gated_sum, mixer_norm),
        grad_proj_mixed.done(),
        own_part(norm_attn_sum, norm_attn),
        grad_proj_heads.done(),
        grad_proj_attended.done(),
        own_part(norm_ffn_sum, norm_ffn),
        grad_ffn_gate.done(),
        grad_ffn_up.done(),
        grad_ffn_down.done(),
    )


def solution(mesh):
    return jax.shard_map(
        local,
        mesh=mesh,
        in_specs=(
            P(("dp", "fsdp"), None, None),
            P(("dp", "fsdp"), None),
            P(("dp", "fsdp"), None),
            P(("dp", "fsdp"), None, None),
            P(("dp", "fsdp"), None),
            P(("dp", "fsdp")),
            P(("dp", "fsdp"), None),
            P(("dp", "fsdp"), None),
            P(("dp", "fsdp"), None),
            P(None, ("dp", "fsdp")),
            P(("dp", "fsdp")),
            P(),
            P(),
            P(),
            P(("dp", "fsdp")),
            P(("dp", "fsdp"), None),
            P(("dp", "fsdp")),
            P(("dp", "fsdp"), None),
            P(("dp", "fsdp"), None),
            P(("dp", "fsdp")),
            P(("dp", "fsdp"), None),
            P(("dp", "fsdp"), None),
            P(("dp", "fsdp"), None),
        ),
        out_specs=(
            P(("dp", "fsdp"), None, None),
            P(("dp", "fsdp"), None, None),
            P(),
            P(("dp", "fsdp"), None),
            P(("dp", "fsdp")),
            P(("dp", "fsdp"), None),
            P(("dp", "fsdp"), None),
            P(("dp", "fsdp"), None),
            P(None, ("dp", "fsdp")),
            P(("dp", "fsdp")),
            P(),
            P(),
            P(),
            P(("dp", "fsdp")),
            P(("dp", "fsdp"), None),
            P(("dp", "fsdp")),
            P(("dp", "fsdp"), None),
            P(("dp", "fsdp"), None),
            P(("dp", "fsdp")),
            P(("dp", "fsdp"), None),
            P(("dp", "fsdp"), None),
            P(("dp", "fsdp"), None),
        ),
        check_vma=False,
    )
```

```python
from functools import partial

import jax
import jax.numpy as jnp
from jax import lax
from jax.experimental import pallas as pl
from jax.experimental.pallas import tpu as pltpu
from jax.sharding import PartitionSpec as P

DI = 2048
NS = 128
PM = 64
HD = 64
HM = 32


EPS = 1e-05


def matmul(former, latter):
    return jnp.dot(former, latter, preferred_element_type=jnp.float32)


def matmul_left(former, latter):
    return lax.dot_general(
        former, latter, (((0,), (0,)), ((), ())), preferred_element_type=jnp.float32
    )


def matmul_right(former, latter):
    return lax.dot_general(
        former, latter, (((1,), (1,)), ((), ())), preferred_element_type=jnp.float32
    )


def rms_norm(values, scaling):
    return values * lax.rsqrt(jnp.mean(values * values, axis=-1, keepdims=True) + EPS) * scaling


VMEM_LIMIT = 48 * 1024 * 1024
BRIEF = pl.CostEstimate(flops=1024, transcendentals=0, bytes_accessed=1024)


def column_sum(v):
    return jnp.sum(v, axis=0, keepdims=True)


def sigmoid(v):
    return 1.0 / (1.0 + jnp.exp(-v))


def down_rows(v, count):
    return pltpu.roll(v, count, 0)


def up_rows(v, count):
    return pltpu.roll(v, v.shape[0] - count, 0)


def turned(v):
    length = v.shape[0]
    row = lax.broadcasted_iota(jnp.int32, (length, length), 0)
    column = lax.broadcasted_iota(jnp.int32, (length, length), 1)
    unit = (row == column).astype(jnp.float32)
    return lax.dot_general(
        v,
        unit,
        (((0,), (0,)), ((), ())),
        precision=lax.Precision.HIGHEST,
        preferred_element_type=jnp.float32,
    )


def turned_back(v):
    length = v.shape[1]
    row = lax.broadcasted_iota(jnp.int32, (length, length), 0)
    column = lax.broadcasted_iota(jnp.int32, (length, length), 1)
    unit = (row == column).astype(jnp.float32)
    return lax.dot_general(
        unit,
        v,
        (((1,), (1,)), ((), ())),
        precision=lax.Precision.HIGHEST,
        preferred_element_type=jnp.float32,
    )


def allowed_mask(ids_column, ids_row):
    length = ids_column.shape[0]
    row = lax.broadcasted_iota(jnp.int32, (length, length), 0)
    column = lax.broadcasted_iota(jnp.int32, (length, length), 1)
    return (ids_column == ids_row) & (row >= column)


def link_columns(ids_column, taps):
    length = ids_column.shape[0]
    place = lax.broadcasted_iota(jnp.int32, (length, 128), 0)
    wide = jnp.broadcast_to(ids_column, (length, 128))
    return [
        ((down_rows(wide, j) == wide) & (place >= j)).astype(jnp.float32)[:, :1]
        for j in range(1, taps)
    ]


def conv_chunk(raw, taps_chunk, offset, links):
    taps = taps_chunk.shape[0]
    shifted = [raw] + [down_rows(raw, j) * links[j - 1] for j in range(1, taps)]
    total = offset
    for j in range(taps):
        total = total + shifted[j] * taps_chunk[taps - 1 - j : taps - j]
    return total, shifted


def step_terms(step_raw, step_bias, decay_log):
    shifted = step_raw + step_bias
    step = jnp.maximum(shifted, 0.0) + jnp.log1p(jnp.exp(-jnp.abs(shifted)))
    rate = -jnp.exp(decay_log) * step
    length = step.shape[0]
    place = lax.broadcasted_iota(jnp.int32, step.shape, 0)
    total = rate
    shift = 1
    while shift < length:
        total = total + jnp.where(place >= shift, down_rows(total, shift), 0.0)
        shift *= 2
    return shifted, step, rate, total


def mixer_forward_kernel(
    raw_ref, zgate_ref, ids_column_ref, ids_row_ref, taps_ref, offset_ref,
    bias_ref, decay_ref, skip_ref, gain_ref,
    values_ref, states_ref, combined_ref, gate_ref,
):
    taps = taps_ref.shape[0]
    ids_column = ids_column_ref[0]
    links = link_columns(ids_column, taps)
    channels = taps_ref.shape[1]
    for start in range(0, channels, 256):
        part = slice(start, start + 256)
        total, _ = conv_chunk(raw_ref[0, :, part], taps_ref[:, part], offset_ref[:, part], links)
        low = (total * sigmoid(total)).astype(jnp.bfloat16)
        if start < DI:
            values_ref[0, :, part] = low
        else:
            states_ref[0] = low
    state_in, state_out = states_ref[0, :, :NS], states_ref[0, :, NS:]
    gram = matmul_right(state_out, state_in)
    _, step, _, total = step_terms(
        raw_ref[0, :, channels : channels + 128], bias_ref[...], decay_ref[...]
    )
    total_rows, step_rows = turned(total), turned(step)
    mask = allowed_mask(ids_column, ids_row_ref[0])
    gram = jnp.where(mask, gram, 0.0)
    length = gram.shape[0]
    first = lax.broadcasted_iota(jnp.int32, (length, 2 * PM), 1) < PM
    squares = jnp.zeros((length, 1), jnp.float32)
    for pair in range(HM // 2):
        lanes = slice(pair * 2 * PM, (pair + 1) * 2 * PM)
        values = values_ref[0, :, lanes]
        outs = []
        for head in (2 * pair, 2 * pair + 1):
            between = total[:, head : head + 1] - total_rows[head : head + 1, :]
            decayed = jnp.exp(jnp.where(mask, between, 0.0))
            mix = gram * decayed * step_rows[head : head + 1, :]
            outs.append(matmul(mix.astype(jnp.bfloat16), values))
        combined = jnp.where(first, outs[0], outs[1]) + skip_ref[:, lanes] * values.astype(
            jnp.float32
        )
        combined_ref[0, :, lanes] = combined
        zgate = zgate_ref[0, :, lanes]
        gated = combined * (zgate * sigmoid(zgate))
        squares = squares + jnp.sum(gated * gated, axis=1, keepdims=True)
    scale = lax.rsqrt(squares / DI + EPS)
    for start in range(0, DI, 256):
        part = slice(start, start + 256)
        zgate = zgate_ref[0, :, part]
        gated = combined_ref[0, :, part] * (zgate * sigmoid(zgate))
        gate_ref[0, :, part] = (gated * scale * gain_ref[:, part]).astype(jnp.bfloat16)


def gate_backward_kernel(
    grad_ref, zgate_ref, gain_ref, values_ref, combined_ref,
    zgrad_ref, heads_ref, gain_grad_ref, skip_grad_ref,
):
    @pl.when(pl.program_id(0) == 0)
    def _():
        for ref in (gain_grad_ref, skip_grad_ref):
            ref[...] = jnp.zeros(ref.shape, ref.dtype)

    length = grad_ref.shape[1]
    squares = jnp.zeros((length, 1), jnp.float32)
    product = jnp.zeros((length, 1), jnp.float32)
    for start in range(0, DI, 256):
        part = slice(start, start + 256)
        zgate = zgate_ref[0, :, part]
        gated = combined_ref[0, :, part] * (zgate * sigmoid(zgate))
        squares = squares + jnp.sum(gated * gated, axis=1, keepdims=True)
        product = product + jnp.sum(
            gated * grad_ref[0, :, part] * gain_ref[:, part], axis=1, keepdims=True
        )
    scale = lax.rsqrt(squares / DI + EPS)
    inner = scale * scale * scale * (product / DI)
    for start in range(0, DI, 256):
        part = slice(start, start + 256)
        zgate = zgate_ref[0, :, part]
        combined = combined_ref[0, :, part]
        sig = sigmoid(zgate)
        silu = zgate * sig
        gated = combined * silu
        grad = grad_ref[0, :, part]
        gain_grad_ref[:, part] += column_sum(grad * gated * scale)
        grad_gated = scale * grad * gain_ref[:, part] - gated * inner
        grad_combined = grad_gated * silu
        zgrad_ref[0, :, part] = (grad_gated * combined * (sig + silu * (1.0 - sig))).astype(
            jnp.bfloat16
        )
        skip_grad_ref[:, part] += column_sum(
            grad_combined * values_ref[0, :, part].astype(jnp.float32)
        )
        heads_ref[0, :, part] = grad_combined.astype(jnp.bfloat16)


def mixer_backward_kernel(
    heads_ref, raw_ref, ids_column_ref, ids_row_ref, taps_ref, offset_ref,
    bias_ref, decay_ref, skip_ref, values_ref, states_ref,
    xgrad_ref, taps_grad_ref, offset_grad_ref, bias_grad_ref, decay_grad_ref, through_ref,
):
    taps = taps_ref.shape[0]
    channels = taps_ref.shape[1]
    length = raw_ref.shape[1]

    @pl.when(pl.program_id(0) == 0)
    def _():
        for ref in (taps_grad_ref, offset_grad_ref, bias_grad_ref, decay_grad_ref):
            ref[...] = jnp.zeros(ref.shape, ref.dtype)

    ids_column = ids_column_ref[0]
    links = link_columns(ids_column, taps)
    state_in, state_out = states_ref[0, :, :NS], states_ref[0, :, NS:]
    shifted_step, step, rate, total = step_terms(
        raw_ref[0, :, channels : channels + 128], bias_ref[...], decay_ref[...]
    )
    total_rows, step_rows = turned(total), turned(step)
    mask = allowed_mask(ids_column, ids_row_ref[0])
    gram = jnp.where(mask, matmul_right(state_out, state_in), 0.0)
    first = lax.broadcasted_iota(jnp.int32, (length, 2 * PM), 1) < PM
    lane = lax.broadcasted_iota(jnp.int32, (length, 128), 1)
    row = lax.broadcasted_iota(jnp.int32, (128, length), 0)
    grad_gram = jnp.zeros((length, length), jnp.float32)
    by_row = jnp.zeros((length, 128), jnp.float32)
    by_column = jnp.zeros((128, length), jnp.float32)
    nothing = jnp.zeros((length, 2 * PM), jnp.bfloat16)
    for pair in range(HM // 2):
        lanes = slice(pair * 2 * PM, (pair + 1) * 2 * PM)
        values = values_ref[0, :, lanes]
        heads = heads_ref[0, :, lanes]
        outs = []
        for head, own in ((2 * pair, first), (2 * pair + 1, ~first)):
            between = total[:, head : head + 1] - total_rows[head : head + 1, :]
            decayed = jnp.where(mask, jnp.exp(jnp.where(mask, between, 0.0)), 0.0)
            step_row = step_rows[head : head + 1, :]
            mixed = gram * decayed
            grad_mix = matmul_right(jnp.where(own, heads, nothing), values)
            outs.append(matmul_left((mixed * step_row).astype(jnp.bfloat16), heads))
            grad_gram = grad_gram + grad_mix * decayed * step_row
            direct = grad_mix * mixed
            by_column = by_column + jnp.where(row == head, column_sum(direct), 0.0)
            by_row = by_row + jnp.where(
                lane == head, jnp.sum(direct * step_row, axis=1, keepdims=True), 0.0
            )
        through_ref[:, lanes] = jnp.where(first, outs[0], outs[1]) + skip_ref[
            :, lanes
        ] * heads.astype(jnp.float32)
    grad_step = turned_back(by_column)
    grad_total = by_row - grad_step * step
    place = lax.broadcasted_iota(jnp.int32, grad_total.shape, 0)
    shift = 1
    while shift < length:
        grad_total = grad_total + jnp.where(
            place < length - shift, up_rows(grad_total, shift), 0.0
        )
        shift *= 2
    decay_grad_ref[...] += column_sum(grad_total * rate)
    grad_step = grad_step - grad_total * jnp.exp(decay_ref[...])
    grad_raw = jnp.where(lane < HM, grad_step * sigmoid(shifted_step), 0.0)
    bias_grad_ref[...] += column_sum(grad_raw)
    xgrad_ref[0, :, channels : channels + 128] = grad_raw.astype(jnp.bfloat16)
    gram_low = grad_gram.astype(jnp.bfloat16)
    grad_in = matmul_left(gram_low, state_out)
    grad_out = matmul(gram_low, state_in)
    for start in range(0, channels, 128):
        part = slice(start, start + 128)
        chunk_taps = taps_ref[:, part]
        total, shifted = conv_chunk(raw_ref[0, :, part], chunk_taps, offset_ref[:, part], links)
        sig = sigmoid(total)
        if start < DI:
            grad = through_ref[:, part]
        else:
            grad = grad_in if start == DI else grad_out
        grad = grad * (sig + total * sig * (1.0 - sig))
        offset_grad_ref[:, part] += column_sum(grad)
        back = grad * chunk_taps[taps - 1 : taps]
        sums = [column_sum(grad * shifted[0])]
        for j in range(1, taps):
            sums.append(column_sum(grad * shifted[j]))
            linked = grad * links[j - 1]
            back = back + up_rows(linked, j) * chunk_taps[taps - 1 - j : taps - j]
        taps_grad_ref[:, part] += jnp.concatenate(sums[::-1], axis=0)
        xgrad_ref[0, :, part] = back.astype(jnp.bfloat16)


def whole(rows, columns):
    return pl.BlockSpec((rows, columns), lambda n: (0, 0))


def mixer_forward(raw, zgate, ids, taps, offset, bias, decay, skip, gain):
    count, length, columns = raw.shape
    row = lambda c: pl.BlockSpec((1, length, c), lambda n: (n, 0, 0))
    channels = taps.shape[1]
    return pl.pallas_call(
        mixer_forward_kernel,
        grid=(count,),
        in_specs=[
            row(columns), row(DI), row(1), pl.BlockSpec((1, 1, length), lambda n: (n, 0, 0)),
            whole(*taps.shape), whole(1, channels), whole(1, 128), whole(1, 128),
            whole(1, DI), whole(1, DI),
        ],
        out_specs=[row(DI), row(2 * NS), row(DI), row(DI)],
        out_shape=[
            jax.ShapeDtypeStruct((count, length, DI), jnp.bfloat16),
            jax.ShapeDtypeStruct((count, length, 2 * NS), jnp.bfloat16),
            jax.ShapeDtypeStruct((count, length, DI), jnp.float32),
            jax.ShapeDtypeStruct((count, length, DI), jnp.bfloat16),
        ],
        compiler_params=pltpu.CompilerParams(vmem_limit_bytes=VMEM_LIMIT),
        cost_estimate=BRIEF,
    )(raw, zgate, ids[:, :, None], ids[:, None, :], taps, offset, bias, decay, skip, gain)


def gate_backward(grad, zgate, gain, values, combined):
    count, length, _ = grad.shape
    row = lambda c: pl.BlockSpec((1, length, c), lambda n: (n, 0, 0))
    one = lambda r, c: jax.ShapeDtypeStruct((r, c), jnp.float32)
    return pl.pallas_call(
        gate_backward_kernel,
        grid=(count,),
        in_specs=[row(DI), row(DI), whole(1, DI), row(DI), row(DI)],
        out_specs=[row(DI), row(DI), whole(1, DI), whole(1, DI)],
        out_shape=[
            jax.ShapeDtypeStruct((count, length, DI), jnp.bfloat16),
            jax.ShapeDtypeStruct((count, length, DI), jnp.bfloat16),
            one(1, DI), one(1, DI),
        ],
        compiler_params=pltpu.CompilerParams(vmem_limit_bytes=VMEM_LIMIT),
        cost_estimate=BRIEF,
    )(grad, zgate, gain, values, combined)


def mixer_backward(heads, raw, ids, taps, offset, bias, decay, skip, values, states):
    count, length, columns = raw.shape
    row = lambda c: pl.BlockSpec((1, length, c), lambda n: (n, 0, 0))
    channels = taps.shape[1]
    one = lambda r, c: jax.ShapeDtypeStruct((r, c), jnp.float32)
    return pl.pallas_call(
        mixer_backward_kernel,
        grid=(count,),
        in_specs=[
            row(DI), row(columns), row(1),
            pl.BlockSpec((1, 1, length), lambda n: (n, 0, 0)),
            whole(*taps.shape), whole(1, channels), whole(1, 128), whole(1, 128),
            whole(1, DI), row(DI), row(2 * NS),
        ],
        out_specs=[
            row(columns), whole(*taps.shape), whole(1, channels), whole(1, 128), whole(1, 128),
        ],
        out_shape=[
            jax.ShapeDtypeStruct((count, length, columns), jnp.bfloat16),
            one(*taps.shape), one(1, channels), one(1, 128), one(1, 128),
        ],
        scratch_shapes=[pltpu.VMEM((length, DI), jnp.float32)],
        compiler_params=pltpu.CompilerParams(vmem_limit_bytes=VMEM_LIMIT),
        cost_estimate=BRIEF,
    )(heads, raw, ids[:, :, None], ids[:, None, :], taps, offset, bias, decay, skip, values, states)


def head_scores(query, key, own, mask, nothing):
    scores = matmul_right(jnp.where(own, query, nothing), key) * HD ** (-0.5)
    masked = jnp.where(mask, scores, -1e30)
    highest = jnp.max(masked, axis=1, keepdims=True)
    exponents = jnp.exp(masked - highest)
    return exponents / jnp.sum(exponents, axis=1, keepdims=True)


def attention_forward_kernel(joined_ref, ids_column_ref, ids_row_ref, out_ref):
    mask = allowed_mask(ids_column_ref[0], ids_row_ref[0])
    length, width = out_ref.shape[1:]
    first = lax.broadcasted_iota(jnp.int32, (length, 2 * HD), 1) < HD
    nothing = jnp.zeros((length, 2 * HD), jnp.bfloat16)
    for start in range(0, width, 2 * HD):
        query, key, value = (
            joined_ref[0, :, k * width + start : k * width + start + 2 * HD] for k in range(3)
        )
        outs = []
        for own in (first, ~first):
            chances = head_scores(query, key, own, mask, nothing)
            outs.append(matmul(chances.astype(jnp.bfloat16), value))
        out_ref[0, :, start : start + 2 * HD] = jnp.where(first, outs[0], outs[1]).astype(
            jnp.bfloat16
        )


def attention_backward_kernel(joined_ref, grad_ref, ids_column_ref, ids_row_ref, *rest):
    out_ref = rest[-1]
    mask = allowed_mask(ids_column_ref[0], ids_row_ref[0])
    length, width = grad_ref.shape[1:]
    first = lax.broadcasted_iota(jnp.int32, (length, 2 * HD), 1) < HD
    nothing = jnp.zeros((length, 2 * HD), jnp.bfloat16)
    scale = HD ** (-0.5)
    for start in range(0, width, 2 * HD):
        query, key, value = (
            joined_ref[0, :, k * width + start : k * width + start + 2 * HD] for k in range(3)
        )
        grad = grad_ref[0, :, start : start + 2 * HD]
        outs = [[], [], []]
        for own in (first, ~first):
            chances = head_scores(query, key, own, mask, nothing)
            grad_chances = matmul_right(jnp.where(own, grad, nothing), value)
            inner = jnp.sum(chances * grad_chances, axis=1, keepdims=True)
            grad_scores = (chances * (grad_chances - inner)).astype(jnp.bfloat16)
            outs[0].append(matmul(grad_scores, key) * scale)
            outs[1].append(matmul_left(grad_scores, query) * scale)
            outs[2].append(matmul_left(chances.astype(jnp.bfloat16), grad))
        for k in range(3):
            out_ref[0, :, k * width + start : k * width + start + 2 * HD] = jnp.where(
                first, outs[k][0], outs[k][1]
            ).astype(jnp.bfloat16)


def attention_forward(joined, ids):
    count, length, columns = joined.shape
    row = lambda c: pl.BlockSpec((1, length, c), lambda n: (n, 0, 0))
    return pl.pallas_call(
        attention_forward_kernel,
        grid=(count,),
        in_specs=[row(columns), row(1), pl.BlockSpec((1, 1, length), lambda n: (n, 0, 0))],
        out_specs=row(columns // 3),
        out_shape=jax.ShapeDtypeStruct((count, length, columns // 3), jnp.bfloat16),
        compiler_params=pltpu.CompilerParams(vmem_limit_bytes=VMEM_LIMIT),
        cost_estimate=BRIEF,
    )(joined, ids[:, :, None], ids[:, None, :])


def attention_backward(joined, grad, ids, waits):
    count, length, columns = joined.shape
    row = lambda c: pl.BlockSpec((1, length, c), lambda n: (n, 0, 0))
    return pl.pallas_call(
        attention_backward_kernel,
        grid=(count,),
        in_specs=[
            row(columns), row(columns // 3), row(1),
            pl.BlockSpec((1, 1, length), lambda n: (n, 0, 0)),
        ] + [pl.BlockSpec(memory_space=pl.ANY)] * len(waits),
        out_specs=row(columns),
        out_shape=jax.ShapeDtypeStruct((count, length, columns), jnp.bfloat16),
        compiler_params=pltpu.CompilerParams(vmem_limit_bytes=VMEM_LIMIT),
        cost_estimate=BRIEF,
    )(joined, grad, ids[:, :, None], ids[:, None, :], *waits)


def ffn_kernel(
    rows, fold, source_ref, grad_ref, gate_ref, upper_ref, folded_ref,
    hidden_ref, gate_grad_ref, upper_grad_ref, out_ref, back_ref, down_ref,
):
    @pl.when(pl.program_id(0) == 0)
    def _():
        out_ref[...] = jnp.zeros(out_ref.shape, jnp.float32)
        back_ref[...] = jnp.zeros(back_ref.shape, jnp.float32)

    width = out_ref.shape[1]
    for d in range(folded_ref.shape[0] // rows):
        for q in range(fold):
            place = (d * fold + q) * rows
            down_ref[place : place + rows, :] = folded_ref[
                d * rows : (d + 1) * rows, q * width : (q + 1) * width
            ]
    source, grad = source_ref[...], grad_ref[...]
    gate_pre = matmul(source, gate_ref[...])
    up_pre = matmul(source, upper_ref[...])
    sig = sigmoid(gate_pre)
    silu = gate_pre * sig
    hidden = (silu * up_pre).astype(jnp.bfloat16)
    hidden_ref[...] = hidden
    out_ref[...] += matmul(hidden, down_ref[...])
    grad_hidden = matmul_right(grad, down_ref[...])
    gate_grad = (grad_hidden * up_pre * (sig + silu * (1.0 - sig))).astype(jnp.bfloat16)
    upper_grad = (grad_hidden * silu).astype(jnp.bfloat16)
    gate_grad_ref[...] = gate_grad
    upper_grad_ref[...] = upper_grad
    back_ref[...] += matmul_right(gate_grad, gate_ref[...]) + matmul_right(
        upper_grad, upper_ref[...]
    )


def feed_forward(source, grad, full, rows, hidden_width, fold):
    tokens, width = source.shape
    tile = 512
    steps = hidden_width // tile
    all_rows = lambda c: pl.BlockSpec((tokens, c), lambda j: (0, j))
    fixed = pl.BlockSpec((tokens, width), lambda j: (0, 0))
    down_block = 2 * hidden_width // (fold * width)
    return pl.pallas_call(
        partial(ffn_kernel, rows, fold),
        grid=(steps,),
        in_specs=[
            fixed,
            fixed,
            pl.BlockSpec((width, tile), lambda j: (0, j)),
            pl.BlockSpec((width, tile), lambda j: (0, steps + j)),
            pl.BlockSpec((tile // fold, fold * width), lambda j: (j, down_block)),
        ],
        out_specs=[all_rows(tile)] * 3 + [fixed] * 2,
        out_shape=[jax.ShapeDtypeStruct((tokens, hidden_width), jnp.bfloat16)] * 3
        + [jax.ShapeDtypeStruct((tokens, width), jnp.float32)] * 2,
        scratch_shapes=[pltpu.VMEM((tile, width), jnp.bfloat16)],
        compiler_params=pltpu.CompilerParams(vmem_limit_bytes=VMEM_LIMIT),
        cost_estimate=BRIEF,
    )(source, grad, full, full, full)


AXES = ("dp", "fsdp")


def axis_bits():
    bits = []
    for name in AXES:
        size = lax.axis_size(name)
        step = size // 2
        while step:
            bits.append((name, size, step))
            step //= 2
    return bits


def phases(flip):
    bits = axis_bits()
    outer = [k for k, b in enumerate(bits) if b[0] == "dp" and b[2] > 1]
    core = [k for k, b in enumerate(bits) if b[0] == "dp" and b[2] == 1]
    inner = [k for k, b in enumerate(bits) if b[0] == "fsdp"]
    return bits, outer + (inner if flip else inner[::-1]) + core


def swap(v, bit):
    name, size, step = bit
    return lax.ppermute(v, name, [(i, i ^ step) for i in range(size)])


def own_bit(bit):
    return (lax.axis_index(bit[0]) // bit[2]) % 2


def own_index():
    return lax.axis_index("dp") * lax.axis_size("fsdp") + lax.axis_index("fsdp")


def bit_weight(bit):
    return bit[2] * (lax.axis_size("fsdp") if bit[0] == "dp" else 1)


def assemble_kernel(offsets, me_ref, *refs):
    pieces, out_ref, sems = refs[:-2], refs[-2], refs[-1]
    me = me_ref[0]
    copies = []
    count = 0
    for piece, places in zip(pieces, offsets):
        for j, place in enumerate(places):
            copies.append(
                pltpu.make_async_copy(piece.at[j], out_ref.at[me ^ place], sems.at[count])
            )
            count += 1
    for c in copies:
        c.start()
    for c in copies:
        c.wait()


def tie(*values):
    return lax.optimization_barrier(values)


class Gather:
    def __init__(self, shard, flip):
        self.rows, self.columns = shard.shape
        self.bits, self.order = phases(flip)
        self.pieces = [(shard[None], [0])]
        self.phase = 0

    def step(self):
        k = self.order[self.phase]
        weight = bit_weight(self.bits[k])
        if len(self.pieces) > 1 and self.phase < len(self.order) - 1:
            joined = jnp.concatenate([p for p, _ in self.pieces], axis=0)
            self.pieces = [(joined, sum((o for _, o in self.pieces), []))]
        self.pieces = self.pieces + [
            (swap(p, self.bits[k]), [o ^ weight for o in offs]) for p, offs in self.pieces
        ]
        self.phase += 1

    def done(self):
        while self.phase < len(self.order):
            self.step()
        count = 2 ** len(self.bits)
        me = own_index().astype(jnp.int32).reshape(1)
        out = pl.pallas_call(
            partial(assemble_kernel, [o for _, o in self.pieces]),
            out_shape=jax.ShapeDtypeStruct((count, self.rows, self.columns), jnp.bfloat16),
            in_specs=[pl.BlockSpec(memory_space=pltpu.SMEM)]
            + [pl.BlockSpec(memory_space=pl.ANY)] * len(self.pieces),
            out_specs=pl.BlockSpec(memory_space=pltpu.VMEM),
            scratch_shapes=[pltpu.SemaphoreType.DMA((count,))],
            compiler_params=pltpu.CompilerParams(vmem_limit_bytes=24 * 1024 * 1024),
            cost_estimate=BRIEF,
        )(me, *[p for p, _ in self.pieces])
        return out.reshape(count * self.rows, self.columns)


def unfold_kernel(start, fold, full_ref, out_ref, sems):
    columns = out_ref.shape[3]
    copies = [
        pltpu.make_async_copy(
            full_ref.at[:, :, pl.ds(start + q * columns, columns)], out_ref.at[:, q], sems.at[q]
        )
        for q in range(fold)
    ]
    for c in copies:
        c.start()
    for c in copies:
        c.wait()


def unfold(full, rows, start, fold, columns):
    count = full.shape[0] // rows
    out = pl.pallas_call(
        partial(unfold_kernel, start, fold),
        out_shape=jax.ShapeDtypeStruct((count, fold, rows, columns), full.dtype),
        in_specs=[pl.BlockSpec(memory_space=pl.ANY)],
        out_specs=pl.BlockSpec(memory_space=pltpu.VMEM),
        scratch_shapes=[pltpu.SemaphoreType.DMA((fold,))],
        compiler_params=pltpu.CompilerParams(vmem_limit_bytes=24 * 1024 * 1024),
        cost_estimate=BRIEF,
    )(full.reshape(count, rows, full.shape[1]))
    return out.reshape(count * fold * rows, columns)


def gather_round(gathers, values=(), fresh=()):
    sizes = [len(g.pieces) for g in gathers]
    tied = tie(
        *values, *[g.pieces[0][0] for g in fresh], *[p for g in gathers for p, _ in g.pieces]
    )
    head = len(values)
    for g in fresh:
        g.pieces[0] = (tied[head], g.pieces[0][1])
        head += 1
    for g, size in zip(gathers, sizes):
        g.pieces = [(tied[head + k], g.pieces[k][1]) for k in range(size)]
        head += size
    for g in [*gathers, *fresh]:
        if g.phase < len(g.order):
            g.step()
    return tied[: len(values)]


def gather_small(shard):
    bits = axis_bits()
    out = shard[None]
    for bit in bits[::-1]:
        other = swap(out, bit)
        mine = own_bit(bit) == 0
        out = jnp.concatenate([jnp.where(mine, out, other), jnp.where(mine, other, out)], axis=0)
    return out


def scatter_sum(part, flip, core_done, wide=False):
    bits, order = phases(flip)
    names = [k for k in range(len(bits)) if not (core_done and bits[k][0] == "dp" and bits[k][2] == 1)]
    count = 2 ** len(names)
    part = part.reshape([2] * len(names) + [part.shape[0] // count, part.shape[1]])
    for n, k in enumerate([k for k in order[::-1] if k in names]):
        axis = names.index(k)
        names.remove(k)
        mine = own_bit(bits[k])
        send = lax.dynamic_index_in_dim(part, 1 - mine, axis, keepdims=False)
        keep = lax.dynamic_index_in_dim(part, mine, axis, keepdims=False)
        total = keep.astype(jnp.float32) + swap(send, bits[k]).astype(jnp.float32)
        part = total if not names else total.astype(part.dtype)
    return part.astype(jnp.float32)


def core_columns(former, core):
    outer = lax.axis_size("dp") // 2
    group = former.shape[1] // (2 * outer)
    return jnp.concatenate(
        [lax.dynamic_slice_in_dim(former, (2 * i + core) * group, group, 1) for i in range(outer)],
        axis=1,
    )


def grads_kernel(plan, rows, counts, core_ref, *refs):
    formers, latters = refs[: counts[0]], refs[counts[0] : counts[0] + counts[1]]
    products = {}
    for out_ref, items in zip(refs[counts[0] + counts[1] :], plan):
        start = 0
        for former, latter, fold, low, high in items:
            if (former, latter) not in products:
                products[former, latter] = matmul_left(
                    formers[former][...], latters[latter][...]
                ).astype(jnp.bfloat16)
            product = products[former, latter]
            if fold == 1:
                out_ref[:, start : start + high - low] = product[:, low:high]
            else:
                width = product.shape[1]
                for d in range(product.shape[0] // (fold * rows)):
                    for q in range(low // width, high // width):
                        to = start + q * width - low
                        place = (d * fold + q) * rows
                        out_ref[d * rows : (d + 1) * rows, to : to + width] = product[
                            place : place + rows, :
                        ]
            start += high - low


def part_grads(formers, latters, plan, rows, core):
    tokens = formers[0].shape[0]
    outer = lax.axis_size("dp") // 2
    groups = [f.shape[1] // (2 * outer) for f in formers]
    height = rows * lax.axis_size("fsdp")
    widths = [sum(item[4] - item[3] for item in items) for items in plan]
    shapes = [jax.ShapeDtypeStruct((outer * height, w), jnp.bfloat16) for w in widths]
    if any(g % 128 for g in groups):
        outs = []
        for items in plan:
            parts = []
            for former, latter, fold, low, high in items:
                product = matmul_left(core_columns(formers[former], core), latters[latter])
                width = product.shape[1]
                product = jnp.swapaxes(product.reshape(-1, fold, rows, width), 1, 2)
                parts.append(product.reshape(-1, fold * width)[:, low:high])
            outs.append(jnp.concatenate(parts, axis=1).astype(jnp.bfloat16))
        return outs
    return pl.pallas_call(
        partial(grads_kernel, plan, rows, (len(formers), len(latters))),
        grid_spec=pltpu.PrefetchScalarGridSpec(
            num_scalar_prefetch=1,
            grid=(outer,),
            in_specs=[pl.BlockSpec((tokens, g), lambda i, c: (0, 2 * i + c[0])) for g in groups]
            + [pl.BlockSpec(v.shape, lambda i, c: (0, 0)) for v in latters],
            out_specs=[pl.BlockSpec((height, w), lambda i, c: (i, 0)) for w in widths],
        ),
        out_shape=shapes,
        compiler_params=pltpu.CompilerParams(vmem_limit_bytes=VMEM_LIMIT),
        cost_estimate=BRIEF,
    )(core.astype(jnp.int32).reshape(1), *formers, *latters)


class Scatter:
    def __init__(self, send, keep, flip):
        self.bits, order = phases(flip)
        self.core = [k for k, b in enumerate(self.bits) if b[0] == "dp" and b[2] == 1][0]
        self.received = swap(send, self.bits[self.core])
        self.keep = keep
        self.names = [k for k in range(len(self.bits)) if k != self.core]
        self.order = [k for k in order[::-1] if k != self.core]
        self.partner = None

    def step(self):
        self.send = None
        keep, received = self.keep, self.received
        if not self.names:
            self.keep = keep.astype(jnp.float32) + received.astype(jnp.float32)
            self.received = None
            return
        shape = [2] * len(self.names) + [-1, keep.shape[-1]]
        keep, received = keep.reshape(shape), received.reshape(shape)
        k = self.order.pop(0)
        axis = self.names.index(k)
        self.names.remove(k)
        mine = own_bit(self.bits[k])

        def half(which):
            former, latter = (
                lax.dynamic_index_in_dim(v, which, axis, keepdims=False).astype(jnp.float32)
                for v in (keep, received)
            )
            return (former + latter).astype(jnp.bfloat16)

        self.send = (half(1 - mine), self.bits[k])
        self.keep = half(mine)

    def merge(self):
        other = self.partner
        if other is None or self.send is None or self.send[1][0] != "dp":
            return
        side_by_side = lambda *v: jnp.concatenate(v, axis=-1)
        self.send = (side_by_side(self.send[0], other.send[0]), self.send[1])
        self.keep = side_by_side(self.keep, other.keep)
        self.partner = other.received = other.send = None

    def launch(self):
        if self.send is not None:
            self.received = swap(*self.send)

    def done(self):
        while self.received is not None:
            self.step()
            self.launch()
        return self.keep


def scatter_pair(formers, latters, plan, rows):
    mine = own_bit(("dp", lax.axis_size("dp"), 1))
    sends = part_grads(formers, latters, plan, rows, 1 - mine)
    keeps = part_grads(formers, latters, plan, rows, mine)
    pair = [Scatter(send, keep, flip) for send, keep, flip in zip(sends, keeps, (False, True))]
    pair[0].partner = pair[1]
    return pair


class SmallScatter:
    def __init__(self, part):
        self.bits, order = phases(False)
        self.names = list(range(len(self.bits)))
        self.order = order[::-1]
        self.keep = part.reshape([2] * len(self.bits) + [1, part.shape[1]])
        self.received = None
        self.step()
        self.launch()

    def step(self):
        self.send = None
        if self.received is not None:
            self.keep = self.keep + self.received
            self.received = None
        if not self.names:
            return
        k = self.order.pop(0)
        axis = self.names.index(k)
        self.names.remove(k)
        mine = own_bit(self.bits[k])
        self.send = (
            lax.dynamic_index_in_dim(self.keep, 1 - mine, axis, keepdims=False), self.bits[k]
        )
        self.keep = lax.dynamic_index_in_dim(self.keep, mine, axis, keepdims=False)

    launch = Scatter.launch
    done = Scatter.done


class SmallSum:
    def __init__(self, part):
        bits, order = phases(False)
        self.bits = bits
        self.names = order[::-1]
        self.keep = part
        self.received = swap(part, bits[self.names.pop(0)])

    def step(self):
        self.keep = self.keep + self.received
        self.received = None
        self.send = (self.keep, self.bits[self.names.pop(0)]) if self.names else None

    launch = Scatter.launch
    done = Scatter.done


def advance(values, pipes):
    pipes = [p for p in pipes if p.received is not None]
    size = len(values)
    tied = tie(*values, *[p.received for p in pipes], *[p.keep for p in pipes])
    for k, p in enumerate(pipes):
        p.received, p.keep = tied[size + k], tied[size + len(pipes) + k]
        p.step()
    for p in pipes:
        if isinstance(p, Scatter):
            p.merge()
    values = tied[:size]
    pipes = [p for p in pipes if p.send is not None]
    tied = tie(*values, *[p.send[0] for p in pipes], *[p.keep for p in pipes])
    for k, p in enumerate(pipes):
        p.send = (tied[size + k], p.send[1])
        p.keep = tied[size + len(pipes) + k]
        p.launch()
    return tied[:size]


def local(
    context,
    byte_ids,
    segment_ids,
    cotangent,
    byte_table,
    norm_mixer,
    proj_zgate,
    proj_inputs,
    proj_step,
    conv_kernel,
    conv_bias,
    step_bias,
    decay_log,
    skip_gain,
    mixer_norm,
    proj_mixed,
    norm_attn,
    proj_heads,
    proj_attended,
    norm_ffn,
    ffn_gate,
    ffn_up,
    ffn_down,
):
    row_count, length = segment_ids.shape
    tokens = row_count * length
    model_width = context.shape[2]
    model_rows = norm_mixer.shape[0]
    small = [
        byte_table.reshape(-1),
        norm_mixer,
        conv_kernel.reshape(-1),
        conv_bias,
        mixer_norm,
        norm_attn,
        norm_ffn,
    ]
    lengths = [v.shape[0] for v in small]
    packed = jnp.concatenate(small)
    packed = jnp.pad(packed, (0, -packed.shape[0] % 1024)).reshape(8, -1)
    everyone = gather_small(packed).reshape(-1, packed.size)
    unpacked = []
    start = 0
    for count in lengths:
        unpacked.append(everyone[:, start : start + count])
        start += count
    table_full = unpacked[0].reshape(-1, byte_table.shape[1])
    gain_one = unpacked[1].reshape(-1)
    taps = conv_kernel.shape[0]
    kernel_full = jnp.swapaxes(
        unpacked[2].reshape(-1, taps, conv_kernel.shape[1]), 0, 1
    ).reshape(taps, -1)
    offset_full = unpacked[3].reshape(-1)
    gated_gain = unpacked[4].reshape(-1)
    gain_two = unpacked[5].reshape(-1)
    gain_three = unpacked[6].reshape(-1)
    wide = proj_inputs.shape[1]
    step_padded = jnp.pad(proj_step, ((0, 0), (0, 128 - proj_step.shape[1])))
    g_inputs = Gather(jnp.concatenate([proj_inputs, step_padded], axis=1), False)
    g_zgate = Gather(proj_zgate, True)
    fold_mixed = proj_mixed.shape[0] // model_rows
    fold_down = ffn_down.shape[0] // model_rows
    folded = lambda v, fold: [v[q * model_rows : (q + 1) * model_rows] for q in range(fold)]
    outer_shard = jnp.concatenate(
        [ffn_gate, ffn_up]
        + folded(ffn_down, fold_down)
        + folded(proj_mixed, fold_mixed)
        + [proj_heads, proj_attended],
        axis=1,
    )
    outer_full = lax.all_gather(outer_shard, AXES, axis=0, tiled=True)
    g_inputs.step()
    g_zgate.step()
    (table_full,) = gather_round([g_inputs, g_zgate], [table_full])
    gather_round([g_inputs, g_zgate])
    gather_round([g_inputs, g_zgate])
    gather_round([g_inputs, g_zgate])
    gather_round([g_inputs, g_zgate])
    inputs_step_full = g_inputs.done()
    zgate_full = g_zgate.done()
    symbols = jnp.arange(table_full.shape[0], dtype=jnp.int32)
    onehot = (byte_ids.reshape(-1)[:, None] == symbols[None, :]).astype(jnp.bfloat16)
    embedded = matmul(onehot, table_full).reshape(tokens, model_width)
    stream_zero = embedded + context.reshape(tokens, model_width).astype(jnp.float32)
    normed_one, norm_one_back = jax.vjp(rms_norm, stream_zero, gain_one.astype(jnp.float32))
    normed_one_low = normed_one.astype(jnp.bfloat16)
    zgate = matmul(normed_one_low, zgate_full).reshape(row_count, length, -1)
    raw = matmul(normed_one_low, inputs_step_full).reshape(row_count, length, -1)
    ids = segment_ids.astype(jnp.float32)
    pad_heads = lambda v: jnp.pad(v, (0, 128 - HM)).reshape(1, 128)
    mixer_terms = (
        ids,
        kernel_full.astype(jnp.float32),
        offset_full.astype(jnp.float32).reshape(1, -1),
        pad_heads(step_bias),
        pad_heads(decay_log),
        jnp.repeat(skip_gain, PM).reshape(1, -1),
        gated_gain.astype(jnp.float32).reshape(1, -1),
    )
    values_low, states_low, combined, gate_low = mixer_forward(raw, zgate, *mixer_terms)
    gate_low = gate_low.reshape(tokens, -1)
    outer_full, _ = tie(outer_full, gate_low)
    hidden_width = ffn_gate.shape[1]
    mixed_start = 2 * hidden_width + fold_down * model_width
    heads_start = mixed_start + fold_mixed * model_width
    attended_start = heads_start + proj_heads.shape[1]
    heads_full = outer_full[:, heads_start:attended_start]
    attended_full = outer_full[:, attended_start:]
    mixed_full = unfold(outer_full, model_rows, mixed_start, fold_mixed, model_width)
    mixer_out = matmul(gate_low, mixed_full)
    stream_one = stream_zero + mixer_out
    normed_two, norm_two_back = jax.vjp(rms_norm, stream_one, gain_two.astype(jnp.float32))
    normed_two_low = normed_two.astype(jnp.bfloat16)
    joined = matmul(normed_two_low, heads_full).astype(jnp.bfloat16)
    joined = joined.reshape(row_count, length, -1)
    attended_low = attention_forward(joined, ids).reshape(tokens, model_width)
    attn_out = matmul(attended_low, attended_full)
    stream_two = stream_one + attn_out
    normed_three, norm_three_back = jax.vjp(rms_norm, stream_two, gain_three.astype(jnp.float32))
    normed_three_low = normed_three.astype(jnp.bfloat16)
    ffn_grad_low = cotangent.reshape(tokens, model_width)
    grad_three = ffn_grad_low.astype(jnp.float32)
    hidden_low, gate_grad_low, upper_grad_low, ffn_out, grad_normed_three = feed_forward(
        normed_three_low, ffn_grad_low, outer_full, model_rows, hidden_width, fold_down
    )
    stream_three = stream_two + ffn_out
    valid_rows = (segment_ids.reshape(tokens, 1) >= 0).astype(jnp.float32)
    moments = jnp.stack(
        [
            jnp.sum(valid_rows * stream_zero * stream_zero),
            jnp.sum(valid_rows * mixer_out * mixer_out),
            jnp.sum(valid_rows * attn_out * attn_out),
            jnp.sum(valid_rows * ffn_out * ffn_out),
            jnp.sum(valid_rows),
        ]
    )
    fold_width = fold_down * model_width
    pipes = scatter_pair(
        [normed_three_low, hidden_low],
        [gate_grad_low, upper_grad_low, ffn_grad_low],
        [
            [(0, 0, 1, 0, hidden_width), (1, 2, fold_down, 0, fold_width // 2)],
            [(0, 1, 1, 0, hidden_width), (1, 2, fold_down, fold_width // 2, fold_width)],
        ],
        model_rows,
    )
    s_ffn = pipes[0]
    stream_part, grad_norm_ffn = norm_three_back(grad_normed_three)
    grad_two = grad_three + stream_part
    attn_grad_low = grad_two.astype(jnp.bfloat16)
    attn_grad_low, grad_two = advance((attn_grad_low, grad_two), pipes)
    grad_attended = (
        matmul_right(attn_grad_low, attended_full)
        .astype(jnp.bfloat16)
        .reshape(row_count, length, model_width)
    )
    grad_joined = attention_backward(joined, grad_attended, ids, []).reshape(tokens, -1)
    (grad_joined,) = advance((grad_joined,), pipes)
    heads_width = proj_heads.shape[1]
    cut_heads = (heads_width + model_width) // 2
    pair = scatter_pair(
        [normed_two_low, attended_low],
        [grad_joined, attn_grad_low],
        [
            [(0, 0, 1, 0, cut_heads)],
            [(0, 0, 1, cut_heads, heads_width), (1, 1, 1, 0, model_width)],
        ],
        model_rows,
    )
    s_heads = pair[0]
    pipes += pair
    grad_normed_two = matmul_right(grad_joined, heads_full)
    stream_part_two, grad_norm_attn = norm_two_back(grad_normed_two)
    grad_one = grad_two + stream_part_two
    mixer_grad_low = grad_one.astype(jnp.bfloat16)
    mixer_grad_low, grad_one = advance((mixer_grad_low, grad_one), pipes)
    grad_normed_gate = matmul_right(mixer_grad_low, mixed_full).reshape(row_count, length, -1)
    zgate_grad_low, heads_grad_low, grad_gated_gain, skip_lanes = gate_backward(
        grad_normed_gate, zgate, mixer_terms[-1], values_low, combined
    )
    zgate_grad_low = zgate_grad_low.reshape(tokens, -1)
    pair = scatter_pair(
        [normed_one_low, gate_low],
        [zgate_grad_low, mixer_grad_low],
        [
            [(0, 0, 1, 0, zgate_grad_low.shape[1])],
            [(1, 1, fold_mixed, 0, fold_mixed * model_width)],
        ],
        model_rows,
    )
    s_zgate = pair[0]
    pipes += pair
    zgate_grad_low, heads_grad_low = advance((zgate_grad_low, heads_grad_low), pipes)
    inputs_step_grad_low, grad_conv_kernel, grad_conv_bias, bias_lanes, decay_lanes = (
        mixer_backward(heads_grad_low, raw, *mixer_terms[:-1], values_low, states_low)
    )
    inputs_step_grad_low = inputs_step_grad_low.reshape(tokens, -1)
    (inputs_step_grad_low,) = advance((inputs_step_grad_low,), pipes)
    channels = inputs_step_grad_low.shape[1]
    middle = (channels // 256) * 128
    pair = scatter_pair(
        [normed_one_low],
        [inputs_step_grad_low],
        [[(0, 0, 1, 0, middle)], [(0, 0, 1, middle, channels)]],
        model_rows,
    )
    s_inputs = pair[0]
    pipes = pair + pipes
    small_grads = [
        moments,
        bias_lanes[0, :HM],
        decay_lanes[0, :HM],
        jnp.sum(skip_lanes.reshape(HM, PM), axis=1),
        grad_conv_kernel.reshape(-1),
        grad_conv_bias.reshape(-1),
        grad_gated_gain.reshape(-1),
        grad_norm_attn,
        grad_norm_ffn,
    ]
    small_lengths = [v.shape[0] for v in small_grads]
    small_packed = jnp.concatenate(small_grads)
    s_small = SmallSum(jnp.pad(small_packed, (0, -small_packed.shape[0] % 1024)).reshape(8, -1))
    pipes += [s_small]
    (inputs_step_grad_low,) = advance((inputs_step_grad_low,), pipes)
    grad_normed_one = matmul_right(zgate_grad_low, zgate_full) + matmul_right(
        inputs_step_grad_low, inputs_step_full
    )
    stream_part_one, grad_norm_mixer = norm_one_back(grad_normed_one)
    grad_zero = grad_one + stream_part_one
    embed_grad_low = grad_zero.reshape(-1, table_full.shape[1]).astype(jnp.bfloat16)
    grad_byte_table = matmul_left(onehot, embed_grad_low)
    late = jnp.concatenate(
        [
            grad_byte_table.reshape(-1, byte_table.size),
            grad_norm_mixer.reshape(-1, model_rows),
        ],
        axis=1,
    )
    late = jnp.pad(late, ((0, 0), (0, -late.shape[1] % 128)))
    s_late = SmallScatter(late)
    pipes = pipes[:2] + [s_late] + pipes[2:]
    while any(p.received is not None for p in pipes):
        advance((), pipes)
    late = s_late.done().reshape(-1)
    grad_inputs_step = s_inputs.done()
    zgate_mixed = s_zgate.done()
    attention_sums = s_heads.done()
    ffn_sums = s_ffn.done()
    half_fold = fold_width // 2
    second = hidden_width + half_fold
    down_sums = [ffn_sums[:, hidden_width:second], ffn_sums[:, second + hidden_width :]]
    zgate_width = zgate_grad_low.shape[1]

    def stacked(v):
        return jnp.concatenate(
            [v[:, q : q + model_width] for q in range(0, v.shape[1], model_width)], axis=0
        )

    table_sum = late[: byte_table.size].reshape(byte_table.shape)
    norm_mixer_sum = late[byte_table.size : byte_table.size + model_rows]
    small_sums = s_small.done().reshape(-1)
    sums = []
    start = 0
    for count in small_lengths:
        sums.append(small_sums[start : start + count])
        start += count
    totals, bias_total, decay_total, skip_total = sums[:4]
    kernel_sum = sums[4].reshape(taps, -1)
    offset_sum, gated_sum, norm_attn_sum, norm_ffn_sum = sums[5:]

    def own_part(total, share):
        length = share.shape[-1]
        return lax.dynamic_slice_in_dim(total, own_index() * length, length, total.ndim - 1)

    rms_stats = jnp.sqrt(totals[:4] / (totals[4] * model_width))
    return (
        stream_three.reshape(row_count, length, model_width),
        grad_zero.reshape(row_count, length, model_width),
        rms_stats,
        table_sum,
        norm_mixer_sum,
        zgate_mixed[:, :zgate_width],
        grad_inputs_step[:, :wide],
        grad_inputs_step[:, wide : wide + HM],
        own_part(kernel_sum, conv_kernel),
        own_part(offset_sum, conv_bias),
        bias_total,
        decay_total,
        skip_total,
        own_part(gated_sum, mixer_norm),
        stacked(zgate_mixed[:, zgate_width:]),
        own_part(norm_attn_sum, norm_attn),
        attention_sums[:, :heads_width],
        attention_sums[:, heads_width:],
        own_part(norm_ffn_sum, norm_ffn),
        ffn_sums[:, :hidden_width],
        ffn_sums[:, second : second + hidden_width],
        stacked(jnp.concatenate(down_sums, axis=1)),
    )


def solution(mesh):
    return jax.shard_map(
        local,
        mesh=mesh,
        in_specs=(
            P(("dp", "fsdp"), None, None),
            P(("dp", "fsdp"), None),
            P(("dp", "fsdp"), None),
            P(("dp", "fsdp"), None, None),
            P(("dp", "fsdp"), None),
            P(("dp", "fsdp")),
            P(("dp", "fsdp"), None),
            P(("dp", "fsdp"), None),
            P(("dp", "fsdp"), None),
            P(None, ("dp", "fsdp")),
            P(("dp", "fsdp")),
            P(),
            P(),
            P(),
            P(("dp", "fsdp")),
            P(("dp", "fsdp"), None),
            P(("dp", "fsdp")),
            P(("dp", "fsdp"), None),
            P(("dp", "fsdp"), None),
            P(("dp", "fsdp")),
            P(("dp", "fsdp"), None),
            P(("dp", "fsdp"), None),
            P(("dp", "fsdp"), None),
        ),
        out_specs=(
            P(("dp", "fsdp"), None, None),
            P(("dp", "fsdp"), None, None),
            P(),
            P(("dp", "fsdp"), None),
            P(("dp", "fsdp")),
            P(("dp", "fsdp"), None),
            P(("dp", "fsdp"), None),
            P(("dp", "fsdp"), None),
            P(None, ("dp", "fsdp")),
            P(("dp", "fsdp")),
            P(),
            P(),
            P(),
            P(("dp", "fsdp")),
            P(("dp", "fsdp"), None),
            P(("dp", "fsdp")),
            P(("dp", "fsdp"), None),
            P(("dp", "fsdp"), None),
            P(("dp", "fsdp")),
            P(("dp", "fsdp"), None),
            P(("dp", "fsdp"), None),
            P(("dp", "fsdp"), None),
        ),
        check_vma=False,
    )
```

```python
from functools import partial

import jax
import jax.numpy as jnp
from jax import lax
from jax.experimental import pallas as pl
from jax.experimental.pallas import tpu as pltpu
from jax.sharding import PartitionSpec as P

DI = 2048
NS = 128
PM = 64
HD = 64
HM = 32


EPS = 1e-05


def matmul(former, latter):
    return jnp.dot(former, latter, preferred_element_type=jnp.float32)


def matmul_left(former, latter):
    return lax.dot_general(
        former, latter, (((0,), (0,)), ((), ())), preferred_element_type=jnp.float32
    )


def matmul_right(former, latter):
    return lax.dot_general(
        former, latter, (((1,), (1,)), ((), ())), preferred_element_type=jnp.float32
    )


def rms_norm(values, scaling):
    return values * lax.rsqrt(jnp.mean(values * values, axis=-1, keepdims=True) + EPS) * scaling


VMEM_LIMIT = 48 * 1024 * 1024
BRIEF = pl.CostEstimate(flops=1024, transcendentals=0, bytes_accessed=1024)


def column_sum(v):
    return jnp.sum(v, axis=0, keepdims=True)


def sigmoid(v):
    return 1.0 / (1.0 + jnp.exp(-v))


def down_rows(v, count):
    return pltpu.roll(v, count, 0)


def up_rows(v, count):
    return pltpu.roll(v, v.shape[0] - count, 0)


def turned(v):
    length = v.shape[0]
    row = lax.broadcasted_iota(jnp.int32, (length, length), 0)
    column = lax.broadcasted_iota(jnp.int32, (length, length), 1)
    unit = (row == column).astype(jnp.float32)
    return lax.dot_general(
        v,
        unit,
        (((0,), (0,)), ((), ())),
        precision=lax.Precision.HIGHEST,
        preferred_element_type=jnp.float32,
    )


def turned_back(v):
    length = v.shape[1]
    row = lax.broadcasted_iota(jnp.int32, (length, length), 0)
    column = lax.broadcasted_iota(jnp.int32, (length, length), 1)
    unit = (row == column).astype(jnp.float32)
    return lax.dot_general(
        unit,
        v,
        (((1,), (1,)), ((), ())),
        precision=lax.Precision.HIGHEST,
        preferred_element_type=jnp.float32,
    )


def allowed_mask(ids_column, ids_row):
    length = ids_column.shape[0]
    row = lax.broadcasted_iota(jnp.int32, (length, length), 0)
    column = lax.broadcasted_iota(jnp.int32, (length, length), 1)
    return (ids_column == ids_row) & (row >= column)


def link_columns(ids_column, taps):
    length = ids_column.shape[0]
    place = lax.broadcasted_iota(jnp.int32, (length, 128), 0)
    wide = jnp.broadcast_to(ids_column, (length, 128))
    return [
        ((down_rows(wide, j) == wide) & (place >= j)).astype(jnp.float32)[:, :1]
        for j in range(1, taps)
    ]


def conv_chunk(raw, taps_chunk, offset, links):
    taps = taps_chunk.shape[0]
    shifted = [raw] + [down_rows(raw, j) * links[j - 1] for j in range(1, taps)]
    total = offset
    for j in range(taps):
        total = total + shifted[j] * taps_chunk[taps - 1 - j : taps - j]
    return total, shifted


def step_terms(step_raw, step_bias, decay_log):
    shifted = step_raw + step_bias
    step = jnp.maximum(shifted, 0.0) + jnp.log1p(jnp.exp(-jnp.abs(shifted)))
    rate = -jnp.exp(decay_log) * step
    length = step.shape[0]
    place = lax.broadcasted_iota(jnp.int32, step.shape, 0)
    total = rate
    shift = 1
    while shift < length:
        total = total + jnp.where(place >= shift, down_rows(total, shift), 0.0)
        shift *= 2
    return shifted, step, rate, total


def mixer_forward_kernel(
    raw_ref, zgate_ref, ids_column_ref, ids_row_ref, taps_ref, offset_ref,
    bias_ref, decay_ref, skip_ref, gain_ref,
    values_ref, states_ref, combined_ref, gate_ref,
):
    taps = taps_ref.shape[0]
    ids_column = ids_column_ref[0]
    links = link_columns(ids_column, taps)
    channels = taps_ref.shape[1]
    for start in range(0, channels, 256):
        part = slice(start, start + 256)
        total, _ = conv_chunk(raw_ref[0, :, part], taps_ref[:, part], offset_ref[:, part], links)
        low = (total * sigmoid(total)).astype(jnp.bfloat16)
        if start < DI:
            values_ref[0, :, part] = low
        else:
            states_ref[0] = low
    state_in, state_out = states_ref[0, :, :NS], states_ref[0, :, NS:]
    gram = matmul_right(state_out, state_in)
    _, step, _, total = step_terms(
        raw_ref[0, :, channels : channels + 128], bias_ref[...], decay_ref[...]
    )
    total_rows, step_rows = turned(total), turned(step)
    mask = allowed_mask(ids_column, ids_row_ref[0])
    gram = jnp.where(mask, gram, 0.0)
    length = gram.shape[0]
    first = lax.broadcasted_iota(jnp.int32, (length, 2 * PM), 1) < PM
    squares = jnp.zeros((length, 1), jnp.float32)
    for pair in range(HM // 2):
        lanes = slice(pair * 2 * PM, (pair + 1) * 2 * PM)
        values = values_ref[0, :, lanes]
        outs = []
        for head in (2 * pair, 2 * pair + 1):
            between = total[:, head : head + 1] - total_rows[head : head + 1, :]
            decayed = jnp.exp(jnp.where(mask, between, 0.0))
            mix = gram * decayed * step_rows[head : head + 1, :]
            outs.append(matmul(mix.astype(jnp.bfloat16), values))
        combined = jnp.where(first, outs[0], outs[1]) + skip_ref[:, lanes] * values.astype(
            jnp.float32
        )
        combined_ref[0, :, lanes] = combined
        zgate = zgate_ref[0, :, lanes]
        gated = combined * (zgate * sigmoid(zgate))
        squares = squares + jnp.sum(gated * gated, axis=1, keepdims=True)
    scale = lax.rsqrt(squares / DI + EPS)
    for start in range(0, DI, 256):
        part = slice(start, start + 256)
        zgate = zgate_ref[0, :, part]
        gated = combined_ref[0, :, part] * (zgate * sigmoid(zgate))
        gate_ref[0, :, part] = (gated * scale * gain_ref[:, part]).astype(jnp.bfloat16)


def gate_backward_kernel(
    upper_ref, weight_ref, zgate_ref, gain_ref, values_ref, combined_ref,
    zgrad_ref, heads_ref, gain_grad_ref, skip_grad_ref, grad_ref,
):
    grad_ref[0] = matmul_right(upper_ref[0], weight_ref[...])

    @pl.when(pl.program_id(0) == 0)
    def _():
        for ref in (gain_grad_ref, skip_grad_ref):
            ref[...] = jnp.zeros(ref.shape, ref.dtype)

    length = grad_ref.shape[1]
    squares = jnp.zeros((length, 1), jnp.float32)
    product = jnp.zeros((length, 1), jnp.float32)
    for start in range(0, DI, 256):
        part = slice(start, start + 256)
        zgate = zgate_ref[0, :, part]
        gated = combined_ref[0, :, part] * (zgate * sigmoid(zgate))
        squares = squares + jnp.sum(gated * gated, axis=1, keepdims=True)
        product = product + jnp.sum(
            gated * grad_ref[0, :, part] * gain_ref[:, part], axis=1, keepdims=True
        )
    scale = lax.rsqrt(squares / DI + EPS)
    inner = scale * scale * scale * (product / DI)
    for start in range(0, DI, 256):
        part = slice(start, start + 256)
        zgate = zgate_ref[0, :, part]
        combined = combined_ref[0, :, part]
        sig = sigmoid(zgate)
        silu = zgate * sig
        gated = combined * silu
        grad = grad_ref[0, :, part]
        gain_grad_ref[:, part] += column_sum(grad * gated * scale)
        grad_gated = scale * grad * gain_ref[:, part] - gated * inner
        grad_combined = grad_gated * silu
        zgrad_ref[0, :, part] = (grad_gated * combined * (sig + silu * (1.0 - sig))).astype(
            jnp.bfloat16
        )
        skip_grad_ref[:, part] += column_sum(
            grad_combined * values_ref[0, :, part].astype(jnp.float32)
        )
        heads_ref[0, :, part] = grad_combined.astype(jnp.bfloat16)


def mixer_backward_kernel(
    heads_ref, raw_ref, ids_column_ref, ids_row_ref, taps_ref, offset_ref,
    bias_ref, decay_ref, skip_ref, values_ref, states_ref,
    xgrad_ref, taps_grad_ref, offset_grad_ref, bias_grad_ref, decay_grad_ref, through_ref,
):
    taps = taps_ref.shape[0]
    channels = taps_ref.shape[1]
    length = raw_ref.shape[1]

    @pl.when(pl.program_id(0) == 0)
    def _():
        for ref in (taps_grad_ref, offset_grad_ref, bias_grad_ref, decay_grad_ref):
            ref[...] = jnp.zeros(ref.shape, ref.dtype)

    ids_column = ids_column_ref[0]
    links = link_columns(ids_column, taps)
    state_in, state_out = states_ref[0, :, :NS], states_ref[0, :, NS:]
    shifted_step, step, rate, total = step_terms(
        raw_ref[0, :, channels : channels + 128], bias_ref[...], decay_ref[...]
    )
    total_rows, step_rows = turned(total), turned(step)
    mask = allowed_mask(ids_column, ids_row_ref[0])
    gram = jnp.where(mask, matmul_right(state_out, state_in), 0.0)
    first = lax.broadcasted_iota(jnp.int32, (length, 2 * PM), 1) < PM
    lane = lax.broadcasted_iota(jnp.int32, (length, 128), 1)
    row = lax.broadcasted_iota(jnp.int32, (128, length), 0)
    grad_gram = jnp.zeros((length, length), jnp.float32)
    by_row = jnp.zeros((length, 128), jnp.float32)
    by_column = jnp.zeros((128, length), jnp.float32)
    nothing = jnp.zeros((length, 2 * PM), jnp.bfloat16)
    for pair in range(HM // 2):
        lanes = slice(pair * 2 * PM, (pair + 1) * 2 * PM)
        values = values_ref[0, :, lanes]
        heads = heads_ref[0, :, lanes]
        outs = []
        for head, own in ((2 * pair, first), (2 * pair + 1, ~first)):
            between = total[:, head : head + 1] - total_rows[head : head + 1, :]
            decayed = jnp.where(mask, jnp.exp(jnp.where(mask, between, 0.0)), 0.0)
            step_row = step_rows[head : head + 1, :]
            mixed = gram * decayed
            grad_mix = matmul_right(jnp.where(own, heads, nothing), values)
            outs.append(matmul_left((mixed * step_row).astype(jnp.bfloat16), heads))
            grad_gram = grad_gram + grad_mix * decayed * step_row
            direct = grad_mix * mixed
            by_column = by_column + jnp.where(row == head, column_sum(direct), 0.0)
            by_row = by_row + jnp.where(
                lane == head, jnp.sum(direct * step_row, axis=1, keepdims=True), 0.0
            )
        through_ref[:, lanes] = jnp.where(first, outs[0], outs[1]) + skip_ref[
            :, lanes
        ] * heads.astype(jnp.float32)
    grad_step = turned_back(by_column)
    grad_total = by_row - grad_step * step
    place = lax.broadcasted_iota(jnp.int32, grad_total.shape, 0)
    shift = 1
    while shift < length:
        grad_total = grad_total + jnp.where(
            place < length - shift, up_rows(grad_total, shift), 0.0
        )
        shift *= 2
    decay_grad_ref[...] += column_sum(grad_total * rate)
    grad_step = grad_step - grad_total * jnp.exp(decay_ref[...])
    grad_raw = jnp.where(lane < HM, grad_step * sigmoid(shifted_step), 0.0)
    bias_grad_ref[...] += column_sum(grad_raw)
    xgrad_ref[0, :, channels : channels + 128] = grad_raw.astype(jnp.bfloat16)
    extra = xgrad_ref.shape[2] - channels - 128
    if extra:
        xgrad_ref[0, :, channels + 128 :] = jnp.zeros((length, extra), jnp.bfloat16)
    gram_low = grad_gram.astype(jnp.bfloat16)
    grad_in = matmul_left(gram_low, state_out)
    grad_out = matmul(gram_low, state_in)
    for start in range(0, channels, 128):
        part = slice(start, start + 128)
        chunk_taps = taps_ref[:, part]
        total, shifted = conv_chunk(raw_ref[0, :, part], chunk_taps, offset_ref[:, part], links)
        sig = sigmoid(total)
        if start < DI:
            grad = through_ref[:, part]
        else:
            grad = grad_in if start == DI else grad_out
        grad = grad * (sig + total * sig * (1.0 - sig))
        offset_grad_ref[:, part] += column_sum(grad)
        back = grad * chunk_taps[taps - 1 : taps]
        sums = [column_sum(grad * shifted[0])]
        for j in range(1, taps):
            sums.append(column_sum(grad * shifted[j]))
            linked = grad * links[j - 1]
            back = back + up_rows(linked, j) * chunk_taps[taps - 1 - j : taps - j]
        taps_grad_ref[:, part] += jnp.concatenate(sums[::-1], axis=0)
        xgrad_ref[0, :, part] = back.astype(jnp.bfloat16)


def whole(rows, columns):
    return pl.BlockSpec((rows, columns), lambda n: (0, 0))


def mixer_forward(raw, zgate, ids, taps, offset, bias, decay, skip, gain):
    count, length, columns = raw.shape
    row = lambda c: pl.BlockSpec((1, length, c), lambda n: (n, 0, 0))
    channels = taps.shape[1]
    return pl.pallas_call(
        mixer_forward_kernel,
        grid=(count,),
        in_specs=[
            row(columns), row(DI), row(1), pl.BlockSpec((1, 1, length), lambda n: (n, 0, 0)),
            whole(*taps.shape), whole(1, channels), whole(1, 128), whole(1, 128),
            whole(1, DI), whole(1, DI),
        ],
        out_specs=[row(DI), row(2 * NS), row(DI), row(DI)],
        out_shape=[
            jax.ShapeDtypeStruct((count, length, DI), jnp.bfloat16),
            jax.ShapeDtypeStruct((count, length, 2 * NS), jnp.bfloat16),
            jax.ShapeDtypeStruct((count, length, DI), jnp.float32),
            jax.ShapeDtypeStruct((count, length, DI), jnp.bfloat16),
        ],
        compiler_params=pltpu.CompilerParams(vmem_limit_bytes=VMEM_LIMIT),
        cost_estimate=BRIEF,
    )(raw, zgate, ids[:, :, None], ids[:, None, :], taps, offset, bias, decay, skip, gain)


def gate_backward(upper, weight, zgate, gain, values, combined):
    count, length, width = upper.shape
    row = lambda c: pl.BlockSpec((1, length, c), lambda n: (n, 0, 0))
    one = lambda r, c: jax.ShapeDtypeStruct((r, c), jnp.float32)
    return pl.pallas_call(
        gate_backward_kernel,
        grid=(count,),
        in_specs=[
            row(width), whole(DI, width), row(DI), whole(1, DI), row(DI), row(DI)
        ],
        out_specs=[row(DI), row(DI), whole(1, DI), whole(1, DI)],
        out_shape=[
            jax.ShapeDtypeStruct((count, length, DI), jnp.bfloat16),
            jax.ShapeDtypeStruct((count, length, DI), jnp.bfloat16),
            one(1, DI), one(1, DI),
        ],
        scratch_shapes=[pltpu.VMEM((1, length, DI), jnp.float32)],
        compiler_params=pltpu.CompilerParams(vmem_limit_bytes=VMEM_LIMIT),
        cost_estimate=BRIEF,
    )(upper, weight, zgate, gain, values, combined)


def mixer_backward(heads, raw, ids, taps, offset, bias, decay, skip, values, states):
    count, length, columns = raw.shape
    row = lambda c: pl.BlockSpec((1, length, c), lambda n: (n, 0, 0))
    channels = taps.shape[1]
    extra = -columns % 256
    one = lambda r, c: jax.ShapeDtypeStruct((r, c), jnp.float32)
    return pl.pallas_call(
        mixer_backward_kernel,
        grid=(count,),
        in_specs=[
            row(DI), row(columns), row(1),
            pl.BlockSpec((1, 1, length), lambda n: (n, 0, 0)),
            whole(*taps.shape), whole(1, channels), whole(1, 128), whole(1, 128),
            whole(1, DI), row(DI), row(2 * NS),
        ],
        out_specs=[
            row(columns + extra), whole(*taps.shape), whole(1, channels), whole(1, 128),
            whole(1, 128),
        ],
        out_shape=[
            jax.ShapeDtypeStruct((count, length, columns + extra), jnp.bfloat16),
            one(*taps.shape), one(1, channels), one(1, 128), one(1, 128),
        ],
        scratch_shapes=[pltpu.VMEM((length, DI), jnp.float32)],
        compiler_params=pltpu.CompilerParams(vmem_limit_bytes=VMEM_LIMIT),
        cost_estimate=BRIEF,
    )(heads, raw, ids[:, :, None], ids[:, None, :], taps, offset, bias, decay, skip, values, states)


def head_scores(query, key, own, mask, nothing):
    scores = matmul_right(jnp.where(own, query, nothing), key) * HD ** (-0.5)
    masked = jnp.where(mask, scores, -1e30)
    highest = jnp.max(masked, axis=1, keepdims=True)
    exponents = jnp.exp(masked - highest)
    return exponents / jnp.sum(exponents, axis=1, keepdims=True)


def attention_forward_kernel(joined_ref, ids_column_ref, ids_row_ref, out_ref):
    mask = allowed_mask(ids_column_ref[0], ids_row_ref[0])
    length, width = out_ref.shape[1:]
    first = lax.broadcasted_iota(jnp.int32, (length, 2 * HD), 1) < HD
    nothing = jnp.zeros((length, 2 * HD), jnp.bfloat16)
    for start in range(0, width, 2 * HD):
        query, key, value = (
            joined_ref[0, :, k * width + start : k * width + start + 2 * HD] for k in range(3)
        )
        outs = []
        for own in (first, ~first):
            chances = head_scores(query, key, own, mask, nothing)
            outs.append(matmul(chances.astype(jnp.bfloat16), value))
        out_ref[0, :, start : start + 2 * HD] = jnp.where(first, outs[0], outs[1]).astype(
            jnp.bfloat16
        )


def attention_backward_kernel(
    joined_ref, upper_ref, weight_ref, ids_column_ref, ids_row_ref, out_ref, grad_ref
):
    grad_ref[0] = matmul_right(upper_ref[0], weight_ref[...]).astype(jnp.bfloat16)
    mask = allowed_mask(ids_column_ref[0], ids_row_ref[0])
    length, width = grad_ref.shape[1:]
    first = lax.broadcasted_iota(jnp.int32, (length, 2 * HD), 1) < HD
    nothing = jnp.zeros((length, 2 * HD), jnp.bfloat16)
    scale = HD ** (-0.5)
    for start in range(0, width, 2 * HD):
        query, key, value = (
            joined_ref[0, :, k * width + start : k * width + start + 2 * HD] for k in range(3)
        )
        grad = grad_ref[0, :, start : start + 2 * HD]
        outs = [[], [], []]
        for own in (first, ~first):
            chances = head_scores(query, key, own, mask, nothing)
            grad_chances = matmul_right(jnp.where(own, grad, nothing), value)
            inner = jnp.sum(chances * grad_chances, axis=1, keepdims=True)
            grad_scores = (chances * (grad_chances - inner)).astype(jnp.bfloat16)
            outs[0].append(matmul(grad_scores, key) * scale)
            outs[1].append(matmul_left(grad_scores, query) * scale)
            outs[2].append(matmul_left(chances.astype(jnp.bfloat16), grad))
        for k in range(3):
            out_ref[0, :, k * width + start : k * width + start + 2 * HD] = jnp.where(
                first, outs[k][0], outs[k][1]
            ).astype(jnp.bfloat16)


def attention_forward(joined, ids):
    count, length, columns = joined.shape
    row = lambda c: pl.BlockSpec((1, length, c), lambda n: (n, 0, 0))
    return pl.pallas_call(
        attention_forward_kernel,
        grid=(count,),
        in_specs=[row(columns), row(1), pl.BlockSpec((1, 1, length), lambda n: (n, 0, 0))],
        out_specs=row(columns // 3),
        out_shape=jax.ShapeDtypeStruct((count, length, columns // 3), jnp.bfloat16),
        compiler_params=pltpu.CompilerParams(vmem_limit_bytes=VMEM_LIMIT),
        cost_estimate=BRIEF,
    )(joined, ids[:, :, None], ids[:, None, :])


def attention_backward(joined, upper, full, block, ids):
    count, length, columns = joined.shape
    width = columns // 3
    row = lambda c: pl.BlockSpec((1, length, c), lambda n: (n, 0, 0))
    return pl.pallas_call(
        attention_backward_kernel,
        grid=(count,),
        in_specs=[
            row(columns), row(width), pl.BlockSpec((width, width), lambda n: (0, block)), row(1),
            pl.BlockSpec((1, 1, length), lambda n: (n, 0, 0)),
        ],
        out_specs=row(columns),
        out_shape=jax.ShapeDtypeStruct((count, length, columns), jnp.bfloat16),
        scratch_shapes=[pltpu.VMEM((1, length, width), jnp.bfloat16)],
        compiler_params=pltpu.CompilerParams(vmem_limit_bytes=VMEM_LIMIT),
        cost_estimate=BRIEF,
    )(joined, upper, full, ids[:, :, None], ids[:, None, :])


def norm_backward_kernel(count, *refs):
    acts, weights = refs[:count], refs[count : 2 * count]
    stream_ref, gain_ref, base_ref, total_ref, low_ref, gain_grad_ref, sum_ref = refs[2 * count :]
    step = pl.program_id(0)
    rows = weights[0].shape[0]
    part = 0.0
    for act, weight in zip(acts, weights):
        part = part + matmul_right(act[:, : weight.shape[1]], weight[...])
    sum_ref[:, pl.ds(pl.multiple_of(step * rows, rows), rows)] = part

    @pl.when(step == pl.num_programs(0) - 1)
    def _():
        values, grad, gain = stream_ref[...], sum_ref[...], gain_ref[...]
        scale = lax.rsqrt(jnp.mean(values * values, axis=1, keepdims=True) + EPS)
        gain_grad_ref[...] = column_sum(grad * values * scale)
        scaled = grad * gain
        inner = jnp.mean(scaled * values, axis=1, keepdims=True)
        total = base_ref[...] + scale * scaled - values * (scale * scale * scale * inner)
        total_ref[...] = total
        low_ref[...] = total.astype(jnp.bfloat16)


def norm_backward(pairs, stream, gain, base):
    tokens, width = stream.shape
    rows = width // 4
    fixed = lambda r, c, k=0: pl.BlockSpec((r, c), lambda i: (0, k))
    return pl.pallas_call(
        partial(norm_backward_kernel, len(pairs)),
        grid=(4,),
        in_specs=[fixed(tokens, a.shape[1] if w is None else w, k) for a, k, _, _, w in pairs]
        + [
            pl.BlockSpec((rows, m.shape[1] if w is None else w), lambda i, k=k: (i, k))
            for _, _, m, k, w in pairs
        ]
        + [fixed(tokens, width), fixed(1, width), fixed(tokens, width)],
        out_specs=[fixed(tokens, width), fixed(tokens, width), fixed(1, width)],
        out_shape=[
            jax.ShapeDtypeStruct((tokens, width), jnp.float32),
            jax.ShapeDtypeStruct((tokens, width), jnp.bfloat16),
            jax.ShapeDtypeStruct((1, width), jnp.float32),
        ],
        scratch_shapes=[pltpu.VMEM((tokens, width), jnp.float32)],
        compiler_params=pltpu.CompilerParams(vmem_limit_bytes=VMEM_LIMIT),
        cost_estimate=BRIEF,
    )(*[p[0] for p in pairs], *[p[2] for p in pairs], stream, gain, base)


def ffn_kernel(
    rows, fold, source_ref, grad_ref, gate_ref, upper_ref, folded_ref,
    hidden_ref, gate_grad_ref, upper_grad_ref, out_ref, back_ref, down_ref,
):
    @pl.when(pl.program_id(0) == 0)
    def _():
        out_ref[...] = jnp.zeros(out_ref.shape, jnp.float32)
        back_ref[...] = jnp.zeros(back_ref.shape, jnp.float32)

    width = out_ref.shape[1]
    for d in range(folded_ref.shape[0] // rows):
        for q in range(fold):
            place = (d * fold + q) * rows
            down_ref[place : place + rows, :] = folded_ref[
                d * rows : (d + 1) * rows, q * width : (q + 1) * width
            ]
    source, grad = source_ref[...], grad_ref[...]
    gate_pre = matmul(source, gate_ref[...])
    up_pre = matmul(source, upper_ref[...])
    sig = sigmoid(gate_pre)
    silu = gate_pre * sig
    hidden = (silu * up_pre).astype(jnp.bfloat16)
    hidden_ref[...] = hidden
    out_ref[...] += matmul(hidden, down_ref[...])
    grad_hidden = matmul_right(grad, down_ref[...])
    gate_grad = (grad_hidden * up_pre * (sig + silu * (1.0 - sig))).astype(jnp.bfloat16)
    upper_grad = (grad_hidden * silu).astype(jnp.bfloat16)
    gate_grad_ref[...] = gate_grad
    upper_grad_ref[...] = upper_grad
    back_ref[...] += matmul_right(gate_grad, gate_ref[...]) + matmul_right(
        upper_grad, upper_ref[...]
    )


def feed_forward(source, grad, full, rows, hidden_width, fold):
    tokens, width = source.shape
    tile = 512
    steps = hidden_width // tile
    all_rows = lambda c: pl.BlockSpec((tokens, c), lambda j: (0, j))
    fixed = pl.BlockSpec((tokens, width), lambda j: (0, 0))
    down_block = 2 * hidden_width // (fold * width)
    return pl.pallas_call(
        partial(ffn_kernel, rows, fold),
        grid=(steps,),
        in_specs=[
            fixed,
            fixed,
            pl.BlockSpec((width, tile), lambda j: (0, j)),
            pl.BlockSpec((width, tile), lambda j: (0, steps + j)),
            pl.BlockSpec((tile // fold, fold * width), lambda j: (j, down_block)),
        ],
        out_specs=[all_rows(tile)] * 3 + [fixed] * 2,
        out_shape=[jax.ShapeDtypeStruct((tokens, hidden_width), jnp.bfloat16)] * 3
        + [jax.ShapeDtypeStruct((tokens, width), jnp.float32)] * 2,
        scratch_shapes=[pltpu.VMEM((tile, width), jnp.bfloat16)],
        compiler_params=pltpu.CompilerParams(vmem_limit_bytes=VMEM_LIMIT),
        cost_estimate=BRIEF,
    )(source, grad, full, full, full)


AXES = ("dp", "fsdp")


def axis_bits():
    bits = []
    for name in AXES:
        size = lax.axis_size(name)
        step = size // 2
        while step:
            bits.append((name, size, step))
            step //= 2
    return bits


def phases(flip, turn=False):
    bits = axis_bits()
    outer = [k for k, b in enumerate(bits) if b[0] == "dp" and b[2] > 1]
    core = [k for k, b in enumerate(bits) if b[0] == "dp" and b[2] == 1]
    inner = [k for k, b in enumerate(bits) if b[0] == "fsdp"]
    return bits, (outer[::-1] if turn else outer) + (inner if flip else inner[::-1]) + core


def swap(v, bit):
    name, size, step = bit
    return lax.ppermute(v, name, [(i, i ^ step) for i in range(size)])


def own_bit(bit):
    return (lax.axis_index(bit[0]) // bit[2]) % 2


def own_index():
    return lax.axis_index("dp") * lax.axis_size("fsdp") + lax.axis_index("fsdp")


def bit_weight(bit):
    return bit[2] * (lax.axis_size("fsdp") if bit[0] == "dp" else 1)


def assemble_kernel(offsets, me_ref, *refs):
    pieces, out_ref, sems = refs[:-2], refs[-2], refs[-1]
    me = me_ref[0]
    copies = []
    count = 0
    for piece, places in zip(pieces, offsets):
        for j, place in enumerate(places):
            copies.append(
                pltpu.make_async_copy(piece.at[j], out_ref.at[me ^ place], sems.at[count])
            )
            count += 1
    for c in copies:
        c.start()
    for c in copies:
        c.wait()


def tie(*values):
    return lax.optimization_barrier(values)


class Gather:
    def __init__(self, shard, flip):
        self.rows, self.columns = shard.shape
        self.bits, self.order = phases(flip)
        self.pieces = [(shard[None], [0])]
        self.phase = 0

    def step(self):
        k = self.order[self.phase]
        weight = bit_weight(self.bits[k])
        if len(self.pieces) > 1 and self.phase < len(self.order) - 1:
            joined = jnp.concatenate([p for p, _ in self.pieces], axis=0)
            self.pieces = [(joined, sum((o for _, o in self.pieces), []))]
        self.pieces = self.pieces + [
            (swap(p, self.bits[k]), [o ^ weight for o in offs]) for p, offs in self.pieces
        ]
        self.phase += 1

    def done(self):
        while self.phase < len(self.order):
            self.step()
        count = 2 ** len(self.bits)
        me = own_index().astype(jnp.int32).reshape(1)
        out = pl.pallas_call(
            partial(assemble_kernel, [o for _, o in self.pieces]),
            out_shape=jax.ShapeDtypeStruct((count, self.rows, self.columns), jnp.bfloat16),
            in_specs=[pl.BlockSpec(memory_space=pltpu.SMEM)]
            + [pl.BlockSpec(memory_space=pl.ANY)] * len(self.pieces),
            out_specs=pl.BlockSpec(memory_space=pltpu.VMEM),
            scratch_shapes=[pltpu.SemaphoreType.DMA((count,))],
            compiler_params=pltpu.CompilerParams(vmem_limit_bytes=24 * 1024 * 1024),
            cost_estimate=BRIEF,
        )(me, *[p for p, _ in self.pieces])
        return out.reshape(count * self.rows, self.columns)


def unfold_kernel(start, fold, full_ref, out_ref, sems):
    columns = out_ref.shape[3]
    copies = [
        pltpu.make_async_copy(
            full_ref.at[:, :, pl.ds(start + q * columns, columns)], out_ref.at[:, q], sems.at[q]
        )
        for q in range(fold)
    ]
    for c in copies:
        c.start()
    for c in copies:
        c.wait()


def unfold(full, rows, start, fold, columns):
    count = full.shape[0] // rows
    out = pl.pallas_call(
        partial(unfold_kernel, start, fold),
        out_shape=jax.ShapeDtypeStruct((count, fold, rows, columns), full.dtype),
        in_specs=[pl.BlockSpec(memory_space=pl.ANY)],
        out_specs=pl.BlockSpec(memory_space=pltpu.VMEM),
        scratch_shapes=[pltpu.SemaphoreType.DMA((fold,))],
        compiler_params=pltpu.CompilerParams(vmem_limit_bytes=24 * 1024 * 1024),
        cost_estimate=BRIEF,
    )(full.reshape(count, rows, full.shape[1]))
    return out.reshape(count * fold * rows, columns)


def gather_round(gathers, values=(), fresh=()):
    sizes = [len(g.pieces) for g in gathers]
    tied = tie(
        *values, *[g.pieces[0][0] for g in fresh], *[p for g in gathers for p, _ in g.pieces]
    )
    head = len(values)
    for g in fresh:
        g.pieces[0] = (tied[head], g.pieces[0][1])
        head += 1
    for g, size in zip(gathers, sizes):
        g.pieces = [(tied[head + k], g.pieces[k][1]) for k in range(size)]
        head += size
    for g in [*gathers, *fresh]:
        if g.phase < len(g.order):
            g.step()
    return tied[: len(values)]


def gather_small(shard):
    bits = axis_bits()
    out = shard[None]
    for bit in bits[::-1]:
        other = swap(out, bit)
        mine = own_bit(bit) == 0
        out = jnp.concatenate([jnp.where(mine, out, other), jnp.where(mine, other, out)], axis=0)
    return out


def scatter_sum(part, flip, core_done, wide=False):
    bits, order = phases(flip)
    names = [k for k in range(len(bits)) if not (core_done and bits[k][0] == "dp" and bits[k][2] == 1)]
    count = 2 ** len(names)
    part = part.reshape([2] * len(names) + [part.shape[0] // count, part.shape[1]])
    for n, k in enumerate([k for k in order[::-1] if k in names]):
        axis = names.index(k)
        names.remove(k)
        mine = own_bit(bits[k])
        send = lax.dynamic_index_in_dim(part, 1 - mine, axis, keepdims=False)
        keep = lax.dynamic_index_in_dim(part, mine, axis, keepdims=False)
        total = keep.astype(jnp.float32) + swap(send, bits[k]).astype(jnp.float32)
        part = total if not names else total.astype(part.dtype)
    return part.astype(jnp.float32)


def core_columns(former, core):
    outer = lax.axis_size("dp") // 2
    group = former.shape[1] // (2 * outer)
    return jnp.concatenate(
        [lax.dynamic_slice_in_dim(former, (2 * i + core) * group, group, 1) for i in range(outer)],
        axis=1,
    )


def grads_kernel(plan, rows, counts, core_ref, *refs):
    formers, latters = refs[: counts[0]], refs[counts[0] : counts[0] + counts[1]]
    products = {}
    for out_ref, items in zip(refs[counts[0] + counts[1] :], plan):
        start = 0
        for former, latter, fold, low, high in items:
            if fold == 1:
                for at in range(low, high, 512):
                    to = min(at + 512, high)
                    out_ref[:, start + at - low : start + to - low] = matmul_left(
                        formers[former][...], latters[latter][:, at:to]
                    ).astype(jnp.bfloat16)
            else:
                if (former, latter) not in products:
                    products[former, latter] = matmul_left(
                        formers[former][...], latters[latter][...]
                    ).astype(jnp.bfloat16)
                product = products[former, latter]
                width = product.shape[1]
                for d in range(product.shape[0] // (fold * rows)):
                    for q in range(low // width, high // width):
                        to = start + q * width - low
                        place = (d * fold + q) * rows
                        out_ref[d * rows : (d + 1) * rows, to : to + width] = product[
                            place : place + rows, :
                        ]
            start += high - low


def part_grads(formers, latters, plan, rows, core):
    tokens = formers[0].shape[0]
    outer = lax.axis_size("dp") // 2
    groups = [f.shape[1] // (2 * outer) for f in formers]
    height = rows * lax.axis_size("fsdp")
    widths = [sum(item[4] - item[3] for item in items) for items in plan]
    shapes = [jax.ShapeDtypeStruct((outer * height, w), jnp.bfloat16) for w in widths]
    if any(g % 128 for g in groups):
        outs = []
        for items in plan:
            parts = []
            for former, latter, fold, low, high in items:
                product = matmul_left(core_columns(formers[former], core), latters[latter])
                width = product.shape[1]
                product = jnp.swapaxes(product.reshape(-1, fold, rows, width), 1, 2)
                parts.append(product.reshape(-1, fold * width)[:, low:high])
            outs.append(jnp.concatenate(parts, axis=1).astype(jnp.bfloat16))
        return outs
    return pl.pallas_call(
        partial(grads_kernel, plan, rows, (len(formers), len(latters))),
        grid_spec=pltpu.PrefetchScalarGridSpec(
            num_scalar_prefetch=1,
            grid=(outer,),
            in_specs=[pl.BlockSpec((tokens, g), lambda i, c: (0, 2 * i + c[0])) for g in groups]
            + [pl.BlockSpec(v.shape, lambda i, c: (0, 0)) for v in latters],
            out_specs=[pl.BlockSpec((height, w), lambda i, c: (i, 0)) for w in widths],
        ),
        out_shape=shapes,
        compiler_params=pltpu.CompilerParams(vmem_limit_bytes=VMEM_LIMIT),
        cost_estimate=BRIEF,
    )(core.astype(jnp.int32).reshape(1), *formers, *latters)


def add_halves_kernel(mine_ref, give, give_more, hold, hold_more, send_ref, keep_ref):
    for former, latter, out in ((give, give_more, send_ref), (hold, hold_more, keep_ref)):
        out[...] = (
            former[...].astype(jnp.float32) + latter[...].astype(jnp.float32)
        ).astype(jnp.bfloat16)


def add_halves(keep, received, mine, part=0, parts=1):
    before, _, rows, columns = keep.shape
    columns //= parts
    tiles = 1
    while before * tiles < 4 and columns % (256 * tiles) == 0:
        tiles *= 2
    width = columns // tiles
    several = max(1, before // 4)
    other = pl.BlockSpec((several, None, rows, width), lambda i, j, m: (i, 1 - m[0], 0, part * tiles + j))
    own = pl.BlockSpec((several, None, rows, width), lambda i, j, m: (i, m[0], 0, part * tiles + j))
    out = pl.BlockSpec((several, rows, width), lambda i, j, m: (i, 0, j))
    return pl.pallas_call(
        add_halves_kernel,
        grid_spec=pltpu.PrefetchScalarGridSpec(
            num_scalar_prefetch=1,
            grid=(before // several, tiles),
            in_specs=[other, other, own, own],
            out_specs=[out, out],
        ),
        out_shape=[jax.ShapeDtypeStruct((before, rows, columns), jnp.bfloat16)] * 2,
        compiler_params=pltpu.CompilerParams(vmem_limit_bytes=VMEM_LIMIT),
        cost_estimate=BRIEF,
    )(mine.astype(jnp.int32).reshape(1), keep, received, keep, received)


class Scatter:
    def __init__(self, keep, received, part):
        self.bits, order = phases(part == 1, part == 1)
        core = [k for k, b in enumerate(self.bits) if b[0] == "dp" and b[2] == 1][0]
        self.names = [k for k in range(len(self.bits)) if k != core]
        self.order = [k for k in order[::-1] if k != core]
        self.keep, self.received = keep, received
        self.step(part, 2)

    def step(self, part=0, parts=1):
        self.send = None
        keep, received = self.keep, self.received
        if not self.names:
            total = keep.astype(jnp.float32) + received.astype(jnp.float32)
            self.keep, self.received = total.reshape(-1, total.shape[-1]), None
            return
        k = self.order.pop(0)
        axis = self.names.index(k)
        self.names.remove(k)
        columns = keep.shape[-1]
        shape = (2**axis, 2, keep.size // columns // 2 ** (axis + 1), columns)
        send, self.keep = add_halves(
            keep.reshape(shape), received.reshape(shape), own_bit(self.bits[k]), part, parts
        )
        self.send = (send, self.bits[k])

    def launch(self):
        self.received, self.send = swap(*self.send), None


class Pair:
    def __init__(self, formers, latters, items, rows):
        bit = ("dp", lax.axis_size("dp"), 1)
        self.mine = own_bit(bit)
        self.parts = (formers, latters, [items], rows)
        (send,) = part_grads(*self.parts, 1 - self.mine)
        self.send, self.received, self.keep = (send, bit), None, None

    def own(self):
        (self.keep,) = part_grads(*self.parts, self.mine)
        return self

    def launch(self):
        self.received, self.send = swap(*self.send), None

    def split(self):
        self.pipes = [Scatter(self.keep, self.received, part) for part in range(2)]
        return self.pipes

    def done(self):
        return jnp.concatenate([p.keep for p in self.pipes], axis=1)


class SmallSum:
    def __init__(self, part):
        bits, order = phases(False)
        self.bits = bits
        self.names = order[::-1]
        self.keep, self.received = part, None
        self.send = (part, bits[self.names.pop(0)])

    def step(self):
        self.keep = self.keep + self.received
        self.received = None
        self.send = (self.keep, self.bits[self.names.pop(0)]) if self.names else None

    def launch(self):
        self.received, self.send = swap(*self.send), None

    def done(self):
        return self.keep


def advance(values, pipes):
    live = [p for p in pipes if p.received is not None]
    fresh = [p for p in pipes if p.received is None and p.send is not None]
    size = len(values)
    tied = list(
        tie(
            *values,
            *[p.received for p in live],
            *[p.keep for p in live],
            *[p.send[0] for p in fresh],
        )
    )
    values, tied = tied[:size], tied[size:]
    for p in live:
        p.received = tied.pop(0)
    for p in live:
        p.keep = tied.pop(0)
    for p in fresh:
        p.send = (tied.pop(0), p.send[1])
    now = []
    for p in live:
        if isinstance(p, Pair):
            now += p.split()
        else:
            p.step()
            now.append(p)
    now = [p for p in now + fresh if p.send is not None]
    pipes[:] = now
    held = [p for p in now if p.keep is not None]
    tied = list(tie(*values, *[p.send[0] for p in now], *[p.keep for p in held]))
    values, tied = tied[:size], tied[size:]
    for p in now:
        p.send = (tied.pop(0), p.send[1])
    for p in held:
        p.keep = tied.pop(0)
    for p in now:
        p.launch()
    return values


def local(
    context,
    byte_ids,
    segment_ids,
    cotangent,
    byte_table,
    norm_mixer,
    proj_zgate,
    proj_inputs,
    proj_step,
    conv_kernel,
    conv_bias,
    step_bias,
    decay_log,
    skip_gain,
    mixer_norm,
    proj_mixed,
    norm_attn,
    proj_heads,
    proj_attended,
    norm_ffn,
    ffn_gate,
    ffn_up,
    ffn_down,
):
    row_count, length = segment_ids.shape
    tokens = row_count * length
    model_width = context.shape[2]
    model_rows = norm_mixer.shape[0]
    small = [
        byte_table.reshape(-1),
        norm_mixer,
        conv_kernel.reshape(-1),
        conv_bias,
        mixer_norm,
        norm_attn,
        norm_ffn,
    ]
    lengths = [v.shape[0] for v in small]
    packed = jnp.concatenate(small)
    packed = jnp.pad(packed, (0, -packed.shape[0] % 1024)).reshape(8, -1)
    everyone = gather_small(packed).reshape(-1, packed.size)
    unpacked = []
    start = 0
    for count in lengths:
        unpacked.append(everyone[:, start : start + count])
        start += count
    table_full = unpacked[0].reshape(-1, byte_table.shape[1])
    gain_one = unpacked[1].reshape(-1)
    taps = conv_kernel.shape[0]
    kernel_full = jnp.swapaxes(
        unpacked[2].reshape(-1, taps, conv_kernel.shape[1]), 0, 1
    ).reshape(taps, -1)
    offset_full = unpacked[3].reshape(-1)
    gated_gain = unpacked[4].reshape(-1)
    gain_two = unpacked[5].reshape(-1)
    gain_three = unpacked[6].reshape(-1)
    wide = proj_inputs.shape[1]
    step_padded = jnp.pad(proj_step, ((0, 0), (0, 128 - proj_step.shape[1])))
    g_inputs = Gather(jnp.concatenate([proj_inputs, step_padded], axis=1), False)
    g_zgate = Gather(proj_zgate, True)
    fold_mixed = proj_mixed.shape[0] // model_rows
    fold_down = ffn_down.shape[0] // model_rows
    folded = lambda v, fold: [v[q * model_rows : (q + 1) * model_rows] for q in range(fold)]
    outer_shard = jnp.concatenate(
        [ffn_gate, ffn_up]
        + folded(ffn_down, fold_down)
        + folded(proj_mixed, fold_mixed)
        + [proj_heads, proj_attended],
        axis=1,
    )
    outer_full = lax.all_gather(outer_shard, AXES, axis=0, tiled=True)
    g_inputs.step()
    g_zgate.step()
    (table_full,) = gather_round([g_inputs, g_zgate], [table_full])
    gather_round([g_inputs, g_zgate])
    gather_round([g_inputs, g_zgate])
    gather_round([g_inputs, g_zgate])
    gather_round([g_inputs, g_zgate])
    inputs_step_full = g_inputs.done()
    zgate_full = g_zgate.done()
    symbols = jnp.arange(table_full.shape[0], dtype=jnp.int32)
    onehot = (byte_ids.reshape(-1)[:, None] == symbols[None, :]).astype(jnp.bfloat16)
    embedded = matmul(onehot, table_full).reshape(tokens, model_width)
    stream_zero = embedded + context.reshape(tokens, model_width).astype(jnp.float32)
    normed_one = rms_norm(stream_zero, gain_one.astype(jnp.float32))
    normed_one_low = normed_one.astype(jnp.bfloat16)
    zgate = matmul(normed_one_low, zgate_full).reshape(row_count, length, -1)
    raw = matmul(normed_one_low, inputs_step_full).reshape(row_count, length, -1)
    ids = segment_ids.astype(jnp.float32)
    pad_heads = lambda v: jnp.pad(v, (0, 128 - HM)).reshape(1, 128)
    mixer_terms = (
        ids,
        kernel_full.astype(jnp.float32),
        offset_full.astype(jnp.float32).reshape(1, -1),
        pad_heads(step_bias),
        pad_heads(decay_log),
        jnp.repeat(skip_gain, PM).reshape(1, -1),
        gated_gain.astype(jnp.float32).reshape(1, -1),
    )
    values_low, states_low, combined, gate_low = mixer_forward(raw, zgate, *mixer_terms)
    gate_low = gate_low.reshape(tokens, -1)
    outer_full, _ = tie(outer_full, gate_low)
    hidden_width = ffn_gate.shape[1]
    mixed_start = 2 * hidden_width + fold_down * model_width
    heads_start = mixed_start + fold_mixed * model_width
    attended_start = heads_start + proj_heads.shape[1]
    heads_full = outer_full[:, heads_start:attended_start]
    attended_full = outer_full[:, attended_start:]
    mixed_full = unfold(outer_full, model_rows, mixed_start, fold_mixed, model_width)
    mixer_out = matmul(gate_low, mixed_full)
    stream_one = stream_zero + mixer_out
    normed_two = rms_norm(stream_one, gain_two.astype(jnp.float32))
    normed_two_low = normed_two.astype(jnp.bfloat16)
    joined = matmul(normed_two_low, heads_full).astype(jnp.bfloat16)
    joined = joined.reshape(row_count, length, -1)
    attended_low = attention_forward(joined, ids).reshape(tokens, model_width)
    attn_out = matmul(attended_low, attended_full)
    stream_two = stream_one + attn_out
    normed_three, norm_three_back = jax.vjp(rms_norm, stream_two, gain_three.astype(jnp.float32))
    normed_three_low = normed_three.astype(jnp.bfloat16)
    ffn_grad_low = cotangent.reshape(tokens, model_width)
    grad_three = ffn_grad_low.astype(jnp.float32)
    hidden_low, gate_grad_low, upper_grad_low, ffn_out, grad_normed_three = feed_forward(
        normed_three_low, ffn_grad_low, outer_full, model_rows, hidden_width, fold_down
    )
    stream_three = stream_two + ffn_out
    valid_rows = (segment_ids.reshape(tokens, 1) >= 0).astype(jnp.float32)
    moments = jnp.stack(
        [
            jnp.sum(valid_rows * stream_zero * stream_zero),
            jnp.sum(valid_rows * mixer_out * mixer_out),
            jnp.sum(valid_rows * attn_out * attn_out),
            jnp.sum(valid_rows * ffn_out * ffn_out),
            jnp.sum(valid_rows),
        ]
    )
    fold_width = fold_down * model_width
    s_ffn = Pair(
        [normed_three_low, hidden_low],
        [gate_grad_low, upper_grad_low, ffn_grad_low],
        [
            (0, 0, 1, 0, hidden_width),
            (1, 2, fold_down, 0, fold_width // 2),
            (0, 1, 1, 0, hidden_width),
            (1, 2, fold_down, fold_width // 2, fold_width),
        ],
        model_rows,
    )
    pipes = [s_ffn]
    (grad_normed_three,) = advance((grad_normed_three,), pipes)
    s_ffn.own()
    stream_part, grad_norm_ffn = norm_three_back(grad_normed_three)
    grad_two = grad_three + stream_part
    attn_grad_low = grad_two.astype(jnp.bfloat16)
    attn_grad_low, grad_two = advance((attn_grad_low, grad_two), pipes)
    grad_joined = attention_backward(
        joined,
        attn_grad_low.reshape(row_count, length, model_width),
        outer_full,
        attended_start // model_width,
        ids,
    ).reshape(tokens, -1)
    heads_width = proj_heads.shape[1]
    grad_one, mixer_grad_low, grad_norm_attn = norm_backward(
        [
            (grad_joined, q, outer_full, heads_start // model_width + q, model_width)
            for q in range(3)
        ],
        stream_one,
        gain_two.astype(jnp.float32).reshape(1, -1),
        grad_two,
    )
    grad_norm_attn = grad_norm_attn.reshape(-1)
    zgate_grad_low, heads_grad_low, grad_gated_gain, skip_lanes = gate_backward(
        mixer_grad_low.reshape(row_count, length, model_width),
        mixed_full,
        zgate,
        mixer_terms[-1],
        values_low,
        combined,
    )
    zgate_grad_low = zgate_grad_low.reshape(tokens, -1)
    zgate_width = zgate_grad_low.shape[1]
    s_middle = Pair(
        [normed_two_low, attended_low, normed_one_low, gate_low],
        [grad_joined, attn_grad_low, zgate_grad_low, mixer_grad_low],
        [
            (0, 0, 1, 0, heads_width),
            (1, 1, 1, 0, model_width),
            (2, 2, 1, 0, zgate_width),
            (3, 3, fold_mixed, 0, fold_mixed * model_width),
        ],
        model_rows,
    ).own()
    pipes += [s_middle]
    heads_grad_low, grad_one = advance((heads_grad_low, grad_one), pipes)
    inputs_step_grad_low, grad_conv_kernel, grad_conv_bias, bias_lanes, decay_lanes = (
        mixer_backward(heads_grad_low, raw, *mixer_terms[:-1], values_low, states_low)
    )
    inputs_step_grad_low = inputs_step_grad_low.reshape(tokens, -1)
    inputs_step_grad_low, grad_one = advance((inputs_step_grad_low, grad_one), pipes)
    s_inputs = Pair(
        [normed_one_low],
        [inputs_step_grad_low],
        [(0, 0, 1, 0, inputs_step_grad_low.shape[1])],
        model_rows,
    ).own()
    grad_zero, embed_grad_low, grad_norm_mixer = norm_backward(
        [
            (zgate_grad_low, 0, zgate_full, 0, None),
            (inputs_step_grad_low, 0, inputs_step_full, 0, None),
        ],
        stream_zero,
        gain_one.astype(jnp.float32).reshape(1, -1),
        grad_one,
    )
    grad_norm_mixer = grad_norm_mixer.reshape(-1)
    embed_grad_low = embed_grad_low.reshape(-1, table_full.shape[1])
    grad_byte_table = matmul_left(onehot, embed_grad_low)
    small_grads = [
        moments,
        bias_lanes[0, :HM],
        decay_lanes[0, :HM],
        jnp.sum(skip_lanes.reshape(HM, PM), axis=1),
        grad_conv_kernel.reshape(-1),
        grad_conv_bias.reshape(-1),
        grad_gated_gain.reshape(-1),
        grad_norm_attn,
        grad_norm_ffn,
    ]
    small_lengths = [v.shape[0] for v in small_grads]
    small_packed = jnp.concatenate(small_grads)
    small_packed = jnp.pad(small_packed, (0, -small_packed.shape[0] % 1024)).reshape(-1, 128)
    table_rows = grad_byte_table.shape[0]
    s_small = SmallSum(
        jnp.concatenate([grad_byte_table, grad_norm_mixer.reshape(-1, 128), small_packed], axis=0)
    )
    pipes = [s_inputs, s_small] + pipes
    while pipes:
        advance((), pipes)
    grad_inputs_step = s_inputs.done()
    middle_sums = s_middle.done()
    attention_sums = middle_sums[:, : heads_width + model_width]
    zgate_mixed = middle_sums[:, heads_width + model_width :]
    ffn_sums = s_ffn.done()
    half_fold = fold_width // 2
    second = hidden_width + half_fold
    down_sums = [ffn_sums[:, hidden_width:second], ffn_sums[:, second + hidden_width :]]

    def stacked(v):
        return jnp.concatenate(
            [v[:, q : q + model_width] for q in range(0, v.shape[1], model_width)], axis=0
        )

    def own_part(total, share):
        length = share.shape[-1]
        return lax.dynamic_slice_in_dim(total, own_index() * length, length, total.ndim - 1)

    small_sums = s_small.done()
    table_sum = lax.dynamic_slice_in_dim(
        small_sums, own_index() * byte_table.shape[0], byte_table.shape[0], 0
    )
    small_sums = small_sums[table_rows:].reshape(-1)
    norm_mixer_sum = own_part(small_sums[: grad_norm_mixer.shape[0]], norm_mixer)
    sums = []
    start = grad_norm_mixer.shape[0]
    for count in small_lengths:
        sums.append(small_sums[start : start + count])
        start += count
    totals, bias_total, decay_total, skip_total = sums[:4]
    kernel_sum = sums[4].reshape(taps, -1)
    offset_sum, gated_sum, norm_attn_sum, norm_ffn_sum = sums[5:]
    rms_stats = jnp.sqrt(totals[:4] / (totals[4] * model_width))
    return (
        stream_three.reshape(row_count, length, model_width),
        grad_zero.reshape(row_count, length, model_width),
        rms_stats,
        table_sum,
        norm_mixer_sum,
        zgate_mixed[:, :zgate_width],
        grad_inputs_step[:, :wide],
        grad_inputs_step[:, wide : wide + HM],
        own_part(kernel_sum, conv_kernel),
        own_part(offset_sum, conv_bias),
        bias_total,
        decay_total,
        skip_total,
        own_part(gated_sum, mixer_norm),
        stacked(zgate_mixed[:, zgate_width:]),
        own_part(norm_attn_sum, norm_attn),
        attention_sums[:, :heads_width],
        attention_sums[:, heads_width:],
        own_part(norm_ffn_sum, norm_ffn),
        ffn_sums[:, :hidden_width],
        ffn_sums[:, second : second + hidden_width],
        stacked(jnp.concatenate(down_sums, axis=1)),
    )


def solution(mesh):
    return jax.shard_map(
        local,
        mesh=mesh,
        in_specs=(
            P(("dp", "fsdp"), None, None),
            P(("dp", "fsdp"), None),
            P(("dp", "fsdp"), None),
            P(("dp", "fsdp"), None, None),
            P(("dp", "fsdp"), None),
            P(("dp", "fsdp")),
            P(("dp", "fsdp"), None),
            P(("dp", "fsdp"), None),
            P(("dp", "fsdp"), None),
            P(None, ("dp", "fsdp")),
            P(("dp", "fsdp")),
            P(),
            P(),
            P(),
            P(("dp", "fsdp")),
            P(("dp", "fsdp"), None),
            P(("dp", "fsdp")),
            P(("dp", "fsdp"), None),
            P(("dp", "fsdp"), None),
            P(("dp", "fsdp")),
            P(("dp", "fsdp"), None),
            P(("dp", "fsdp"), None),
            P(("dp", "fsdp"), None),
        ),
        out_specs=(
            P(("dp", "fsdp"), None, None),
            P(("dp", "fsdp"), None, None),
            P(),
            P(("dp", "fsdp"), None),
            P(("dp", "fsdp")),
            P(("dp", "fsdp"), None),
            P(("dp", "fsdp"), None),
            P(("dp", "fsdp"), None),
            P(None, ("dp", "fsdp")),
            P(("dp", "fsdp")),
            P(),
            P(),
            P(),
            P(("dp", "fsdp")),
            P(("dp", "fsdp"), None),
            P(("dp", "fsdp")),
            P(("dp", "fsdp"), None),
            P(("dp", "fsdp"), None),
            P(("dp", "fsdp")),
            P(("dp", "fsdp"), None),
            P(("dp", "fsdp"), None),
            P(("dp", "fsdp"), None),
        ),
        check_vma=False,
    )
```

```python
from functools import partial

import jax
import jax.numpy as jnp
from jax import lax
from jax.experimental import pallas as pl
from jax.experimental.pallas import tpu as pltpu
from jax.sharding import PartitionSpec as P

DI = 2048
NS = 128
PM = 64
HD = 64
HM = 32


EPS = 1e-05


def matmul(former, latter):
    return jnp.dot(former, latter, preferred_element_type=jnp.float32)


def matmul_left(former, latter):
    return lax.dot_general(
        former, latter, (((0,), (0,)), ((), ())), preferred_element_type=jnp.float32
    )


def matmul_right(former, latter):
    return lax.dot_general(
        former, latter, (((1,), (1,)), ((), ())), preferred_element_type=jnp.float32
    )


def rms_norm(values, scaling):
    return values * lax.rsqrt(jnp.mean(values * values, axis=-1, keepdims=True) + EPS) * scaling


VMEM_LIMIT = 48 * 1024 * 1024
BRIEF = pl.CostEstimate(flops=1024, transcendentals=0, bytes_accessed=1024)


def column_sum(v):
    return jnp.sum(v, axis=0, keepdims=True)


def sigmoid(v):
    return 1.0 / (1.0 + jnp.exp(-v))


def down_rows(v, count):
    return pltpu.roll(v, count, 0)


def up_rows(v, count):
    return pltpu.roll(v, v.shape[0] - count, 0)


def turned(v):
    length = v.shape[0]
    row = lax.broadcasted_iota(jnp.int32, (length, length), 0)
    column = lax.broadcasted_iota(jnp.int32, (length, length), 1)
    unit = (row == column).astype(jnp.float32)
    return lax.dot_general(
        v,
        unit,
        (((0,), (0,)), ((), ())),
        precision=lax.Precision.HIGHEST,
        preferred_element_type=jnp.float32,
    )


def turned_back(v):
    length = v.shape[1]
    row = lax.broadcasted_iota(jnp.int32, (length, length), 0)
    column = lax.broadcasted_iota(jnp.int32, (length, length), 1)
    unit = (row == column).astype(jnp.float32)
    return lax.dot_general(
        unit,
        v,
        (((1,), (1,)), ((), ())),
        precision=lax.Precision.HIGHEST,
        preferred_element_type=jnp.float32,
    )


def allowed_mask(ids_column, ids_row):
    length = ids_column.shape[0]
    row = lax.broadcasted_iota(jnp.int32, (length, length), 0)
    column = lax.broadcasted_iota(jnp.int32, (length, length), 1)
    return (ids_column == ids_row) & (row >= column)


def link_columns(ids_column, taps):
    length = ids_column.shape[0]
    place = lax.broadcasted_iota(jnp.int32, (length, 128), 0)
    wide = jnp.broadcast_to(ids_column, (length, 128))
    return [
        ((down_rows(wide, j) == wide) & (place >= j)).astype(jnp.float32)[:, :1]
        for j in range(1, taps)
    ]


def conv_chunk(raw, taps_chunk, offset, links):
    taps = taps_chunk.shape[0]
    shifted = [raw] + [down_rows(raw, j) * links[j - 1] for j in range(1, taps)]
    total = offset
    for j in range(taps):
        total = total + shifted[j] * taps_chunk[taps - 1 - j : taps - j]
    return total, shifted


def step_terms(step_raw, step_bias, decay_log):
    shifted = step_raw + step_bias
    step = jnp.maximum(shifted, 0.0) + jnp.log1p(jnp.exp(-jnp.abs(shifted)))
    rate = -jnp.exp(decay_log) * step
    length = step.shape[0]
    place = lax.broadcasted_iota(jnp.int32, step.shape, 0)
    total = rate
    shift = 1
    while shift < length:
        total = total + jnp.where(place >= shift, down_rows(total, shift), 0.0)
        shift *= 2
    return shifted, step, rate, total


def mixer_forward_kernel(
    raw_ref, zgate_ref, ids_column_ref, ids_row_ref, taps_ref, offset_ref,
    bias_ref, decay_ref, skip_ref, gain_ref,
    values_ref, states_ref, combined_ref, gate_ref,
):
    taps = taps_ref.shape[0]
    ids_column = ids_column_ref[0]
    links = link_columns(ids_column, taps)
    channels = taps_ref.shape[1]
    for start in range(0, channels, 256):
        part = slice(start, start + 256)
        total, _ = conv_chunk(raw_ref[0, :, part], taps_ref[:, part], offset_ref[:, part], links)
        low = (total * sigmoid(total)).astype(jnp.bfloat16)
        if start < DI:
            values_ref[0, :, part] = low
        else:
            states_ref[0] = low
    state_in, state_out = states_ref[0, :, :NS], states_ref[0, :, NS:]
    gram = matmul_right(state_out, state_in)
    _, step, _, total = step_terms(
        raw_ref[0, :, channels : channels + 128], bias_ref[...], decay_ref[...]
    )
    total_rows, step_rows = turned(total), turned(step)
    mask = allowed_mask(ids_column, ids_row_ref[0])
    gram = jnp.where(mask, gram, 0.0)
    length = gram.shape[0]
    first = lax.broadcasted_iota(jnp.int32, (length, 2 * PM), 1) < PM
    squares = jnp.zeros((length, 1), jnp.float32)
    for pair in range(HM // 2):
        lanes = slice(pair * 2 * PM, (pair + 1) * 2 * PM)
        values = values_ref[0, :, lanes]
        outs = []
        for head in (2 * pair, 2 * pair + 1):
            between = total[:, head : head + 1] - total_rows[head : head + 1, :]
            decayed = jnp.exp(jnp.where(mask, between, 0.0))
            mix = gram * decayed * step_rows[head : head + 1, :]
            outs.append(matmul(mix.astype(jnp.bfloat16), values))
        combined = jnp.where(first, outs[0], outs[1]) + skip_ref[:, lanes] * values.astype(
            jnp.float32
        )
        combined_ref[0, :, lanes] = combined
        zgate = zgate_ref[0, :, lanes]
        gated = combined * (zgate * sigmoid(zgate))
        squares = squares + jnp.sum(gated * gated, axis=1, keepdims=True)
    scale = lax.rsqrt(squares / DI + EPS)
    for start in range(0, DI, 256):
        part = slice(start, start + 256)
        zgate = zgate_ref[0, :, part]
        gated = combined_ref[0, :, part] * (zgate * sigmoid(zgate))
        gate_ref[0, :, part] = (gated * scale * gain_ref[:, part]).astype(jnp.bfloat16)


def gate_backward_kernel(
    upper_ref, weight_ref, zgate_ref, gain_ref, values_ref, combined_ref,
    zgrad_ref, heads_ref, gain_grad_ref, skip_grad_ref, grad_ref,
):
    grad_ref[0] = matmul_right(upper_ref[0], weight_ref[...])

    @pl.when(pl.program_id(0) == 0)
    def _():
        for ref in (gain_grad_ref, skip_grad_ref):
            ref[...] = jnp.zeros(ref.shape, ref.dtype)

    length = grad_ref.shape[1]
    squares = jnp.zeros((length, 1), jnp.float32)
    product = jnp.zeros((length, 1), jnp.float32)
    for start in range(0, DI, 256):
        part = slice(start, start + 256)
        zgate = zgate_ref[0, :, part]
        gated = combined_ref[0, :, part] * (zgate * sigmoid(zgate))
        squares = squares + jnp.sum(gated * gated, axis=1, keepdims=True)
        product = product + jnp.sum(
            gated * grad_ref[0, :, part] * gain_ref[:, part], axis=1, keepdims=True
        )
    scale = lax.rsqrt(squares / DI + EPS)
    inner = scale * scale * scale * (product / DI)
    for start in range(0, DI, 256):
        part = slice(start, start + 256)
        zgate = zgate_ref[0, :, part]
        combined = combined_ref[0, :, part]
        sig = sigmoid(zgate)
        silu = zgate * sig
        gated = combined * silu
        grad = grad_ref[0, :, part]
        gain_grad_ref[:, part] += column_sum(grad * gated * scale)
        grad_gated = scale * grad * gain_ref[:, part] - gated * inner
        grad_combined = grad_gated * silu
        zgrad_ref[0, :, part] = (grad_gated * combined * (sig + silu * (1.0 - sig))).astype(
            jnp.bfloat16
        )
        skip_grad_ref[:, part] += column_sum(
            grad_combined * values_ref[0, :, part].astype(jnp.float32)
        )
        heads_ref[0, :, part] = grad_combined.astype(jnp.bfloat16)


def mixer_backward_kernel(
    heads_ref, raw_ref, ids_column_ref, ids_row_ref, taps_ref, offset_ref,
    bias_ref, decay_ref, skip_ref, values_ref, states_ref,
    xgrad_ref, taps_grad_ref, offset_grad_ref, bias_grad_ref, decay_grad_ref, through_ref,
):
    taps = taps_ref.shape[0]
    channels = taps_ref.shape[1]
    length = raw_ref.shape[1]

    @pl.when(pl.program_id(0) == 0)
    def _():
        for ref in (taps_grad_ref, offset_grad_ref, bias_grad_ref, decay_grad_ref):
            ref[...] = jnp.zeros(ref.shape, ref.dtype)

    ids_column = ids_column_ref[0]
    links = link_columns(ids_column, taps)
    state_in, state_out = states_ref[0, :, :NS], states_ref[0, :, NS:]
    shifted_step, step, rate, total = step_terms(
        raw_ref[0, :, channels : channels + 128], bias_ref[...], decay_ref[...]
    )
    total_rows, step_rows = turned(total), turned(step)
    mask = allowed_mask(ids_column, ids_row_ref[0])
    gram = jnp.where(mask, matmul_right(state_out, state_in), 0.0)
    first = lax.broadcasted_iota(jnp.int32, (length, 2 * PM), 1) < PM
    lane = lax.broadcasted_iota(jnp.int32, (length, 128), 1)
    row = lax.broadcasted_iota(jnp.int32, (128, length), 0)
    grad_gram = jnp.zeros((length, length), jnp.float32)
    by_row = jnp.zeros((length, 128), jnp.float32)
    by_column = jnp.zeros((128, length), jnp.float32)
    nothing = jnp.zeros((length, 2 * PM), jnp.bfloat16)
    for pair in range(HM // 2):
        lanes = slice(pair * 2 * PM, (pair + 1) * 2 * PM)
        values = values_ref[0, :, lanes]
        heads = heads_ref[0, :, lanes]
        outs = []
        for head, own in ((2 * pair, first), (2 * pair + 1, ~first)):
            between = total[:, head : head + 1] - total_rows[head : head + 1, :]
            decayed = jnp.where(mask, jnp.exp(jnp.where(mask, between, 0.0)), 0.0)
            step_row = step_rows[head : head + 1, :]
            mixed = gram * decayed
            grad_mix = matmul_right(jnp.where(own, heads, nothing), values)
            outs.append(matmul_left((mixed * step_row).astype(jnp.bfloat16), heads))
            grad_gram = grad_gram + grad_mix * decayed * step_row
            direct = grad_mix * mixed
            by_column = by_column + jnp.where(row == head, column_sum(direct), 0.0)
            by_row = by_row + jnp.where(
                lane == head, jnp.sum(direct * step_row, axis=1, keepdims=True), 0.0
            )
        through_ref[:, lanes] = jnp.where(first, outs[0], outs[1]) + skip_ref[
            :, lanes
        ] * heads.astype(jnp.float32)
    grad_step = turned_back(by_column)
    grad_total = by_row - grad_step * step
    place = lax.broadcasted_iota(jnp.int32, grad_total.shape, 0)
    shift = 1
    while shift < length:
        grad_total = grad_total + jnp.where(
            place < length - shift, up_rows(grad_total, shift), 0.0
        )
        shift *= 2
    decay_grad_ref[...] += column_sum(grad_total * rate)
    grad_step = grad_step - grad_total * jnp.exp(decay_ref[...])
    grad_raw = jnp.where(lane < HM, grad_step * sigmoid(shifted_step), 0.0)
    bias_grad_ref[...] += column_sum(grad_raw)
    xgrad_ref[0, :, channels : channels + 128] = grad_raw.astype(jnp.bfloat16)
    extra = xgrad_ref.shape[2] - channels - 128
    if extra:
        xgrad_ref[0, :, channels + 128 :] = jnp.zeros((length, extra), jnp.bfloat16)
    gram_low = grad_gram.astype(jnp.bfloat16)
    grad_in = matmul_left(gram_low, state_out)
    grad_out = matmul(gram_low, state_in)
    for start in range(0, channels, 128):
        part = slice(start, start + 128)
        chunk_taps = taps_ref[:, part]
        total, shifted = conv_chunk(raw_ref[0, :, part], chunk_taps, offset_ref[:, part], links)
        sig = sigmoid(total)
        if start < DI:
            grad = through_ref[:, part]
        else:
            grad = grad_in if start == DI else grad_out
        grad = grad * (sig + total * sig * (1.0 - sig))
        offset_grad_ref[:, part] += column_sum(grad)
        back = grad * chunk_taps[taps - 1 : taps]
        sums = [column_sum(grad * shifted[0])]
        for j in range(1, taps):
            sums.append(column_sum(grad * shifted[j]))
            linked = grad * links[j - 1]
            back = back + up_rows(linked, j) * chunk_taps[taps - 1 - j : taps - j]
        taps_grad_ref[:, part] += jnp.concatenate(sums[::-1], axis=0)
        xgrad_ref[0, :, part] = back.astype(jnp.bfloat16)


def whole(rows, columns):
    return pl.BlockSpec((rows, columns), lambda n: (0, 0))


def mixer_forward(raw, zgate, ids, taps, offset, bias, decay, skip, gain):
    count, length, columns = raw.shape
    row = lambda c: pl.BlockSpec((1, length, c), lambda n: (n, 0, 0))
    channels = taps.shape[1]
    return pl.pallas_call(
        mixer_forward_kernel,
        grid=(count,),
        in_specs=[
            row(columns), row(DI), row(1), pl.BlockSpec((1, 1, length), lambda n: (n, 0, 0)),
            whole(*taps.shape), whole(1, channels), whole(1, 128), whole(1, 128),
            whole(1, DI), whole(1, DI),
        ],
        out_specs=[row(DI), row(2 * NS), row(DI), row(DI)],
        out_shape=[
            jax.ShapeDtypeStruct((count, length, DI), jnp.bfloat16),
            jax.ShapeDtypeStruct((count, length, 2 * NS), jnp.bfloat16),
            jax.ShapeDtypeStruct((count, length, DI), jnp.float32),
            jax.ShapeDtypeStruct((count, length, DI), jnp.bfloat16),
        ],
        compiler_params=pltpu.CompilerParams(vmem_limit_bytes=VMEM_LIMIT),
        cost_estimate=BRIEF,
    )(raw, zgate, ids[:, :, None], ids[:, None, :], taps, offset, bias, decay, skip, gain)


def gate_backward(upper, weight, zgate, gain, values, combined):
    count, length, width = upper.shape
    row = lambda c: pl.BlockSpec((1, length, c), lambda n: (n, 0, 0))
    one = lambda r, c: jax.ShapeDtypeStruct((r, c), jnp.float32)
    return pl.pallas_call(
        gate_backward_kernel,
        grid=(count,),
        in_specs=[
            row(width), whole(DI, width), row(DI), whole(1, DI), row(DI), row(DI)
        ],
        out_specs=[row(DI), row(DI), whole(1, DI), whole(1, DI)],
        out_shape=[
            jax.ShapeDtypeStruct((count, length, DI), jnp.bfloat16),
            jax.ShapeDtypeStruct((count, length, DI), jnp.bfloat16),
            one(1, DI), one(1, DI),
        ],
        scratch_shapes=[pltpu.VMEM((1, length, DI), jnp.float32)],
        compiler_params=pltpu.CompilerParams(vmem_limit_bytes=VMEM_LIMIT),
        cost_estimate=BRIEF,
    )(upper, weight, zgate, gain, values, combined)


def mixer_backward(heads, raw, ids, taps, offset, bias, decay, skip, values, states):
    count, length, columns = raw.shape
    row = lambda c: pl.BlockSpec((1, length, c), lambda n: (n, 0, 0))
    channels = taps.shape[1]
    extra = -columns % 256
    one = lambda r, c: jax.ShapeDtypeStruct((r, c), jnp.float32)
    return pl.pallas_call(
        mixer_backward_kernel,
        grid=(count,),
        in_specs=[
            row(DI), row(columns), row(1),
            pl.BlockSpec((1, 1, length), lambda n: (n, 0, 0)),
            whole(*taps.shape), whole(1, channels), whole(1, 128), whole(1, 128),
            whole(1, DI), row(DI), row(2 * NS),
        ],
        out_specs=[
            row(columns + extra), whole(*taps.shape), whole(1, channels), whole(1, 128),
            whole(1, 128),
        ],
        out_shape=[
            jax.ShapeDtypeStruct((count, length, columns + extra), jnp.bfloat16),
            one(*taps.shape), one(1, channels), one(1, 128), one(1, 128),
        ],
        scratch_shapes=[pltpu.VMEM((length, DI), jnp.float32)],
        compiler_params=pltpu.CompilerParams(vmem_limit_bytes=VMEM_LIMIT),
        cost_estimate=BRIEF,
    )(heads, raw, ids[:, :, None], ids[:, None, :], taps, offset, bias, decay, skip, values, states)


def head_scores(query, key, own, mask, nothing):
    scores = matmul_right(jnp.where(own, query, nothing), key) * HD ** (-0.5)
    masked = jnp.where(mask, scores, -1e30)
    highest = jnp.max(masked, axis=1, keepdims=True)
    exponents = jnp.exp(masked - highest)
    return exponents / jnp.sum(exponents, axis=1, keepdims=True)


def attention_forward_kernel(joined_ref, ids_column_ref, ids_row_ref, out_ref):
    mask = allowed_mask(ids_column_ref[0], ids_row_ref[0])
    length, width = out_ref.shape[1:]
    first = lax.broadcasted_iota(jnp.int32, (length, 2 * HD), 1) < HD
    nothing = jnp.zeros((length, 2 * HD), jnp.bfloat16)
    for start in range(0, width, 2 * HD):
        query, key, value = (
            joined_ref[0, :, k * width + start : k * width + start + 2 * HD] for k in range(3)
        )
        outs = []
        for own in (first, ~first):
            chances = head_scores(query, key, own, mask, nothing)
            outs.append(matmul(chances.astype(jnp.bfloat16), value))
        out_ref[0, :, start : start + 2 * HD] = jnp.where(first, outs[0], outs[1]).astype(
            jnp.bfloat16
        )


def attention_backward_kernel(
    joined_ref, upper_ref, weight_ref, ids_column_ref, ids_row_ref, out_ref, grad_ref
):
    grad_ref[0] = matmul_right(upper_ref[0], weight_ref[...]).astype(jnp.bfloat16)
    mask = allowed_mask(ids_column_ref[0], ids_row_ref[0])
    length, width = grad_ref.shape[1:]
    first = lax.broadcasted_iota(jnp.int32, (length, 2 * HD), 1) < HD
    nothing = jnp.zeros((length, 2 * HD), jnp.bfloat16)
    scale = HD ** (-0.5)
    for start in range(0, width, 2 * HD):
        query, key, value = (
            joined_ref[0, :, k * width + start : k * width + start + 2 * HD] for k in range(3)
        )
        grad = grad_ref[0, :, start : start + 2 * HD]
        outs = [[], [], []]
        for own in (first, ~first):
            chances = head_scores(query, key, own, mask, nothing)
            grad_chances = matmul_right(jnp.where(own, grad, nothing), value)
            inner = jnp.sum(chances * grad_chances, axis=1, keepdims=True)
            grad_scores = (chances * (grad_chances - inner)).astype(jnp.bfloat16)
            outs[0].append(matmul(grad_scores, key) * scale)
            outs[1].append(matmul_left(grad_scores, query) * scale)
            outs[2].append(matmul_left(chances.astype(jnp.bfloat16), grad))
        for k in range(3):
            out_ref[0, :, k * width + start : k * width + start + 2 * HD] = jnp.where(
                first, outs[k][0], outs[k][1]
            ).astype(jnp.bfloat16)


def attention_forward(joined, ids):
    count, length, columns = joined.shape
    row = lambda c: pl.BlockSpec((1, length, c), lambda n: (n, 0, 0))
    return pl.pallas_call(
        attention_forward_kernel,
        grid=(count,),
        in_specs=[row(columns), row(1), pl.BlockSpec((1, 1, length), lambda n: (n, 0, 0))],
        out_specs=row(columns // 3),
        out_shape=jax.ShapeDtypeStruct((count, length, columns // 3), jnp.bfloat16),
        compiler_params=pltpu.CompilerParams(vmem_limit_bytes=VMEM_LIMIT),
        cost_estimate=BRIEF,
    )(joined, ids[:, :, None], ids[:, None, :])


def attention_backward(joined, upper, full, block, ids):
    count, length, columns = joined.shape
    width = columns // 3
    row = lambda c: pl.BlockSpec((1, length, c), lambda n: (n, 0, 0))
    return pl.pallas_call(
        attention_backward_kernel,
        grid=(count,),
        in_specs=[
            row(columns), row(width), pl.BlockSpec((width, width), lambda n: (0, block)), row(1),
            pl.BlockSpec((1, 1, length), lambda n: (n, 0, 0)),
        ],
        out_specs=row(columns),
        out_shape=jax.ShapeDtypeStruct((count, length, columns), jnp.bfloat16),
        scratch_shapes=[pltpu.VMEM((1, length, width), jnp.bfloat16)],
        compiler_params=pltpu.CompilerParams(vmem_limit_bytes=VMEM_LIMIT),
        cost_estimate=BRIEF,
    )(joined, upper, full, ids[:, :, None], ids[:, None, :])


def norm_backward_kernel(count, *refs):
    acts, weights = refs[:count], refs[count : 2 * count]
    stream_ref, gain_ref, base_ref, total_ref, low_ref, gain_grad_ref, sum_ref = refs[2 * count :]
    step = pl.program_id(0)
    rows = weights[0].shape[0]
    part = 0.0
    for act, weight in zip(acts, weights):
        part = part + matmul_right(act[:, : weight.shape[1]], weight[...])
    sum_ref[:, pl.ds(pl.multiple_of(step * rows, rows), rows)] = part

    @pl.when(step == pl.num_programs(0) - 1)
    def _():
        values, grad, gain = stream_ref[...], sum_ref[...], gain_ref[...]
        scale = lax.rsqrt(jnp.mean(values * values, axis=1, keepdims=True) + EPS)
        gain_grad_ref[...] = column_sum(grad * values * scale)
        scaled = grad * gain
        inner = jnp.mean(scaled * values, axis=1, keepdims=True)
        total = base_ref[...] + scale * scaled - values * (scale * scale * scale * inner)
        total_ref[...] = total
        low_ref[...] = total.astype(jnp.bfloat16)


def norm_backward(pairs, stream, gain, base):
    tokens, width = stream.shape
    rows = width // 4
    fixed = lambda r, c, k=0: pl.BlockSpec((r, c), lambda i: (0, k))
    return pl.pallas_call(
        partial(norm_backward_kernel, len(pairs)),
        grid=(4,),
        in_specs=[fixed(tokens, a.shape[1] if w is None else w, k) for a, k, _, _, w in pairs]
        + [
            pl.BlockSpec((rows, m.shape[1] if w is None else w), lambda i, k=k: (i, k))
            for _, _, m, k, w in pairs
        ]
        + [fixed(tokens, width), fixed(1, width), fixed(tokens, width)],
        out_specs=[fixed(tokens, width), fixed(tokens, width), fixed(1, width)],
        out_shape=[
            jax.ShapeDtypeStruct((tokens, width), jnp.float32),
            jax.ShapeDtypeStruct((tokens, width), jnp.bfloat16),
            jax.ShapeDtypeStruct((1, width), jnp.float32),
        ],
        scratch_shapes=[pltpu.VMEM((tokens, width), jnp.float32)],
        compiler_params=pltpu.CompilerParams(vmem_limit_bytes=VMEM_LIMIT),
        cost_estimate=BRIEF,
    )(*[p[0] for p in pairs], *[p[2] for p in pairs], stream, gain, base)


def ffn_kernel(
    rows, fold, source_ref, grad_ref, gate_ref, upper_ref, folded_ref,
    hidden_ref, gate_grad_ref, upper_grad_ref, out_ref, back_ref, down_ref,
):
    @pl.when(pl.program_id(0) == 0)
    def _():
        out_ref[...] = jnp.zeros(out_ref.shape, jnp.float32)
        back_ref[...] = jnp.zeros(back_ref.shape, jnp.float32)

    width = out_ref.shape[1]
    for d in range(folded_ref.shape[0] // rows):
        for q in range(fold):
            place = (d * fold + q) * rows
            down_ref[place : place + rows, :] = folded_ref[
                d * rows : (d + 1) * rows, q * width : (q + 1) * width
            ]
    source, grad = source_ref[...], grad_ref[...]
    gate_pre = matmul(source, gate_ref[...])
    up_pre = matmul(source, upper_ref[...])
    sig = sigmoid(gate_pre)
    silu = gate_pre * sig
    hidden = (silu * up_pre).astype(jnp.bfloat16)
    hidden_ref[...] = hidden
    out_ref[...] += matmul(hidden, down_ref[...])
    grad_hidden = matmul_right(grad, down_ref[...])
    gate_grad = (grad_hidden * up_pre * (sig + silu * (1.0 - sig))).astype(jnp.bfloat16)
    upper_grad = (grad_hidden * silu).astype(jnp.bfloat16)
    gate_grad_ref[...] = gate_grad
    upper_grad_ref[...] = upper_grad
    back_ref[...] += matmul_right(gate_grad, gate_ref[...]) + matmul_right(
        upper_grad, upper_ref[...]
    )


def feed_forward(source, grad, full, rows, hidden_width, fold):
    tokens, width = source.shape
    tile = 512
    steps = hidden_width // tile
    all_rows = lambda c: pl.BlockSpec((tokens, c), lambda j: (0, j))
    fixed = pl.BlockSpec((tokens, width), lambda j: (0, 0))
    down_block = 2 * hidden_width // (fold * width)
    return pl.pallas_call(
        partial(ffn_kernel, rows, fold),
        grid=(steps,),
        in_specs=[
            fixed,
            fixed,
            pl.BlockSpec((width, tile), lambda j: (0, j)),
            pl.BlockSpec((width, tile), lambda j: (0, steps + j)),
            pl.BlockSpec((tile // fold, fold * width), lambda j: (j, down_block)),
        ],
        out_specs=[all_rows(tile)] * 3 + [fixed] * 2,
        out_shape=[jax.ShapeDtypeStruct((tokens, hidden_width), jnp.bfloat16)] * 3
        + [jax.ShapeDtypeStruct((tokens, width), jnp.float32)] * 2,
        scratch_shapes=[pltpu.VMEM((tile, width), jnp.bfloat16)],
        compiler_params=pltpu.CompilerParams(vmem_limit_bytes=VMEM_LIMIT),
        cost_estimate=BRIEF,
    )(source, grad, full, full, full)


AXES = ("dp", "fsdp")


def axis_bits():
    bits = []
    for name in AXES:
        size = lax.axis_size(name)
        step = size // 2
        while step:
            bits.append((name, size, step))
            step //= 2
    return bits


def phases(flip, turn=False):
    bits = axis_bits()
    outer = [k for k, b in enumerate(bits) if b[0] == "dp" and b[2] > 1]
    core = [k for k, b in enumerate(bits) if b[0] == "dp" and b[2] == 1]
    inner = [k for k, b in enumerate(bits) if b[0] == "fsdp"]
    return bits, (outer[::-1] if turn else outer) + (inner if flip else inner[::-1]) + core


def swap(v, bit):
    name, size, step = bit
    return lax.ppermute(v, name, [(i, i ^ step) for i in range(size)])


def own_bit(bit):
    return (lax.axis_index(bit[0]) // bit[2]) % 2


def own_index():
    return lax.axis_index("dp") * lax.axis_size("fsdp") + lax.axis_index("fsdp")


def bit_weight(bit):
    return bit[2] * (lax.axis_size("fsdp") if bit[0] == "dp" else 1)


def assemble_kernel(offsets, me_ref, *refs):
    pieces, out_ref, sems = refs[:-2], refs[-2], refs[-1]
    me = me_ref[0]
    copies = []
    count = 0
    for piece, places in zip(pieces, offsets):
        for j, place in enumerate(places):
            copies.append(
                pltpu.make_async_copy(piece.at[j], out_ref.at[me ^ place], sems.at[count])
            )
            count += 1
    for c in copies:
        c.start()
    for c in copies:
        c.wait()


def tie(*values):
    return lax.optimization_barrier(values)


class Gather:
    def __init__(self, shard, flip):
        self.rows, self.columns = shard.shape
        self.bits, self.order = phases(flip)
        self.pieces = [(shard[None], [0])]
        self.phase = 0

    def step(self):
        k = self.order[self.phase]
        weight = bit_weight(self.bits[k])
        if len(self.pieces) > 1 and self.phase < len(self.order) - 1:
            joined = jnp.concatenate([p for p, _ in self.pieces], axis=0)
            self.pieces = [(joined, sum((o for _, o in self.pieces), []))]
        self.pieces = self.pieces + [
            (swap(p, self.bits[k]), [o ^ weight for o in offs]) for p, offs in self.pieces
        ]
        self.phase += 1

    def done(self):
        while self.phase < len(self.order):
            self.step()
        count = 2 ** len(self.bits)
        me = own_index().astype(jnp.int32).reshape(1)
        out = pl.pallas_call(
            partial(assemble_kernel, [o for _, o in self.pieces]),
            out_shape=jax.ShapeDtypeStruct((count, self.rows, self.columns), jnp.bfloat16),
            in_specs=[pl.BlockSpec(memory_space=pltpu.SMEM)]
            + [pl.BlockSpec(memory_space=pl.ANY)] * len(self.pieces),
            out_specs=pl.BlockSpec(memory_space=pltpu.VMEM),
            scratch_shapes=[pltpu.SemaphoreType.DMA((count,))],
            compiler_params=pltpu.CompilerParams(vmem_limit_bytes=24 * 1024 * 1024),
            cost_estimate=BRIEF,
        )(me, *[p for p, _ in self.pieces])
        return out.reshape(count * self.rows, self.columns)


def unfold_kernel(start, fold, full_ref, out_ref, sems):
    columns = out_ref.shape[3]
    copies = [
        pltpu.make_async_copy(
            full_ref.at[:, :, pl.ds(start + q * columns, columns)], out_ref.at[:, q], sems.at[q]
        )
        for q in range(fold)
    ]
    for c in copies:
        c.start()
    for c in copies:
        c.wait()


def unfold(full, rows, start, fold, columns):
    count = full.shape[0] // rows
    out = pl.pallas_call(
        partial(unfold_kernel, start, fold),
        out_shape=jax.ShapeDtypeStruct((count, fold, rows, columns), full.dtype),
        in_specs=[pl.BlockSpec(memory_space=pl.ANY)],
        out_specs=pl.BlockSpec(memory_space=pltpu.VMEM),
        scratch_shapes=[pltpu.SemaphoreType.DMA((fold,))],
        compiler_params=pltpu.CompilerParams(vmem_limit_bytes=24 * 1024 * 1024),
        cost_estimate=BRIEF,
    )(full.reshape(count, rows, full.shape[1]))
    return out.reshape(count * fold * rows, columns)


def gather_round(gathers, values=(), fresh=()):
    sizes = [len(g.pieces) for g in gathers]
    tied = tie(
        *values, *[g.pieces[0][0] for g in fresh], *[p for g in gathers for p, _ in g.pieces]
    )
    head = len(values)
    for g in fresh:
        g.pieces[0] = (tied[head], g.pieces[0][1])
        head += 1
    for g, size in zip(gathers, sizes):
        g.pieces = [(tied[head + k], g.pieces[k][1]) for k in range(size)]
        head += size
    for g in [*gathers, *fresh]:
        if g.phase < len(g.order):
            g.step()
    return tied[: len(values)]


def gather_small(shard):
    bits = axis_bits()
    out = shard[None]
    for bit in bits[::-1]:
        other = swap(out, bit)
        mine = own_bit(bit) == 0
        out = jnp.concatenate([jnp.where(mine, out, other), jnp.where(mine, other, out)], axis=0)
    return out


def scatter_sum(part, flip, core_done, wide=False):
    bits, order = phases(flip)
    names = [k for k in range(len(bits)) if not (core_done and bits[k][0] == "dp" and bits[k][2] == 1)]
    count = 2 ** len(names)
    part = part.reshape([2] * len(names) + [part.shape[0] // count, part.shape[1]])
    for n, k in enumerate([k for k in order[::-1] if k in names]):
        axis = names.index(k)
        names.remove(k)
        mine = own_bit(bits[k])
        send = lax.dynamic_index_in_dim(part, 1 - mine, axis, keepdims=False)
        keep = lax.dynamic_index_in_dim(part, mine, axis, keepdims=False)
        total = keep.astype(jnp.float32) + swap(send, bits[k]).astype(jnp.float32)
        part = total if not names else total.astype(part.dtype)
    return part.astype(jnp.float32)


def core_columns(former, core):
    outer = lax.axis_size("dp") // 2
    group = former.shape[1] // (2 * outer)
    return jnp.concatenate(
        [lax.dynamic_slice_in_dim(former, (2 * i + core) * group, group, 1) for i in range(outer)],
        axis=1,
    )


def grads_kernel(plan, rows, counts, core_ref, *refs):
    formers, latters = refs[: counts[0]], refs[counts[0] : counts[0] + counts[1]]
    products = {}
    for out_ref, items in zip(refs[counts[0] + counts[1] :], plan):
        start = 0
        for former, latter, fold, low, high in items:
            if fold == 1:
                for at in range(low, high, 512):
                    to = min(at + 512, high)
                    out_ref[:, start + at - low : start + to - low] = matmul_left(
                        formers[former][...], latters[latter][:, at:to]
                    ).astype(jnp.bfloat16)
            else:
                if (former, latter) not in products:
                    products[former, latter] = matmul_left(
                        formers[former][...], latters[latter][...]
                    ).astype(jnp.bfloat16)
                product = products[former, latter]
                width = product.shape[1]
                for d in range(product.shape[0] // (fold * rows)):
                    for q in range(low // width, high // width):
                        to = start + q * width - low
                        place = (d * fold + q) * rows
                        out_ref[d * rows : (d + 1) * rows, to : to + width] = product[
                            place : place + rows, :
                        ]
            start += high - low


def part_grads(formers, latters, plan, rows, core):
    tokens = formers[0].shape[0]
    outer = lax.axis_size("dp") // 2
    groups = [f.shape[1] // (2 * outer) for f in formers]
    height = rows * lax.axis_size("fsdp")
    widths = [sum(item[4] - item[3] for item in items) for items in plan]
    shapes = [jax.ShapeDtypeStruct((outer * height, w), jnp.bfloat16) for w in widths]
    if any(g % 128 for g in groups):
        outs = []
        for items in plan:
            parts = []
            for former, latter, fold, low, high in items:
                product = matmul_left(core_columns(formers[former], core), latters[latter])
                width = product.shape[1]
                product = jnp.swapaxes(product.reshape(-1, fold, rows, width), 1, 2)
                parts.append(product.reshape(-1, fold * width)[:, low:high])
            outs.append(jnp.concatenate(parts, axis=1).astype(jnp.bfloat16))
        return outs
    return pl.pallas_call(
        partial(grads_kernel, plan, rows, (len(formers), len(latters))),
        grid_spec=pltpu.PrefetchScalarGridSpec(
            num_scalar_prefetch=1,
            grid=(outer,),
            in_specs=[pl.BlockSpec((tokens, g), lambda i, c: (0, 2 * i + c[0])) for g in groups]
            + [pl.BlockSpec(v.shape, lambda i, c: (0, 0)) for v in latters],
            out_specs=[pl.BlockSpec((height, w), lambda i, c: (i, 0)) for w in widths],
        ),
        out_shape=shapes,
        compiler_params=pltpu.CompilerParams(vmem_limit_bytes=VMEM_LIMIT),
        cost_estimate=BRIEF,
    )(core.astype(jnp.int32).reshape(1), *formers, *latters)


def add_halves_kernel(count, mine_ref, *refs):
    for k in range(count):
        give, give_more, hold, hold_more = refs[4 * k : 4 * k + 4]
        send_ref, keep_ref = refs[4 * count + 2 * k : 4 * count + 2 * k + 2]
        for former, latter, out in ((give, give_more, send_ref), (hold, hold_more, keep_ref)):
            out[...] = (
                former[...].astype(jnp.float32) + latter[...].astype(jnp.float32)
            ).astype(jnp.bfloat16)


def add_halves(jobs):
    groups = {}
    for number, (keep, _, _, _, parts) in enumerate(jobs):
        before, columns = keep.shape[0], keep.shape[3] // parts
        tiles = 1
        while before * tiles < 4 and columns % (256 * tiles) == 0:
            tiles *= 2
        several = max(1, before // 4)
        groups.setdefault(before // several * tiles, []).append((number, tiles, several))
    results = [None] * len(jobs)
    for steps, members in groups.items():
        in_specs, out_specs, shapes, operands, bits = [], [], [], [], []
        for at, (number, tiles, several) in enumerate(members):
            keep, received, mine, part, parts = jobs[number]
            before, _, rows, columns = keep.shape
            width = columns // parts // tiles

            def spec(own, at=at, tiles=tiles, first=part * tiles, several=several, rows=rows, width=width):
                return pl.BlockSpec(
                    (several, None, rows, width),
                    lambda i, m: (
                        i // tiles, m[at] if own else 1 - m[at], 0, first + i % tiles
                    ),
                )

            in_specs += [spec(False), spec(False), spec(True), spec(True)]
            out_specs += [
                pl.BlockSpec(
                    (several, rows, width), lambda i, m, tiles=tiles: (i // tiles, 0, i % tiles)
                )
            ] * 2
            shapes += [jax.ShapeDtypeStruct((before, rows, columns // parts), jnp.bfloat16)] * 2
            operands += [keep, received, keep, received]
            bits.append(mine)
        outs = pl.pallas_call(
            partial(add_halves_kernel, len(members)),
            grid_spec=pltpu.PrefetchScalarGridSpec(
                num_scalar_prefetch=1, grid=(steps,), in_specs=in_specs, out_specs=out_specs
            ),
            out_shape=shapes,
            compiler_params=pltpu.CompilerParams(vmem_limit_bytes=VMEM_LIMIT),
            cost_estimate=BRIEF,
        )(jnp.stack(bits).astype(jnp.int32), *operands)
        for at, (number, _, _) in enumerate(members):
            results[number] = outs[2 * at : 2 * at + 2]
    return results


class Scatter:
    def __init__(self, keep, received, part):
        self.bits, order = phases(part == 1, part == 1)
        core = [k for k, b in enumerate(self.bits) if b[0] == "dp" and b[2] == 1][0]
        self.names = [k for k in range(len(self.bits)) if k != core]
        self.order = [k for k in order[::-1] if k != core]
        self.keep, self.received = keep, received
        self.part, self.parts = part, 2

    def job(self):
        self.send = None
        keep, received = self.keep, self.received
        if not self.names:
            total = keep.astype(jnp.float32) + received.astype(jnp.float32)
            self.keep, self.received = total.reshape(-1, total.shape[-1]), None
            return None
        k = self.order.pop(0)
        axis = self.names.index(k)
        self.names.remove(k)
        columns = keep.shape[-1]
        shape = (2**axis, 2, keep.size // columns // 2 ** (axis + 1), columns)
        self.bit = self.bits[k]
        job = (
            keep.reshape(shape), received.reshape(shape), own_bit(self.bit), self.part, self.parts
        )
        self.part, self.parts = 0, 1
        return job

    def take(self, send, keep):
        self.send, self.keep = (send, self.bit), keep

    def launch(self):
        self.received, self.send = swap(*self.send), None


class Pair:
    def __init__(self, formers, latters, items, rows):
        bit = ("dp", lax.axis_size("dp"), 1)
        self.mine = own_bit(bit)
        self.parts = (formers, latters, [items], rows)
        (send,) = part_grads(*self.parts, 1 - self.mine)
        self.send, self.received, self.keep = (send, bit), None, None

    def own(self):
        (self.keep,) = part_grads(*self.parts, self.mine)
        return self

    def launch(self):
        self.received, self.send = swap(*self.send), None

    def split(self):
        self.pipes = [Scatter(self.keep, self.received, part) for part in range(2)]
        return self.pipes

    def done(self):
        return jnp.concatenate([p.keep for p in self.pipes], axis=1)


class SmallSum:
    def __init__(self, part):
        bits, order = phases(False)
        self.bits = bits
        self.names = order[::-1]
        self.keep, self.received = part, None
        self.send = (part, bits[self.names.pop(0)])

    def step(self):
        self.keep = self.keep + self.received
        self.received = None
        self.send = (self.keep, self.bits[self.names.pop(0)]) if self.names else None

    def launch(self):
        self.received, self.send = swap(*self.send), None

    def done(self):
        return self.keep


def advance(values, pipes):
    live = [p for p in pipes if p.received is not None]
    fresh = [p for p in pipes if p.received is None and p.send is not None]
    size = len(values)
    tied = list(
        tie(
            *values,
            *[p.received for p in live],
            *[p.keep for p in live],
            *[p.send[0] for p in fresh],
        )
    )
    values, tied = tied[:size], tied[size:]
    for p in live:
        p.received = tied.pop(0)
    for p in live:
        p.keep = tied.pop(0)
    for p in fresh:
        p.send = (tied.pop(0), p.send[1])
    now = []
    for p in live:
        if isinstance(p, Pair):
            now += p.split()
        else:
            now.append(p)
    waiting, jobs = [], []
    for p in now:
        if isinstance(p, SmallSum):
            p.step()
            continue
        job = p.job()
        if job is not None:
            waiting.append(p)
            jobs.append(job)
    for p, halves in zip(waiting, add_halves(jobs)):
        p.take(*halves)
    now = [p for p in now + fresh if p.send is not None]
    pipes[:] = now
    held = [p for p in now if p.keep is not None]
    tied = list(tie(*values, *[p.send[0] for p in now], *[p.keep for p in held]))
    values, tied = tied[:size], tied[size:]
    for p in now:
        p.send = (tied.pop(0), p.send[1])
    for p in held:
        p.keep = tied.pop(0)
    for p in now:
        p.launch()
    return values


def local(
    context,
    byte_ids,
    segment_ids,
    cotangent,
    byte_table,
    norm_mixer,
    proj_zgate,
    proj_inputs,
    proj_step,
    conv_kernel,
    conv_bias,
    step_bias,
    decay_log,
    skip_gain,
    mixer_norm,
    proj_mixed,
    norm_attn,
    proj_heads,
    proj_attended,
    norm_ffn,
    ffn_gate,
    ffn_up,
    ffn_down,
):
    row_count, length = segment_ids.shape
    tokens = row_count * length
    model_width = context.shape[2]
    model_rows = norm_mixer.shape[0]
    small = [
        byte_table.reshape(-1),
        norm_mixer,
        conv_kernel.reshape(-1),
        conv_bias,
        mixer_norm,
        norm_attn,
        norm_ffn,
    ]
    lengths = [v.shape[0] for v in small]
    packed = jnp.concatenate(small)
    packed = jnp.pad(packed, (0, -packed.shape[0] % 1024)).reshape(8, -1)
    everyone = gather_small(packed).reshape(-1, packed.size)
    unpacked = []
    start = 0
    for count in lengths:
        unpacked.append(everyone[:, start : start + count])
        start += count
    table_full = unpacked[0].reshape(-1, byte_table.shape[1])
    gain_one = unpacked[1].reshape(-1)
    taps = conv_kernel.shape[0]
    kernel_full = jnp.swapaxes(
        unpacked[2].reshape(-1, taps, conv_kernel.shape[1]), 0, 1
    ).reshape(taps, -1)
    offset_full = unpacked[3].reshape(-1)
    gated_gain = unpacked[4].reshape(-1)
    gain_two = unpacked[5].reshape(-1)
    gain_three = unpacked[6].reshape(-1)
    wide = proj_inputs.shape[1]
    step_padded = jnp.pad(proj_step, ((0, 0), (0, 128 - proj_step.shape[1])))
    g_inputs = Gather(jnp.concatenate([proj_inputs, step_padded], axis=1), False)
    g_zgate = Gather(proj_zgate, True)
    fold_mixed = proj_mixed.shape[0] // model_rows
    fold_down = ffn_down.shape[0] // model_rows
    folded = lambda v, fold: [v[q * model_rows : (q + 1) * model_rows] for q in range(fold)]
    outer_shard = jnp.concatenate(
        [ffn_gate, ffn_up]
        + folded(ffn_down, fold_down)
        + folded(proj_mixed, fold_mixed)
        + [proj_heads, proj_attended],
        axis=1,
    )
    outer_full = lax.all_gather(outer_shard, AXES, axis=0, tiled=True)
    g_inputs.step()
    g_zgate.step()
    (table_full,) = gather_round([g_inputs, g_zgate], [table_full])
    gather_round([g_inputs, g_zgate])
    gather_round([g_inputs, g_zgate])
    gather_round([g_inputs, g_zgate])
    gather_round([g_inputs, g_zgate])
    inputs_step_full = g_inputs.done()
    zgate_full = g_zgate.done()
    symbols = jnp.arange(table_full.shape[0], dtype=jnp.int32)
    onehot = (byte_ids.reshape(-1)[:, None] == symbols[None, :]).astype(jnp.bfloat16)
    embedded = matmul(onehot, table_full).reshape(tokens, model_width)
    stream_zero = embedded + context.reshape(tokens, model_width).astype(jnp.float32)
    normed_one = rms_norm(stream_zero, gain_one.astype(jnp.float32))
    normed_one_low = normed_one.astype(jnp.bfloat16)
    zgate = matmul(normed_one_low, zgate_full).reshape(row_count, length, -1)
    raw = matmul(normed_one_low, inputs_step_full).reshape(row_count, length, -1)
    ids = segment_ids.astype(jnp.float32)
    pad_heads = lambda v: jnp.pad(v, (0, 128 - HM)).reshape(1, 128)
    mixer_terms = (
        ids,
        kernel_full.astype(jnp.float32),
        offset_full.astype(jnp.float32).reshape(1, -1),
        pad_heads(step_bias),
        pad_heads(decay_log),
        jnp.repeat(skip_gain, PM).reshape(1, -1),
        gated_gain.astype(jnp.float32).reshape(1, -1),
    )
    values_low, states_low, combined, gate_low = mixer_forward(raw, zgate, *mixer_terms)
    gate_low = gate_low.reshape(tokens, -1)
    outer_full, _ = tie(outer_full, gate_low)
    hidden_width = ffn_gate.shape[1]
    mixed_start = 2 * hidden_width + fold_down * model_width
    heads_start = mixed_start + fold_mixed * model_width
    attended_start = heads_start + proj_heads.shape[1]
    heads_full = outer_full[:, heads_start:attended_start]
    attended_full = outer_full[:, attended_start:]
    mixed_full = unfold(outer_full, model_rows, mixed_start, fold_mixed, model_width)
    mixer_out = matmul(gate_low, mixed_full)
    stream_one = stream_zero + mixer_out
    normed_two = rms_norm(stream_one, gain_two.astype(jnp.float32))
    normed_two_low = normed_two.astype(jnp.bfloat16)
    joined = matmul(normed_two_low, heads_full).astype(jnp.bfloat16)
    joined = joined.reshape(row_count, length, -1)
    attended_low = attention_forward(joined, ids).reshape(tokens, model_width)
    attn_out = matmul(attended_low, attended_full)
    stream_two = stream_one + attn_out
    normed_three, norm_three_back = jax.vjp(rms_norm, stream_two, gain_three.astype(jnp.float32))
    normed_three_low = normed_three.astype(jnp.bfloat16)
    ffn_grad_low = cotangent.reshape(tokens, model_width)
    grad_three = ffn_grad_low.astype(jnp.float32)
    hidden_low, gate_grad_low, upper_grad_low, ffn_out, grad_normed_three = feed_forward(
        normed_three_low, ffn_grad_low, outer_full, model_rows, hidden_width, fold_down
    )
    stream_three = stream_two + ffn_out
    valid_rows = (segment_ids.reshape(tokens, 1) >= 0).astype(jnp.float32)
    moments = jnp.stack(
        [
            jnp.sum(valid_rows * stream_zero * stream_zero),
            jnp.sum(valid_rows * mixer_out * mixer_out),
            jnp.sum(valid_rows * attn_out * attn_out),
            jnp.sum(valid_rows * ffn_out * ffn_out),
            jnp.sum(valid_rows),
        ]
    )
    fold_width = fold_down * model_width
    s_ffn = Pair(
        [normed_three_low, hidden_low],
        [gate_grad_low, upper_grad_low, ffn_grad_low],
        [
            (0, 0, 1, 0, hidden_width),
            (1, 2, fold_down, 0, fold_width // 2),
            (0, 1, 1, 0, hidden_width),
            (1, 2, fold_down, fold_width // 2, fold_width),
        ],
        model_rows,
    )
    pipes = [s_ffn]
    (grad_normed_three,) = advance((grad_normed_three,), pipes)
    s_ffn.own()
    stream_part, grad_norm_ffn = norm_three_back(grad_normed_three)
    grad_two = grad_three + stream_part
    attn_grad_low = grad_two.astype(jnp.bfloat16)
    attn_grad_low, grad_two = advance((attn_grad_low, grad_two), pipes)
    grad_joined = attention_backward(
        joined,
        attn_grad_low.reshape(row_count, length, model_width),
        outer_full,
        attended_start // model_width,
        ids,
    ).reshape(tokens, -1)
    heads_width = proj_heads.shape[1]
    grad_one, mixer_grad_low, grad_norm_attn = norm_backward(
        [
            (grad_joined, q, outer_full, heads_start // model_width + q, model_width)
            for q in range(3)
        ],
        stream_one,
        gain_two.astype(jnp.float32).reshape(1, -1),
        grad_two,
    )
    grad_norm_attn = grad_norm_attn.reshape(-1)
    zgate_grad_low, heads_grad_low, grad_gated_gain, skip_lanes = gate_backward(
        mixer_grad_low.reshape(row_count, length, model_width),
        mixed_full,
        zgate,
        mixer_terms[-1],
        values_low,
        combined,
    )
    zgate_grad_low = zgate_grad_low.reshape(tokens, -1)
    zgate_width = zgate_grad_low.shape[1]
    s_middle = Pair(
        [normed_two_low, attended_low, normed_one_low, gate_low],
        [grad_joined, attn_grad_low, zgate_grad_low, mixer_grad_low],
        [
            (0, 0, 1, 0, heads_width),
            (1, 1, 1, 0, model_width),
            (2, 2, 1, 0, zgate_width),
            (3, 3, fold_mixed, 0, fold_mixed * model_width),
        ],
        model_rows,
    ).own()
    pipes += [s_middle]
    heads_grad_low, grad_one = advance((heads_grad_low, grad_one), pipes)
    inputs_step_grad_low, grad_conv_kernel, grad_conv_bias, bias_lanes, decay_lanes = (
        mixer_backward(heads_grad_low, raw, *mixer_terms[:-1], values_low, states_low)
    )
    inputs_step_grad_low = inputs_step_grad_low.reshape(tokens, -1)
    inputs_step_grad_low, grad_one = advance((inputs_step_grad_low, grad_one), pipes)
    s_inputs = Pair(
        [normed_one_low],
        [inputs_step_grad_low],
        [(0, 0, 1, 0, inputs_step_grad_low.shape[1])],
        model_rows,
    ).own()
    grad_zero, embed_grad_low, grad_norm_mixer = norm_backward(
        [
            (zgate_grad_low, 0, zgate_full, 0, None),
            (inputs_step_grad_low, 0, inputs_step_full, 0, None),
        ],
        stream_zero,
        gain_one.astype(jnp.float32).reshape(1, -1),
        grad_one,
    )
    grad_norm_mixer = grad_norm_mixer.reshape(-1)
    embed_grad_low = embed_grad_low.reshape(-1, table_full.shape[1])
    grad_byte_table = matmul_left(onehot, embed_grad_low)
    small_grads = [
        moments,
        bias_lanes[0, :HM],
        decay_lanes[0, :HM],
        jnp.sum(skip_lanes.reshape(HM, PM), axis=1),
        grad_conv_kernel.reshape(-1),
        grad_conv_bias.reshape(-1),
        grad_gated_gain.reshape(-1),
        grad_norm_attn,
        grad_norm_ffn,
    ]
    small_lengths = [v.shape[0] for v in small_grads]
    small_packed = jnp.concatenate(small_grads)
    small_packed = jnp.pad(small_packed, (0, -small_packed.shape[0] % 1024)).reshape(-1, 128)
    table_rows = grad_byte_table.shape[0]
    s_small = SmallSum(
        jnp.concatenate([grad_byte_table, grad_norm_mixer.reshape(-1, 128), small_packed], axis=0)
    )
    pipes = [s_inputs, s_small] + pipes
    while pipes:
        advance((), pipes)
    grad_inputs_step = s_inputs.done()
    middle_sums = s_middle.done()
    attention_sums = middle_sums[:, : heads_width + model_width]
    zgate_mixed = middle_sums[:, heads_width + model_width :]
    ffn_sums = s_ffn.done()
    half_fold = fold_width // 2
    second = hidden_width + half_fold
    down_sums = [ffn_sums[:, hidden_width:second], ffn_sums[:, second + hidden_width :]]

    def stacked(v):
        return jnp.concatenate(
            [v[:, q : q + model_width] for q in range(0, v.shape[1], model_width)], axis=0
        )

    def own_part(total, share):
        length = share.shape[-1]
        return lax.dynamic_slice_in_dim(total, own_index() * length, length, total.ndim - 1)

    small_sums = s_small.done()
    table_sum = lax.dynamic_slice_in_dim(
        small_sums, own_index() * byte_table.shape[0], byte_table.shape[0], 0
    )
    small_sums = small_sums[table_rows:].reshape(-1)
    norm_mixer_sum = own_part(small_sums[: grad_norm_mixer.shape[0]], norm_mixer)
    sums = []
    start = grad_norm_mixer.shape[0]
    for count in small_lengths:
        sums.append(small_sums[start : start + count])
        start += count
    totals, bias_total, decay_total, skip_total = sums[:4]
    kernel_sum = sums[4].reshape(taps, -1)
    offset_sum, gated_sum, norm_attn_sum, norm_ffn_sum = sums[5:]
    rms_stats = jnp.sqrt(totals[:4] / (totals[4] * model_width))
    return (
        stream_three.reshape(row_count, length, model_width),
        grad_zero.reshape(row_count, length, model_width),
        rms_stats,
        table_sum,
        norm_mixer_sum,
        zgate_mixed[:, :zgate_width],
        grad_inputs_step[:, :wide],
        grad_inputs_step[:, wide : wide + HM],
        own_part(kernel_sum, conv_kernel),
        own_part(offset_sum, conv_bias),
        bias_total,
        decay_total,
        skip_total,
        own_part(gated_sum, mixer_norm),
        stacked(zgate_mixed[:, zgate_width:]),
        own_part(norm_attn_sum, norm_attn),
        attention_sums[:, :heads_width],
        attention_sums[:, heads_width:],
        own_part(norm_ffn_sum, norm_ffn),
        ffn_sums[:, :hidden_width],
        ffn_sums[:, second : second + hidden_width],
        stacked(jnp.concatenate(down_sums, axis=1)),
    )


def solution(mesh):
    return jax.shard_map(
        local,
        mesh=mesh,
        in_specs=(
            P(("dp", "fsdp"), None, None),
            P(("dp", "fsdp"), None),
            P(("dp", "fsdp"), None),
            P(("dp", "fsdp"), None, None),
            P(("dp", "fsdp"), None),
            P(("dp", "fsdp")),
            P(("dp", "fsdp"), None),
            P(("dp", "fsdp"), None),
            P(("dp", "fsdp"), None),
            P(None, ("dp", "fsdp")),
            P(("dp", "fsdp")),
            P(),
            P(),
            P(),
            P(("dp", "fsdp")),
            P(("dp", "fsdp"), None),
            P(("dp", "fsdp")),
            P(("dp", "fsdp"), None),
            P(("dp", "fsdp"), None),
            P(("dp", "fsdp")),
            P(("dp", "fsdp"), None),
            P(("dp", "fsdp"), None),
            P(("dp", "fsdp"), None),
        ),
        out_specs=(
            P(("dp", "fsdp"), None, None),
            P(("dp", "fsdp"), None, None),
            P(),
            P(("dp", "fsdp"), None),
            P(("dp", "fsdp")),
            P(("dp", "fsdp"), None),
            P(("dp", "fsdp"), None),
            P(("dp", "fsdp"), None),
            P(None, ("dp", "fsdp")),
            P(("dp", "fsdp")),
            P(),
            P(),
            P(),
            P(("dp", "fsdp")),
            P(("dp", "fsdp"), None),
            P(("dp", "fsdp")),
            P(("dp", "fsdp"), None),
            P(("dp", "fsdp"), None),
            P(("dp", "fsdp")),
            P(("dp", "fsdp"), None),
            P(("dp", "fsdp"), None),
            P(("dp", "fsdp"), None),
        ),
        check_vma=False,
    )
```

```python
from functools import partial

import jax
import jax.numpy as jnp
from jax import lax
from jax.experimental import pallas as pl
from jax.experimental.pallas import tpu as pltpu
from jax.sharding import PartitionSpec as P

DI = 2048
NS = 128
PM = 64
HD = 64
HM = 32


EPS = 1e-05


def matmul(former, latter):
    return jnp.dot(former, latter, preferred_element_type=jnp.float32)


def matmul_left(former, latter):
    return lax.dot_general(
        former, latter, (((0,), (0,)), ((), ())), preferred_element_type=jnp.float32
    )


def matmul_right(former, latter):
    return lax.dot_general(
        former, latter, (((1,), (1,)), ((), ())), preferred_element_type=jnp.float32
    )


def rms_norm(values, scaling):
    return values * lax.rsqrt(jnp.mean(values * values, axis=-1, keepdims=True) + EPS) * scaling


VMEM_LIMIT = 48 * 1024 * 1024
BRIEF = pl.CostEstimate(flops=1024, transcendentals=0, bytes_accessed=1024)


def column_sum(v):
    return jnp.sum(v, axis=0, keepdims=True)


def sigmoid(v):
    return 1.0 / (1.0 + jnp.exp(-v))


def down_rows(v, count):
    return pltpu.roll(v, count, 0)


def up_rows(v, count):
    return pltpu.roll(v, v.shape[0] - count, 0)


def turned(v):
    length = v.shape[0]
    row = lax.broadcasted_iota(jnp.int32, (length, length), 0)
    column = lax.broadcasted_iota(jnp.int32, (length, length), 1)
    unit = (row == column).astype(jnp.float32)
    return lax.dot_general(
        v,
        unit,
        (((0,), (0,)), ((), ())),
        precision=lax.Precision.HIGHEST,
        preferred_element_type=jnp.float32,
    )


def turned_back(v):
    length = v.shape[1]
    row = lax.broadcasted_iota(jnp.int32, (length, length), 0)
    column = lax.broadcasted_iota(jnp.int32, (length, length), 1)
    unit = (row == column).astype(jnp.float32)
    return lax.dot_general(
        unit,
        v,
        (((1,), (1,)), ((), ())),
        precision=lax.Precision.HIGHEST,
        preferred_element_type=jnp.float32,
    )


def allowed_mask(ids_column, ids_row):
    length = ids_column.shape[0]
    row = lax.broadcasted_iota(jnp.int32, (length, length), 0)
    column = lax.broadcasted_iota(jnp.int32, (length, length), 1)
    return (ids_column == ids_row) & (row >= column)


def link_columns(ids_column, taps):
    length = ids_column.shape[0]
    place = lax.broadcasted_iota(jnp.int32, (length, 128), 0)
    wide = jnp.broadcast_to(ids_column, (length, 128))
    return [
        ((down_rows(wide, j) == wide) & (place >= j)).astype(jnp.float32)[:, :1]
        for j in range(1, taps)
    ]


def conv_chunk(raw, taps_chunk, offset, links):
    taps = taps_chunk.shape[0]
    shifted = [raw] + [down_rows(raw, j) * links[j - 1] for j in range(1, taps)]
    total = offset
    for j in range(taps):
        total = total + shifted[j] * taps_chunk[taps - 1 - j : taps - j]
    return total, shifted


def step_terms(step_raw, step_bias, decay_log):
    shifted = step_raw + step_bias
    step = jnp.maximum(shifted, 0.0) + jnp.log1p(jnp.exp(-jnp.abs(shifted)))
    rate = -jnp.exp(decay_log) * step
    length = step.shape[0]
    place = lax.broadcasted_iota(jnp.int32, step.shape, 0)
    total = rate
    shift = 1
    while shift < length:
        total = total + jnp.where(place >= shift, down_rows(total, shift), 0.0)
        shift *= 2
    return shifted, step, rate, total


def mixer_forward_kernel(
    raw_ref, zgate_ref, ids_column_ref, ids_row_ref, taps_ref, offset_ref,
    bias_ref, decay_ref, skip_ref, gain_ref,
    values_ref, states_ref, combined_ref, gate_ref,
):
    taps = taps_ref.shape[0]
    ids_column = ids_column_ref[0]
    links = link_columns(ids_column, taps)
    channels = taps_ref.shape[1]
    for start in range(0, channels, 256):
        part = slice(start, start + 256)
        total, _ = conv_chunk(raw_ref[0, :, part], taps_ref[:, part], offset_ref[:, part], links)
        low = (total * sigmoid(total)).astype(jnp.bfloat16)
        if start < DI:
            values_ref[0, :, part] = low
        else:
            states_ref[0] = low
    state_in, state_out = states_ref[0, :, :NS], states_ref[0, :, NS:]
    gram = matmul_right(state_out, state_in)
    _, step, _, total = step_terms(
        raw_ref[0, :, channels : channels + 128], bias_ref[...], decay_ref[...]
    )
    total_rows, step_rows = turned(total), turned(step)
    mask = allowed_mask(ids_column, ids_row_ref[0])
    gram = jnp.where(mask, gram, 0.0)
    length = gram.shape[0]
    first = lax.broadcasted_iota(jnp.int32, (length, 2 * PM), 1) < PM
    squares = jnp.zeros((length, 1), jnp.float32)
    for pair in range(HM // 2):
        lanes = slice(pair * 2 * PM, (pair + 1) * 2 * PM)
        values = values_ref[0, :, lanes]
        outs = []
        for head in (2 * pair, 2 * pair + 1):
            between = total[:, head : head + 1] - total_rows[head : head + 1, :]
            decayed = jnp.exp(jnp.where(mask, between, 0.0))
            mix = gram * decayed * step_rows[head : head + 1, :]
            outs.append(matmul(mix.astype(jnp.bfloat16), values))
        combined = jnp.where(first, outs[0], outs[1]) + skip_ref[:, lanes] * values.astype(
            jnp.float32
        )
        combined_ref[0, :, lanes] = combined
        zgate = zgate_ref[0, :, lanes]
        gated = combined * (zgate * sigmoid(zgate))
        squares = squares + jnp.sum(gated * gated, axis=1, keepdims=True)
    scale = lax.rsqrt(squares / DI + EPS)
    for start in range(0, DI, 256):
        part = slice(start, start + 256)
        zgate = zgate_ref[0, :, part]
        gated = combined_ref[0, :, part] * (zgate * sigmoid(zgate))
        gate_ref[0, :, part] = (gated * scale * gain_ref[:, part]).astype(jnp.bfloat16)


def gate_backward_kernel(
    upper_ref, weight_ref, zgate_ref, gain_ref, values_ref, combined_ref,
    zgrad_ref, heads_ref, gain_grad_ref, skip_grad_ref, grad_ref,
):
    grad_ref[0] = matmul_right(upper_ref[0], weight_ref[...])

    @pl.when(pl.program_id(0) == 0)
    def _():
        for ref in (gain_grad_ref, skip_grad_ref):
            ref[...] = jnp.zeros(ref.shape, ref.dtype)

    length = grad_ref.shape[1]
    squares = jnp.zeros((length, 1), jnp.float32)
    product = jnp.zeros((length, 1), jnp.float32)
    for start in range(0, DI, 256):
        part = slice(start, start + 256)
        zgate = zgate_ref[0, :, part]
        gated = combined_ref[0, :, part] * (zgate * sigmoid(zgate))
        squares = squares + jnp.sum(gated * gated, axis=1, keepdims=True)
        product = product + jnp.sum(
            gated * grad_ref[0, :, part] * gain_ref[:, part], axis=1, keepdims=True
        )
    scale = lax.rsqrt(squares / DI + EPS)
    inner = scale * scale * scale * (product / DI)
    for start in range(0, DI, 256):
        part = slice(start, start + 256)
        zgate = zgate_ref[0, :, part]
        combined = combined_ref[0, :, part]
        sig = sigmoid(zgate)
        silu = zgate * sig
        gated = combined * silu
        grad = grad_ref[0, :, part]
        gain_grad_ref[:, part] += column_sum(grad * gated * scale)
        grad_gated = scale * grad * gain_ref[:, part] - gated * inner
        grad_combined = grad_gated * silu
        zgrad_ref[0, :, part] = (grad_gated * combined * (sig + silu * (1.0 - sig))).astype(
            jnp.bfloat16
        )
        skip_grad_ref[:, part] += column_sum(
            grad_combined * values_ref[0, :, part].astype(jnp.float32)
        )
        heads_ref[0, :, part] = grad_combined.astype(jnp.bfloat16)


def mixer_backward_kernel(
    heads_ref, raw_ref, ids_column_ref, ids_row_ref, taps_ref, offset_ref,
    bias_ref, decay_ref, skip_ref, values_ref, states_ref,
    xgrad_ref, taps_grad_ref, offset_grad_ref, bias_grad_ref, decay_grad_ref, through_ref,
):
    taps = taps_ref.shape[0]
    channels = taps_ref.shape[1]
    length = raw_ref.shape[1]

    @pl.when(pl.program_id(0) == 0)
    def _():
        for ref in (taps_grad_ref, offset_grad_ref, bias_grad_ref, decay_grad_ref):
            ref[...] = jnp.zeros(ref.shape, ref.dtype)

    ids_column = ids_column_ref[0]
    links = link_columns(ids_column, taps)
    state_in, state_out = states_ref[0, :, :NS], states_ref[0, :, NS:]
    shifted_step, step, rate, total = step_terms(
        raw_ref[0, :, channels : channels + 128], bias_ref[...], decay_ref[...]
    )
    total_rows, step_rows = turned(total), turned(step)
    mask = allowed_mask(ids_column, ids_row_ref[0])
    gram = jnp.where(mask, matmul_right(state_out, state_in), 0.0)
    first = lax.broadcasted_iota(jnp.int32, (length, 2 * PM), 1) < PM
    lane = lax.broadcasted_iota(jnp.int32, (length, 128), 1)
    row = lax.broadcasted_iota(jnp.int32, (128, length), 0)
    grad_gram = jnp.zeros((length, length), jnp.float32)
    by_row = jnp.zeros((length, 128), jnp.float32)
    by_column = jnp.zeros((128, length), jnp.float32)
    nothing = jnp.zeros((length, 2 * PM), jnp.bfloat16)
    for pair in range(HM // 2):
        lanes = slice(pair * 2 * PM, (pair + 1) * 2 * PM)
        values = values_ref[0, :, lanes]
        heads = heads_ref[0, :, lanes]
        outs = []
        for head, own in ((2 * pair, first), (2 * pair + 1, ~first)):
            between = total[:, head : head + 1] - total_rows[head : head + 1, :]
            decayed = jnp.where(mask, jnp.exp(jnp.where(mask, between, 0.0)), 0.0)
            step_row = step_rows[head : head + 1, :]
            mixed = gram * decayed
            grad_mix = matmul_right(jnp.where(own, heads, nothing), values)
            outs.append(matmul_left((mixed * step_row).astype(jnp.bfloat16), heads))
            grad_gram = grad_gram + grad_mix * decayed * step_row
            direct = grad_mix * mixed
            by_column = by_column + jnp.where(row == head, column_sum(direct), 0.0)
            by_row = by_row + jnp.where(
                lane == head, jnp.sum(direct * step_row, axis=1, keepdims=True), 0.0
            )
        through_ref[:, lanes] = jnp.where(first, outs[0], outs[1]) + skip_ref[
            :, lanes
        ] * heads.astype(jnp.float32)
    grad_step = turned_back(by_column)
    grad_total = by_row - grad_step * step
    place = lax.broadcasted_iota(jnp.int32, grad_total.shape, 0)
    shift = 1
    while shift < length:
        grad_total = grad_total + jnp.where(
            place < length - shift, up_rows(grad_total, shift), 0.0
        )
        shift *= 2
    decay_grad_ref[...] += column_sum(grad_total * rate)
    grad_step = grad_step - grad_total * jnp.exp(decay_ref[...])
    grad_raw = jnp.where(lane < HM, grad_step * sigmoid(shifted_step), 0.0)
    bias_grad_ref[...] += column_sum(grad_raw)
    xgrad_ref[0, :, channels : channels + 128] = grad_raw.astype(jnp.bfloat16)
    extra = xgrad_ref.shape[2] - channels - 128
    if extra:
        xgrad_ref[0, :, channels + 128 :] = jnp.zeros((length, extra), jnp.bfloat16)
    gram_low = grad_gram.astype(jnp.bfloat16)
    grad_in = matmul_left(gram_low, state_out)
    grad_out = matmul(gram_low, state_in)
    for start in range(0, channels, 128):
        part = slice(start, start + 128)
        chunk_taps = taps_ref[:, part]
        total, shifted = conv_chunk(raw_ref[0, :, part], chunk_taps, offset_ref[:, part], links)
        sig = sigmoid(total)
        if start < DI:
            grad = through_ref[:, part]
        else:
            grad = grad_in if start == DI else grad_out
        grad = grad * (sig + total * sig * (1.0 - sig))
        offset_grad_ref[:, part] += column_sum(grad)
        back = grad * chunk_taps[taps - 1 : taps]
        sums = [column_sum(grad * shifted[0])]
        for j in range(1, taps):
            sums.append(column_sum(grad * shifted[j]))
            linked = grad * links[j - 1]
            back = back + up_rows(linked, j) * chunk_taps[taps - 1 - j : taps - j]
        taps_grad_ref[:, part] += jnp.concatenate(sums[::-1], axis=0)
        xgrad_ref[0, :, part] = back.astype(jnp.bfloat16)


def whole(rows, columns):
    return pl.BlockSpec((rows, columns), lambda n: (0, 0))


def mixer_forward(raw, zgate, ids, taps, offset, bias, decay, skip, gain):
    count, length, columns = raw.shape
    row = lambda c: pl.BlockSpec((1, length, c), lambda n: (n, 0, 0))
    channels = taps.shape[1]
    return pl.pallas_call(
        mixer_forward_kernel,
        grid=(count,),
        in_specs=[
            row(columns), row(DI), row(1), pl.BlockSpec((1, 1, length), lambda n: (n, 0, 0)),
            whole(*taps.shape), whole(1, channels), whole(1, 128), whole(1, 128),
            whole(1, DI), whole(1, DI),
        ],
        out_specs=[row(DI), row(2 * NS), row(DI), row(DI)],
        out_shape=[
            jax.ShapeDtypeStruct((count, length, DI), jnp.bfloat16),
            jax.ShapeDtypeStruct((count, length, 2 * NS), jnp.bfloat16),
            jax.ShapeDtypeStruct((count, length, DI), jnp.float32),
            jax.ShapeDtypeStruct((count, length, DI), jnp.bfloat16),
        ],
        compiler_params=pltpu.CompilerParams(vmem_limit_bytes=VMEM_LIMIT),
        cost_estimate=BRIEF,
    )(raw, zgate, ids[:, :, None], ids[:, None, :], taps, offset, bias, decay, skip, gain)


def gate_backward(upper, weight, zgate, gain, values, combined):
    count, length, width = upper.shape
    row = lambda c: pl.BlockSpec((1, length, c), lambda n: (n, 0, 0))
    one = lambda r, c: jax.ShapeDtypeStruct((r, c), jnp.float32)
    return pl.pallas_call(
        gate_backward_kernel,
        grid=(count,),
        in_specs=[
            row(width), whole(DI, width), row(DI), whole(1, DI), row(DI), row(DI)
        ],
        out_specs=[row(DI), row(DI), whole(1, DI), whole(1, DI)],
        out_shape=[
            jax.ShapeDtypeStruct((count, length, DI), jnp.bfloat16),
            jax.ShapeDtypeStruct((count, length, DI), jnp.bfloat16),
            one(1, DI), one(1, DI),
        ],
        scratch_shapes=[pltpu.VMEM((1, length, DI), jnp.float32)],
        compiler_params=pltpu.CompilerParams(vmem_limit_bytes=VMEM_LIMIT),
        cost_estimate=BRIEF,
    )(upper, weight, zgate, gain, values, combined)


def mixer_backward(heads, raw, ids, taps, offset, bias, decay, skip, values, states):
    count, length, columns = raw.shape
    row = lambda c: pl.BlockSpec((1, length, c), lambda n: (n, 0, 0))
    channels = taps.shape[1]
    extra = -columns % 256
    one = lambda r, c: jax.ShapeDtypeStruct((r, c), jnp.float32)
    return pl.pallas_call(
        mixer_backward_kernel,
        grid=(count,),
        in_specs=[
            row(DI), row(columns), row(1),
            pl.BlockSpec((1, 1, length), lambda n: (n, 0, 0)),
            whole(*taps.shape), whole(1, channels), whole(1, 128), whole(1, 128),
            whole(1, DI), row(DI), row(2 * NS),
        ],
        out_specs=[
            row(columns + extra), whole(*taps.shape), whole(1, channels), whole(1, 128),
            whole(1, 128),
        ],
        out_shape=[
            jax.ShapeDtypeStruct((count, length, columns + extra), jnp.bfloat16),
            one(*taps.shape), one(1, channels), one(1, 128), one(1, 128),
        ],
        scratch_shapes=[pltpu.VMEM((length, DI), jnp.float32)],
        compiler_params=pltpu.CompilerParams(vmem_limit_bytes=VMEM_LIMIT),
        cost_estimate=BRIEF,
    )(heads, raw, ids[:, :, None], ids[:, None, :], taps, offset, bias, decay, skip, values, states)


def head_scores(query, key, own, mask, nothing):
    scores = matmul_right(jnp.where(own, query, nothing), key) * HD ** (-0.5)
    masked = jnp.where(mask, scores, -1e30)
    highest = jnp.max(masked, axis=1, keepdims=True)
    exponents = jnp.exp(masked - highest)
    return exponents / jnp.sum(exponents, axis=1, keepdims=True)


def attention_forward_kernel(joined_ref, ids_column_ref, ids_row_ref, out_ref):
    mask = allowed_mask(ids_column_ref[0], ids_row_ref[0])
    length, width = out_ref.shape[1:]
    first = lax.broadcasted_iota(jnp.int32, (length, 2 * HD), 1) < HD
    nothing = jnp.zeros((length, 2 * HD), jnp.bfloat16)
    for start in range(0, width, 2 * HD):
        query, key, value = (
            joined_ref[0, :, k * width + start : k * width + start + 2 * HD] for k in range(3)
        )
        outs = []
        for own in (first, ~first):
            chances = head_scores(query, key, own, mask, nothing)
            outs.append(matmul(chances.astype(jnp.bfloat16), value))
        out_ref[0, :, start : start + 2 * HD] = jnp.where(first, outs[0], outs[1]).astype(
            jnp.bfloat16
        )


def attention_backward_kernel(
    joined_ref, upper_ref, weight_ref, ids_column_ref, ids_row_ref, out_ref, grad_ref
):
    grad_ref[0] = matmul_right(upper_ref[0], weight_ref[...]).astype(jnp.bfloat16)
    mask = allowed_mask(ids_column_ref[0], ids_row_ref[0])
    length, width = grad_ref.shape[1:]
    first = lax.broadcasted_iota(jnp.int32, (length, 2 * HD), 1) < HD
    nothing = jnp.zeros((length, 2 * HD), jnp.bfloat16)
    scale = HD ** (-0.5)
    for start in range(0, width, 2 * HD):
        query, key, value = (
            joined_ref[0, :, k * width + start : k * width + start + 2 * HD] for k in range(3)
        )
        grad = grad_ref[0, :, start : start + 2 * HD]
        outs = [[], [], []]
        for own in (first, ~first):
            chances = head_scores(query, key, own, mask, nothing)
            grad_chances = matmul_right(jnp.where(own, grad, nothing), value)
            inner = jnp.sum(chances * grad_chances, axis=1, keepdims=True)
            grad_scores = (chances * (grad_chances - inner)).astype(jnp.bfloat16)
            outs[0].append(matmul(grad_scores, key) * scale)
            outs[1].append(matmul_left(grad_scores, query) * scale)
            outs[2].append(matmul_left(chances.astype(jnp.bfloat16), grad))
        for k in range(3):
            out_ref[0, :, k * width + start : k * width + start + 2 * HD] = jnp.where(
                first, outs[k][0], outs[k][1]
            ).astype(jnp.bfloat16)


def attention_forward(joined, ids):
    count, length, columns = joined.shape
    row = lambda c: pl.BlockSpec((1, length, c), lambda n: (n, 0, 0))
    return pl.pallas_call(
        attention_forward_kernel,
        grid=(count,),
        in_specs=[row(columns), row(1), pl.BlockSpec((1, 1, length), lambda n: (n, 0, 0))],
        out_specs=row(columns // 3),
        out_shape=jax.ShapeDtypeStruct((count, length, columns // 3), jnp.bfloat16),
        compiler_params=pltpu.CompilerParams(vmem_limit_bytes=VMEM_LIMIT),
        cost_estimate=BRIEF,
    )(joined, ids[:, :, None], ids[:, None, :])


def attention_backward(joined, upper, full, block, ids):
    count, length, columns = joined.shape
    width = columns // 3
    row = lambda c: pl.BlockSpec((1, length, c), lambda n: (n, 0, 0))
    return pl.pallas_call(
        attention_backward_kernel,
        grid=(count,),
        in_specs=[
            row(columns), row(width), pl.BlockSpec((width, width), lambda n: (0, block)), row(1),
            pl.BlockSpec((1, 1, length), lambda n: (n, 0, 0)),
        ],
        out_specs=row(columns),
        out_shape=jax.ShapeDtypeStruct((count, length, columns), jnp.bfloat16),
        scratch_shapes=[pltpu.VMEM((1, length, width), jnp.bfloat16)],
        compiler_params=pltpu.CompilerParams(vmem_limit_bytes=VMEM_LIMIT),
        cost_estimate=BRIEF,
    )(joined, upper, full, ids[:, :, None], ids[:, None, :])


def norm_backward_kernel(count, *refs):
    acts, weights = refs[:count], refs[count : 2 * count]
    stream_ref, gain_ref, base_ref, total_ref, low_ref, gain_grad_ref, sum_ref = refs[2 * count :]
    step = pl.program_id(0)
    rows = weights[0].shape[0]
    part = 0.0
    for act, weight in zip(acts, weights):
        part = part + matmul_right(act[:, : weight.shape[1]], weight[...])
    sum_ref[:, pl.ds(pl.multiple_of(step * rows, rows), rows)] = part

    @pl.when(step == pl.num_programs(0) - 1)
    def _():
        values, grad, gain = stream_ref[...], sum_ref[...], gain_ref[...]
        scale = lax.rsqrt(jnp.mean(values * values, axis=1, keepdims=True) + EPS)
        gain_grad_ref[...] = column_sum(grad * values * scale)
        scaled = grad * gain
        inner = jnp.mean(scaled * values, axis=1, keepdims=True)
        total = base_ref[...] + scale * scaled - values * (scale * scale * scale * inner)
        total_ref[...] = total
        low_ref[...] = total.astype(jnp.bfloat16)


def norm_backward(pairs, stream, gain, base):
    tokens, width = stream.shape
    rows = width // 4
    fixed = lambda r, c, k=0: pl.BlockSpec((r, c), lambda i: (0, k))
    return pl.pallas_call(
        partial(norm_backward_kernel, len(pairs)),
        grid=(4,),
        in_specs=[fixed(tokens, a.shape[1] if w is None else w, k) for a, k, _, _, w in pairs]
        + [
            pl.BlockSpec((rows, m.shape[1] if w is None else w), lambda i, k=k: (i, k))
            for _, _, m, k, w in pairs
        ]
        + [fixed(tokens, width), fixed(1, width), fixed(tokens, width)],
        out_specs=[fixed(tokens, width), fixed(tokens, width), fixed(1, width)],
        out_shape=[
            jax.ShapeDtypeStruct((tokens, width), jnp.float32),
            jax.ShapeDtypeStruct((tokens, width), jnp.bfloat16),
            jax.ShapeDtypeStruct((1, width), jnp.float32),
        ],
        scratch_shapes=[pltpu.VMEM((tokens, width), jnp.float32)],
        compiler_params=pltpu.CompilerParams(vmem_limit_bytes=VMEM_LIMIT),
        cost_estimate=BRIEF,
    )(*[p[0] for p in pairs], *[p[2] for p in pairs], stream, gain, base)


def ffn_kernel(
    rows, fold, source_ref, grad_ref, gate_ref, upper_ref, folded_ref,
    hidden_ref, gate_grad_ref, upper_grad_ref, out_ref, back_ref, down_ref,
):
    @pl.when(pl.program_id(0) == 0)
    def _():
        out_ref[...] = jnp.zeros(out_ref.shape, jnp.float32)
        back_ref[...] = jnp.zeros(back_ref.shape, jnp.float32)

    width = out_ref.shape[1]
    for d in range(folded_ref.shape[0] // rows):
        for q in range(fold):
            place = (d * fold + q) * rows
            down_ref[place : place + rows, :] = folded_ref[
                d * rows : (d + 1) * rows, q * width : (q + 1) * width
            ]
    source, grad = source_ref[...], grad_ref[...]
    gate_pre = matmul(source, gate_ref[...])
    up_pre = matmul(source, upper_ref[...])
    sig = sigmoid(gate_pre)
    silu = gate_pre * sig
    hidden = (silu * up_pre).astype(jnp.bfloat16)
    hidden_ref[...] = hidden
    out_ref[...] += matmul(hidden, down_ref[...])
    grad_hidden = matmul_right(grad, down_ref[...])
    gate_grad = (grad_hidden * up_pre * (sig + silu * (1.0 - sig))).astype(jnp.bfloat16)
    upper_grad = (grad_hidden * silu).astype(jnp.bfloat16)
    gate_grad_ref[...] = gate_grad
    upper_grad_ref[...] = upper_grad
    back_ref[...] += matmul_right(gate_grad, gate_ref[...]) + matmul_right(
        upper_grad, upper_ref[...]
    )


def feed_forward(source, grad, full, rows, hidden_width, fold):
    tokens, width = source.shape
    tile = 512
    steps = hidden_width // tile
    all_rows = lambda c: pl.BlockSpec((tokens, c), lambda j: (0, j))
    fixed = pl.BlockSpec((tokens, width), lambda j: (0, 0))
    down_block = 2 * hidden_width // (fold * width)
    return pl.pallas_call(
        partial(ffn_kernel, rows, fold),
        grid=(steps,),
        in_specs=[
            fixed,
            fixed,
            pl.BlockSpec((width, tile), lambda j: (0, j)),
            pl.BlockSpec((width, tile), lambda j: (0, steps + j)),
            pl.BlockSpec((tile // fold, fold * width), lambda j: (j, down_block)),
        ],
        out_specs=[all_rows(tile)] * 3 + [fixed] * 2,
        out_shape=[jax.ShapeDtypeStruct((tokens, hidden_width), jnp.bfloat16)] * 3
        + [jax.ShapeDtypeStruct((tokens, width), jnp.float32)] * 2,
        scratch_shapes=[pltpu.VMEM((tile, width), jnp.bfloat16)],
        compiler_params=pltpu.CompilerParams(vmem_limit_bytes=VMEM_LIMIT),
        cost_estimate=BRIEF,
    )(source, grad, full, full, full)


AXES = ("dp", "fsdp")


def axis_bits():
    bits = []
    for name in AXES:
        size = lax.axis_size(name)
        step = size // 2
        while step:
            bits.append((name, size, step))
            step //= 2
    return bits


def phases(flip, turn=False):
    bits = axis_bits()
    outer = [k for k, b in enumerate(bits) if b[0] == "dp" and b[2] > 1]
    core = [k for k, b in enumerate(bits) if b[0] == "dp" and b[2] == 1]
    inner = [k for k, b in enumerate(bits) if b[0] == "fsdp"]
    return bits, (outer[::-1] if turn else outer) + (inner if flip else inner[::-1]) + core


def swap(v, bit):
    name, size, step = bit
    return lax.ppermute(v, name, [(i, i ^ step) for i in range(size)])


def own_bit(bit):
    return (lax.axis_index(bit[0]) // bit[2]) % 2


def own_index():
    return lax.axis_index("dp") * lax.axis_size("fsdp") + lax.axis_index("fsdp")


def bit_weight(bit):
    return bit[2] * (lax.axis_size("fsdp") if bit[0] == "dp" else 1)


def assemble_kernel(offsets, me_ref, *refs):
    pieces, out_ref, sems = refs[:-2], refs[-2], refs[-1]
    me = me_ref[0]
    copies = []
    count = 0
    for piece, places in zip(pieces, offsets):
        for j, place in enumerate(places):
            copies.append(
                pltpu.make_async_copy(piece.at[j], out_ref.at[me ^ place], sems.at[count])
            )
            count += 1
    for c in copies:
        c.start()
    for c in copies:
        c.wait()


def tie(*values):
    return lax.optimization_barrier(values)


class Gather:
    def __init__(self, shard, flip):
        self.rows, self.columns = shard.shape
        self.bits, self.order = phases(flip, True)
        self.pieces = [(shard[None], [0])]
        self.phase = 0

    def step(self):
        k = self.order[self.phase]
        weight = bit_weight(self.bits[k])
        if len(self.pieces) > 1 and self.phase < len(self.order) - 1:
            joined = jnp.concatenate([p for p, _ in self.pieces], axis=0)
            self.pieces = [(joined, sum((o for _, o in self.pieces), []))]
        self.pieces = self.pieces + [
            (swap(p, self.bits[k]), [o ^ weight for o in offs]) for p, offs in self.pieces
        ]
        self.phase += 1

    def done(self):
        while self.phase < len(self.order):
            self.step()
        count = 2 ** len(self.bits)
        me = own_index().astype(jnp.int32).reshape(1)
        out = pl.pallas_call(
            partial(assemble_kernel, [o for _, o in self.pieces]),
            out_shape=jax.ShapeDtypeStruct((count, self.rows, self.columns), jnp.bfloat16),
            in_specs=[pl.BlockSpec(memory_space=pltpu.SMEM)]
            + [pl.BlockSpec(memory_space=pl.ANY)] * len(self.pieces),
            out_specs=pl.BlockSpec(memory_space=pltpu.VMEM),
            scratch_shapes=[pltpu.SemaphoreType.DMA((count,))],
            compiler_params=pltpu.CompilerParams(vmem_limit_bytes=24 * 1024 * 1024),
            cost_estimate=BRIEF,
        )(me, *[p for p, _ in self.pieces])
        return out.reshape(count * self.rows, self.columns)


def unfold_kernel(start, fold, full_ref, out_ref, sems):
    columns = out_ref.shape[3]
    copies = [
        pltpu.make_async_copy(
            full_ref.at[:, :, pl.ds(start + q * columns, columns)], out_ref.at[:, q], sems.at[q]
        )
        for q in range(fold)
    ]
    for c in copies:
        c.start()
    for c in copies:
        c.wait()


def unfold(full, rows, start, fold, columns):
    count = full.shape[0] // rows
    out = pl.pallas_call(
        partial(unfold_kernel, start, fold),
        out_shape=jax.ShapeDtypeStruct((count, fold, rows, columns), full.dtype),
        in_specs=[pl.BlockSpec(memory_space=pl.ANY)],
        out_specs=pl.BlockSpec(memory_space=pltpu.VMEM),
        scratch_shapes=[pltpu.SemaphoreType.DMA((fold,))],
        compiler_params=pltpu.CompilerParams(vmem_limit_bytes=24 * 1024 * 1024),
        cost_estimate=BRIEF,
    )(full.reshape(count, rows, full.shape[1]))
    return out.reshape(count * fold * rows, columns)


def gather_round(gathers, values=(), fresh=()):
    sizes = [len(g.pieces) for g in gathers]
    tied = tie(
        *values, *[g.pieces[0][0] for g in fresh], *[p for g in gathers for p, _ in g.pieces]
    )
    head = len(values)
    for g in fresh:
        g.pieces[0] = (tied[head], g.pieces[0][1])
        head += 1
    for g, size in zip(gathers, sizes):
        g.pieces = [(tied[head + k], g.pieces[k][1]) for k in range(size)]
        head += size
    for g in [*gathers, *fresh]:
        if g.phase < len(g.order):
            g.step()
    return tied[: len(values)]


def gather_small(shard):
    bits = axis_bits()
    out = shard[None]
    for bit in bits[::-1]:
        other = swap(out, bit)
        mine = own_bit(bit) == 0
        out = jnp.concatenate([jnp.where(mine, out, other), jnp.where(mine, other, out)], axis=0)
    return out


def scatter_sum(part, flip, core_done, wide=False):
    bits, order = phases(flip)
    names = [k for k in range(len(bits)) if not (core_done and bits[k][0] == "dp" and bits[k][2] == 1)]
    count = 2 ** len(names)
    part = part.reshape([2] * len(names) + [part.shape[0] // count, part.shape[1]])
    for n, k in enumerate([k for k in order[::-1] if k in names]):
        axis = names.index(k)
        names.remove(k)
        mine = own_bit(bits[k])
        send = lax.dynamic_index_in_dim(part, 1 - mine, axis, keepdims=False)
        keep = lax.dynamic_index_in_dim(part, mine, axis, keepdims=False)
        total = keep.astype(jnp.float32) + swap(send, bits[k]).astype(jnp.float32)
        part = total if not names else total.astype(part.dtype)
    return part.astype(jnp.float32)


def core_columns(former, core):
    outer = lax.axis_size("dp") // 2
    group = former.shape[1] // (2 * outer)
    return jnp.concatenate(
        [lax.dynamic_slice_in_dim(former, (2 * i + core) * group, group, 1) for i in range(outer)],
        axis=1,
    )


def grads_kernel(plan, rows, counts, core_ref, *refs):
    formers, latters = refs[: counts[0]], refs[counts[0] : counts[0] + counts[1]]
    products = {}
    for out_ref, items in zip(refs[counts[0] + counts[1] :], plan):
        start = 0
        for former, latter, fold, low, high in items:
            if fold == 1:
                for at in range(low, high, 512):
                    to = min(at + 512, high)
                    out_ref[:, start + at - low : start + to - low] = matmul_left(
                        formers[former][...], latters[latter][:, at:to]
                    ).astype(jnp.bfloat16)
            else:
                if (former, latter) not in products:
                    products[former, latter] = matmul_left(
                        formers[former][...], latters[latter][...]
                    ).astype(jnp.bfloat16)
                product = products[former, latter]
                width = product.shape[1]
                for d in range(product.shape[0] // (fold * rows)):
                    for q in range(low // width, high // width):
                        to = start + q * width - low
                        place = (d * fold + q) * rows
                        out_ref[d * rows : (d + 1) * rows, to : to + width] = product[
                            place : place + rows, :
                        ]
            start += high - low


def part_grads(formers, latters, plan, rows, core):
    tokens = formers[0].shape[0]
    outer = lax.axis_size("dp") // 2
    groups = [f.shape[1] // (2 * outer) for f in formers]
    height = rows * lax.axis_size("fsdp")
    widths = [sum(item[4] - item[3] for item in items) for items in plan]
    shapes = [jax.ShapeDtypeStruct((outer * height, w), jnp.bfloat16) for w in widths]
    if any(g % 128 for g in groups):
        outs = []
        for items in plan:
            parts = []
            for former, latter, fold, low, high in items:
                product = matmul_left(core_columns(formers[former], core), latters[latter])
                width = product.shape[1]
                product = jnp.swapaxes(product.reshape(-1, fold, rows, width), 1, 2)
                parts.append(product.reshape(-1, fold * width)[:, low:high])
            outs.append(jnp.concatenate(parts, axis=1).astype(jnp.bfloat16))
        return outs
    return pl.pallas_call(
        partial(grads_kernel, plan, rows, (len(formers), len(latters))),
        grid_spec=pltpu.PrefetchScalarGridSpec(
            num_scalar_prefetch=1,
            grid=(outer,),
            in_specs=[pl.BlockSpec((tokens, g), lambda i, c: (0, 2 * i + c[0])) for g in groups]
            + [pl.BlockSpec(v.shape, lambda i, c: (0, 0)) for v in latters],
            out_specs=[pl.BlockSpec((height, w), lambda i, c: (i, 0)) for w in widths],
        ),
        out_shape=shapes,
        compiler_params=pltpu.CompilerParams(vmem_limit_bytes=VMEM_LIMIT),
        cost_estimate=BRIEF,
    )(core.astype(jnp.int32).reshape(1), *formers, *latters)


def add_halves_kernel(count, mine_ref, *refs):
    for k in range(count):
        give, give_more, hold, hold_more = refs[4 * k : 4 * k + 4]
        send_ref, keep_ref = refs[4 * count + 2 * k : 4 * count + 2 * k + 2]
        for former, latter, out in ((give, give_more, send_ref), (hold, hold_more, keep_ref)):
            out[...] = (
                former[...].astype(jnp.float32) + latter[...].astype(jnp.float32)
            ).astype(jnp.bfloat16)


def add_halves(jobs):
    groups = {}
    for number, (keep, _, _, _, parts) in enumerate(jobs):
        before, columns = keep.shape[0], keep.shape[3] // parts
        tiles = 1
        while before * tiles < 4 and columns % (256 * tiles) == 0:
            tiles *= 2
        several = max(1, before // 4)
        groups.setdefault(before // several * tiles, []).append((number, tiles, several))
    results = [None] * len(jobs)
    for steps, members in groups.items():
        in_specs, out_specs, shapes, operands, bits = [], [], [], [], []
        for at, (number, tiles, several) in enumerate(members):
            keep, received, mine, part, parts = jobs[number]
            before, _, rows, columns = keep.shape
            width = columns // parts // tiles

            def spec(own, at=at, tiles=tiles, first=part * tiles, several=several, rows=rows, width=width):
                return pl.BlockSpec(
                    (several, None, rows, width),
                    lambda i, m: (
                        i // tiles, m[at] if own else 1 - m[at], 0, first + i % tiles
                    ),
                )

            in_specs += [spec(False), spec(False), spec(True), spec(True)]
            out_specs += [
                pl.BlockSpec(
                    (several, rows, width), lambda i, m, tiles=tiles: (i // tiles, 0, i % tiles)
                )
            ] * 2
            shapes += [jax.ShapeDtypeStruct((before, rows, columns // parts), jnp.bfloat16)] * 2
            operands += [keep, received, keep, received]
            bits.append(mine)
        outs = pl.pallas_call(
            partial(add_halves_kernel, len(members)),
            grid_spec=pltpu.PrefetchScalarGridSpec(
                num_scalar_prefetch=1, grid=(steps,), in_specs=in_specs, out_specs=out_specs
            ),
            out_shape=shapes,
            compiler_params=pltpu.CompilerParams(vmem_limit_bytes=VMEM_LIMIT),
            cost_estimate=BRIEF,
        )(jnp.stack(bits).astype(jnp.int32), *operands)
        for at, (number, _, _) in enumerate(members):
            results[number] = outs[2 * at : 2 * at + 2]
    return results


class Scatter:
    def __init__(self, keep, received, part):
        self.bits, order = phases(part == 1, part == 1)
        core = [k for k, b in enumerate(self.bits) if b[0] == "dp" and b[2] == 1][0]
        self.names = [k for k in range(len(self.bits)) if k != core]
        self.order = [k for k in order[::-1] if k != core]
        self.keep, self.received = keep, received
        self.part, self.parts = part, 2

    def job(self):
        self.send = None
        keep, received = self.keep, self.received
        if not self.names:
            total = keep.astype(jnp.float32) + received.astype(jnp.float32)
            self.keep, self.received = total.reshape(-1, total.shape[-1]), None
            return None
        k = self.order.pop(0)
        axis = self.names.index(k)
        self.names.remove(k)
        columns = keep.shape[-1]
        shape = (2**axis, 2, keep.size // columns // 2 ** (axis + 1), columns)
        self.bit = self.bits[k]
        job = (
            keep.reshape(shape), received.reshape(shape), own_bit(self.bit), self.part, self.parts
        )
        self.part, self.parts = 0, 1
        return job

    def take(self, send, keep):
        self.send, self.keep = (send, self.bit), keep

    def launch(self):
        self.received, self.send = swap(*self.send), None


class Pair:
    def __init__(self, formers, latters, items, rows):
        bit = ("dp", lax.axis_size("dp"), 1)
        self.mine = own_bit(bit)
        self.parts = (formers, latters, [items], rows)
        (send,) = part_grads(*self.parts, 1 - self.mine)
        self.send, self.received, self.keep = (send, bit), None, None

    def own(self):
        (self.keep,) = part_grads(*self.parts, self.mine)
        return self

    def launch(self):
        self.received, self.send = swap(*self.send), None

    def split(self):
        self.pipes = [Scatter(self.keep, self.received, part) for part in range(2)]
        return self.pipes

    def done(self):
        return jnp.concatenate([p.keep for p in self.pipes], axis=1)


class SmallSum:
    def __init__(self, part):
        bits, order = phases(False)
        self.bits = bits
        self.names = order[::-1]
        self.keep, self.received = part, None
        self.send = (part, bits[self.names.pop(0)])

    def step(self):
        self.keep = self.keep + self.received
        self.received = None
        self.send = (self.keep, self.bits[self.names.pop(0)]) if self.names else None

    def launch(self):
        self.received, self.send = swap(*self.send), None

    def done(self):
        return self.keep


def advance(values, pipes):
    live = [p for p in pipes if p.received is not None]
    fresh = [p for p in pipes if p.received is None and p.send is not None]
    size = len(values)
    tied = list(
        tie(
            *values,
            *[p.received for p in live],
            *[p.keep for p in live],
            *[p.send[0] for p in fresh],
        )
    )
    values, tied = tied[:size], tied[size:]
    for p in live:
        p.received = tied.pop(0)
    for p in live:
        p.keep = tied.pop(0)
    for p in fresh:
        p.send = (tied.pop(0), p.send[1])
    now = []
    for p in live:
        if isinstance(p, Pair):
            now += p.split()
        else:
            now.append(p)
    waiting, jobs = [], []
    for p in now:
        if isinstance(p, SmallSum):
            p.step()
            continue
        job = p.job()
        if job is not None:
            waiting.append(p)
            jobs.append(job)
    for p, halves in zip(waiting, add_halves(jobs)):
        p.take(*halves)
    now = [p for p in now + fresh if p.send is not None]
    pipes[:] = now
    held = [p for p in now if p.keep is not None]
    tied = list(tie(*values, *[p.send[0] for p in now], *[p.keep for p in held]))
    values, tied = tied[:size], tied[size:]
    for p in now:
        p.send = (tied.pop(0), p.send[1])
    for p in held:
        p.keep = tied.pop(0)
    for p in now:
        p.launch()
    return values


def local(
    context,
    byte_ids,
    segment_ids,
    cotangent,
    byte_table,
    norm_mixer,
    proj_zgate,
    proj_inputs,
    proj_step,
    conv_kernel,
    conv_bias,
    step_bias,
    decay_log,
    skip_gain,
    mixer_norm,
    proj_mixed,
    norm_attn,
    proj_heads,
    proj_attended,
    norm_ffn,
    ffn_gate,
    ffn_up,
    ffn_down,
):
    row_count, length = segment_ids.shape
    tokens = row_count * length
    model_width = context.shape[2]
    model_rows = norm_mixer.shape[0]
    small = [
        byte_table.reshape(-1),
        norm_mixer,
        conv_kernel.reshape(-1),
        conv_bias,
        mixer_norm,
        norm_attn,
        norm_ffn,
    ]
    lengths = [v.shape[0] for v in small]
    packed = jnp.concatenate(small)
    packed = jnp.pad(packed, (0, -packed.shape[0] % 1024)).reshape(8, -1)
    everyone = gather_small(packed).reshape(-1, packed.size)
    unpacked = []
    start = 0
    for count in lengths:
        unpacked.append(everyone[:, start : start + count])
        start += count
    table_full = unpacked[0].reshape(-1, byte_table.shape[1])
    gain_one = unpacked[1].reshape(-1)
    taps = conv_kernel.shape[0]
    kernel_full = jnp.swapaxes(
        unpacked[2].reshape(-1, taps, conv_kernel.shape[1]), 0, 1
    ).reshape(taps, -1)
    offset_full = unpacked[3].reshape(-1)
    gated_gain = unpacked[4].reshape(-1)
    gain_two = unpacked[5].reshape(-1)
    gain_three = unpacked[6].reshape(-1)
    wide = proj_inputs.shape[1]
    step_padded = jnp.pad(proj_step, ((0, 0), (0, 128 - proj_step.shape[1])))
    g_inputs = Gather(jnp.concatenate([proj_inputs, step_padded], axis=1), False)
    g_zgate = Gather(proj_zgate, True)
    fold_mixed = proj_mixed.shape[0] // model_rows
    fold_down = ffn_down.shape[0] // model_rows
    folded = lambda v, fold: [v[q * model_rows : (q + 1) * model_rows] for q in range(fold)]
    outer_shard = jnp.concatenate(
        [ffn_gate, ffn_up]
        + folded(ffn_down, fold_down)
        + folded(proj_mixed, fold_mixed)
        + [proj_heads, proj_attended],
        axis=1,
    )
    outer_full = lax.all_gather(outer_shard, AXES, axis=0, tiled=True)
    g_inputs.step()
    g_zgate.step()
    (table_full,) = gather_round([g_inputs, g_zgate], [table_full])
    gather_round([g_inputs, g_zgate])
    gather_round([g_inputs, g_zgate])
    gather_round([g_inputs, g_zgate])
    gather_round([g_inputs, g_zgate])
    inputs_step_full = g_inputs.done()
    zgate_full = g_zgate.done()
    symbols = jnp.arange(table_full.shape[0], dtype=jnp.int32)
    onehot = (byte_ids.reshape(-1)[:, None] == symbols[None, :]).astype(jnp.bfloat16)
    embedded = matmul(onehot, table_full).reshape(tokens, model_width)
    stream_zero = embedded + context.reshape(tokens, model_width).astype(jnp.float32)
    normed_one = rms_norm(stream_zero, gain_one.astype(jnp.float32))
    normed_one_low = normed_one.astype(jnp.bfloat16)
    zgate = matmul(normed_one_low, zgate_full).reshape(row_count, length, -1)
    raw = matmul(normed_one_low, inputs_step_full).reshape(row_count, length, -1)
    ids = segment_ids.astype(jnp.float32)
    pad_heads = lambda v: jnp.pad(v, (0, 128 - HM)).reshape(1, 128)
    mixer_terms = (
        ids,
        kernel_full.astype(jnp.float32),
        offset_full.astype(jnp.float32).reshape(1, -1),
        pad_heads(step_bias),
        pad_heads(decay_log),
        jnp.repeat(skip_gain, PM).reshape(1, -1),
        gated_gain.astype(jnp.float32).reshape(1, -1),
    )
    values_low, states_low, combined, gate_low = mixer_forward(raw, zgate, *mixer_terms)
    gate_low = gate_low.reshape(tokens, -1)
    outer_full, _ = tie(outer_full, gate_low)
    hidden_width = ffn_gate.shape[1]
    mixed_start = 2 * hidden_width + fold_down * model_width
    heads_start = mixed_start + fold_mixed * model_width
    attended_start = heads_start + proj_heads.shape[1]
    heads_full = outer_full[:, heads_start:attended_start]
    attended_full = outer_full[:, attended_start:]
    mixed_full = unfold(outer_full, model_rows, mixed_start, fold_mixed, model_width)
    mixer_out = matmul(gate_low, mixed_full)
    stream_one = stream_zero + mixer_out
    normed_two = rms_norm(stream_one, gain_two.astype(jnp.float32))
    normed_two_low = normed_two.astype(jnp.bfloat16)
    joined = matmul(normed_two_low, heads_full).astype(jnp.bfloat16)
    joined = joined.reshape(row_count, length, -1)
    attended_low = attention_forward(joined, ids).reshape(tokens, model_width)
    attn_out = matmul(attended_low, attended_full)
    stream_two = stream_one + attn_out
    normed_three, norm_three_back = jax.vjp(rms_norm, stream_two, gain_three.astype(jnp.float32))
    normed_three_low = normed_three.astype(jnp.bfloat16)
    ffn_grad_low = cotangent.reshape(tokens, model_width)
    grad_three = ffn_grad_low.astype(jnp.float32)
    hidden_low, gate_grad_low, upper_grad_low, ffn_out, grad_normed_three = feed_forward(
        normed_three_low, ffn_grad_low, outer_full, model_rows, hidden_width, fold_down
    )
    stream_three = stream_two + ffn_out
    valid_rows = (segment_ids.reshape(tokens, 1) >= 0).astype(jnp.float32)
    moments = jnp.stack(
        [
            jnp.sum(valid_rows * stream_zero * stream_zero),
            jnp.sum(valid_rows * mixer_out * mixer_out),
            jnp.sum(valid_rows * attn_out * attn_out),
            jnp.sum(valid_rows * ffn_out * ffn_out),
            jnp.sum(valid_rows),
        ]
    )
    fold_width = fold_down * model_width
    s_ffn = Pair(
        [normed_three_low, hidden_low],
        [gate_grad_low, upper_grad_low, ffn_grad_low],
        [
            (0, 0, 1, 0, hidden_width),
            (1, 2, fold_down, 0, fold_width // 2),
            (0, 1, 1, 0, hidden_width),
            (1, 2, fold_down, fold_width // 2, fold_width),
        ],
        model_rows,
    )
    pipes = [s_ffn]
    (grad_normed_three,) = advance((grad_normed_three,), pipes)
    s_ffn.own()
    stream_part, grad_norm_ffn = norm_three_back(grad_normed_three)
    grad_two = grad_three + stream_part
    attn_grad_low = grad_two.astype(jnp.bfloat16)
    attn_grad_low, grad_two = advance((attn_grad_low, grad_two), pipes)
    grad_joined = attention_backward(
        joined,
        attn_grad_low.reshape(row_count, length, model_width),
        outer_full,
        attended_start // model_width,
        ids,
    ).reshape(tokens, -1)
    heads_width = proj_heads.shape[1]
    grad_one, mixer_grad_low, grad_norm_attn = norm_backward(
        [
            (grad_joined, q, outer_full, heads_start // model_width + q, model_width)
            for q in range(3)
        ],
        stream_one,
        gain_two.astype(jnp.float32).reshape(1, -1),
        grad_two,
    )
    grad_norm_attn = grad_norm_attn.reshape(-1)
    zgate_grad_low, heads_grad_low, grad_gated_gain, skip_lanes = gate_backward(
        mixer_grad_low.reshape(row_count, length, model_width),
        mixed_full,
        zgate,
        mixer_terms[-1],
        values_low,
        combined,
    )
    zgate_grad_low = zgate_grad_low.reshape(tokens, -1)
    zgate_width = zgate_grad_low.shape[1]
    s_middle = Pair(
        [normed_two_low, attended_low, normed_one_low, gate_low],
        [grad_joined, attn_grad_low, zgate_grad_low, mixer_grad_low],
        [
            (0, 0, 1, 0, heads_width),
            (1, 1, 1, 0, model_width),
            (2, 2, 1, 0, zgate_width),
            (3, 3, fold_mixed, 0, fold_mixed * model_width),
        ],
        model_rows,
    ).own()
    pipes += [s_middle]
    heads_grad_low, grad_one = advance((heads_grad_low, grad_one), pipes)
    inputs_step_grad_low, grad_conv_kernel, grad_conv_bias, bias_lanes, decay_lanes = (
        mixer_backward(heads_grad_low, raw, *mixer_terms[:-1], values_low, states_low)
    )
    inputs_step_grad_low = inputs_step_grad_low.reshape(tokens, -1)
    inputs_step_grad_low, grad_one = advance((inputs_step_grad_low, grad_one), pipes)
    s_inputs = Pair(
        [normed_one_low],
        [inputs_step_grad_low],
        [(0, 0, 1, 0, inputs_step_grad_low.shape[1])],
        model_rows,
    ).own()
    grad_zero, embed_grad_low, grad_norm_mixer = norm_backward(
        [
            (zgate_grad_low, 0, zgate_full, 0, None),
            (inputs_step_grad_low, 0, inputs_step_full, 0, None),
        ],
        stream_zero,
        gain_one.astype(jnp.float32).reshape(1, -1),
        grad_one,
    )
    grad_norm_mixer = grad_norm_mixer.reshape(-1)
    embed_grad_low = embed_grad_low.reshape(-1, table_full.shape[1])
    grad_byte_table = matmul_left(onehot, embed_grad_low)
    small_grads = [
        moments,
        bias_lanes[0, :HM],
        decay_lanes[0, :HM],
        jnp.sum(skip_lanes.reshape(HM, PM), axis=1),
        grad_conv_kernel.reshape(-1),
        grad_conv_bias.reshape(-1),
        grad_gated_gain.reshape(-1),
        grad_norm_attn,
        grad_norm_ffn,
    ]
    small_lengths = [v.shape[0] for v in small_grads]
    small_packed = jnp.concatenate(small_grads)
    small_packed = jnp.pad(small_packed, (0, -small_packed.shape[0] % 1024)).reshape(-1, 128)
    table_rows = grad_byte_table.shape[0]
    s_small = SmallSum(
        jnp.concatenate([grad_byte_table, grad_norm_mixer.reshape(-1, 128), small_packed], axis=0)
    )
    pipes = [s_inputs, s_small] + pipes
    while pipes:
        advance((), pipes)
    grad_inputs_step = s_inputs.done()
    middle_sums = s_middle.done()
    attention_sums = middle_sums[:, : heads_width + model_width]
    zgate_mixed = middle_sums[:, heads_width + model_width :]
    ffn_sums = s_ffn.done()
    half_fold = fold_width // 2
    second = hidden_width + half_fold
    down_sums = [ffn_sums[:, hidden_width:second], ffn_sums[:, second + hidden_width :]]

    def stacked(v):
        return jnp.concatenate(
            [v[:, q : q + model_width] for q in range(0, v.shape[1], model_width)], axis=0
        )

    def own_part(total, share):
        length = share.shape[-1]
        return lax.dynamic_slice_in_dim(total, own_index() * length, length, total.ndim - 1)

    small_sums = s_small.done()
    table_sum = lax.dynamic_slice_in_dim(
        small_sums, own_index() * byte_table.shape[0], byte_table.shape[0], 0
    )
    small_sums = small_sums[table_rows:].reshape(-1)
    norm_mixer_sum = own_part(small_sums[: grad_norm_mixer.shape[0]], norm_mixer)
    sums = []
    start = grad_norm_mixer.shape[0]
    for count in small_lengths:
        sums.append(small_sums[start : start + count])
        start += count
    totals, bias_total, decay_total, skip_total = sums[:4]
    kernel_sum = sums[4].reshape(taps, -1)
    offset_sum, gated_sum, norm_attn_sum, norm_ffn_sum = sums[5:]
    rms_stats = jnp.sqrt(totals[:4] / (totals[4] * model_width))
    return (
        stream_three.reshape(row_count, length, model_width),
        grad_zero.reshape(row_count, length, model_width),
        rms_stats,
        table_sum,
        norm_mixer_sum,
        zgate_mixed[:, :zgate_width],
        grad_inputs_step[:, :wide],
        grad_inputs_step[:, wide : wide + HM],
        own_part(kernel_sum, conv_kernel),
        own_part(offset_sum, conv_bias),
        bias_total,
        decay_total,
        skip_total,
        own_part(gated_sum, mixer_norm),
        stacked(zgate_mixed[:, zgate_width:]),
        own_part(norm_attn_sum, norm_attn),
        attention_sums[:, :heads_width],
        attention_sums[:, heads_width:],
        own_part(norm_ffn_sum, norm_ffn),
        ffn_sums[:, :hidden_width],
        ffn_sums[:, second : second + hidden_width],
        stacked(jnp.concatenate(down_sums, axis=1)),
    )


def solution(mesh):
    return jax.shard_map(
        local,
        mesh=mesh,
        in_specs=(
            P(("dp", "fsdp"), None, None),
            P(("dp", "fsdp"), None),
            P(("dp", "fsdp"), None),
            P(("dp", "fsdp"), None, None),
            P(("dp", "fsdp"), None),
            P(("dp", "fsdp")),
            P(("dp", "fsdp"), None),
            P(("dp", "fsdp"), None),
            P(("dp", "fsdp"), None),
            P(None, ("dp", "fsdp")),
            P(("dp", "fsdp")),
            P(),
            P(),
            P(),
            P(("dp", "fsdp")),
            P(("dp", "fsdp"), None),
            P(("dp", "fsdp")),
            P(("dp", "fsdp"), None),
            P(("dp", "fsdp"), None),
            P(("dp", "fsdp")),
            P(("dp", "fsdp"), None),
            P(("dp", "fsdp"), None),
            P(("dp", "fsdp"), None),
        ),
        out_specs=(
            P(("dp", "fsdp"), None, None),
            P(("dp", "fsdp"), None, None),
            P(),
            P(("dp", "fsdp"), None),
            P(("dp", "fsdp")),
            P(("dp", "fsdp"), None),
            P(("dp", "fsdp"), None),
            P(("dp", "fsdp"), None),
            P(None, ("dp", "fsdp")),
            P(("dp", "fsdp")),
            P(),
            P(),
            P(),
            P(("dp", "fsdp")),
            P(("dp", "fsdp"), None),
            P(("dp", "fsdp")),
            P(("dp", "fsdp"), None),
            P(("dp", "fsdp"), None),
            P(("dp", "fsdp")),
            P(("dp", "fsdp"), None),
            P(("dp", "fsdp"), None),
            P(("dp", "fsdp"), None),
        ),
        check_vma=False,
    )
```
